32 devices in a mesh: pipe: 2 (over core), dp: 16 (over z, y, x).
Axes of the slice: x: 2, y: 2, z: 4, core: 2. Of those that a mesh axis runs over, the one named last changes fastest.
Arguments:
- patches: bfloat16 [64, 196, 384], P('dp'), may hold values from -6 to 6
- class_token: bfloat16 [64, 384], P('dp'), may hold values from -6 to 6
- keep_mask: int32 [64, 196], P('dp'), may hold values 0 or 1
- class_cotangent: bfloat16 [64, 384], P('dp'), may hold values from -6 to 6
- norm1_gain: bfloat16 [2, 384], P('pipe'), may hold values from 0.5 to 1.5
- norm1_bias: bfloat16 [2, 384], P('pipe'), may hold values from -1.75 to 1.75
- qkv_weight: bfloat16 [2, 384, 1152], P('pipe'), may hold values from -0.3125 to 0.3125
- qv_bias: bfloat16 [2, 768], P('pipe'), may hold values from -1.75 to 1.75
- mix_pre: bfloat16 [8, 8], replicated, may hold values from -2 to 2
- mix_post: bfloat16 [8, 8], replicated, may hold values from -2 to 2
- post_bias: bfloat16 [8], replicated, may hold values from -0.015625 to 0.015625
- proj_weight: bfloat16 [2, 384, 384], P('pipe'), may hold values from -3.5 to 3.5
- proj_bias: bfloat16 [2, 384], P('pipe'), may hold values from -1.75 to 1.75
- scale_attn: bfloat16 [2, 384], P('pipe'), may hold values from 0.3984375 to 1.1953125
- norm2_gain: bfloat16 [2, 384], P('pipe'), may hold values from 0.5 to 1.5
- norm2_bias: bfloat16 [2, 384], P('pipe'), may hold values from -1.75 to 1.75
- fc1_weight: bfloat16 [2, 384, 1536], P('pipe'), may hold values from -0.3125 to 0.3125
- fc1_bias: bfloat16 [2, 1536], P('pipe'), may hold values from -1.75 to 1.75
- fc2_weight: bfloat16 [2, 1536, 384], P('pipe'), may hold values from -0.15625 to 0.15625
- fc2_bias: bfloat16 [2, 384], P('pipe'), may hold values from -1.75 to 1.75
- scale_mlp: bfloat16 [2, 384], P('pipe'), may hold values from 0.3984375 to 1.1953125
Outputs:
- class_output: bfloat16 [64, 384], P('dp', 'pipe')
- patch_grad: float32 [64, 196, 384], P('dp', None, 'pipe')
- class_grad: bfloat16 [64, 384], P('dp', 'pipe')
- grad_norm1_gain: float32 [2, 384], P('pipe')
- grad_norm1_bias: float32 [2, 384], P('pipe')
- grad_qkv_weight: float32 [2, 384, 1152], P('pipe')
- grad_qv_bias: float32 [2, 768], P('pipe')
- grad_proj_weight: float32 [2, 384, 384], P('pipe')
- grad_proj_bias: float32 [2, 384], P('pipe')
- grad_scale_attn: float32 [2, 384], P('pipe')
- grad_norm2_gain: float32 [2, 384], P('pipe')
- grad_norm2_bias: float32 [2, 384], P('pipe')
- grad_fc1_weight: float32 [2, 384, 1536], P('pipe')
- grad_fc1_bias: float32 [2, 1536], P('pipe')
- grad_fc2_weight: float32 [2, 1536, 384], P('pipe')
- grad_fc2_bias: float32 [2, 384], P('pipe')
- grad_scale_mlp: float32 [2, 384], P('pipe')
- grad_mix_pre: float32 [8, 8], replicated
- grad_mix_post: float32 [8, 8], replicated
- grad_post_bias: float32 [8], replicated
The draws below stay inside these ranges and needn't reach their ends.
All inputs are finite; a program needn't handle non-finite values. No bound on the sum of `keep_mask` on one device may be relied on, other than what follows from the above.
Results may differ from the reference program's by a relative error of at most 0.013.
Values may be sent and summed in bfloat16 or wider, within the bound.
No kernel may reach another device: no remote copies, remote signals or barrier semaphores. Data moves between devices by JAX's collectives and lax.ppermute only.
A program may use at most 256 MiB of HBM per device.

```python
import jax
import jax.numpy as jnp
from jax import lax

D = 384
HEADS = 8
FF = 1536
PATCHES = 196
IMG_DEV = 4
IMAGES = 64


def plant(values, rng, smallest, top_value):
    longest = values.shape.index(max(values.shape))
    spots = []
    for shift in (0, 1):
        where = [jax.random.randint(jax.random.fold_in(rng, axis), (), 0, length) for axis, length in enumerate(values.shape)]
        where[longest] = (where[longest] + shift) % values.shape[longest]
        spots.append(tuple(where))
    return values.at[spots[0]].set(smallest).at[spots[1]].set(top_value)


def shard_levels(stream_key, shape, pieces, smallest, high):
    def one(axis_at, blocks):
        draws = jax.random.uniform(jax.random.fold_in(jax.random.fold_in(stream_key, 6), axis_at), (blocks,), jnp.float32, smallest / len(pieces), high / len(pieces))
        return jnp.repeat(jnp.exp(draws), shape[axis_at] // blocks).reshape((-1,) + (1,) * (len(shape) - axis_at - 1))

    loudness = one(*pieces[0])
    for cut in pieces[1:]:
        loudness = loudness * one(*cut)
    return loudness


def noise(rng, extent, scale, reach, pieces=(), kind=jnp.bfloat16):
    values = jax.random.normal(rng, extent, jnp.float32) * scale
    if len(pieces) > 0:
        values = shard_levels(rng, extent, pieces, -0.22, 0.18) * values
    return jnp.clip(values, min=-reach, max=reach).astype(kind)


def setup_inputs(seed: int = 0) -> dict:
    seeds = jax.random.split(jax.random.key(seed), 22)
    patches = noise(seeds[0], (IMAGES, PATCHES, D), 1.0, 6.0, ((0, 16),))
    class_token = noise(seeds[1], (IMAGES, D), 1.0, 6.0, ((0, 16),))
    keep_mask = plant((jax.random.randint(seeds[2], (IMAGES, PATCHES), 0, 4) < 3).astype(jnp.int32), jax.random.fold_in(seeds[2], 1), 0, 1)
    class_cotangent = noise(seeds[3], (IMAGES, D), 1.0, 6.0, ((0, 16),))
    norm1_gain = jnp.clip(1.0 + 0.1 * jax.random.normal(seeds[4], (2, D), jnp.float32), 0.5, 1.5).astype(jnp.bfloat16)
    norm1_bias = noise(seeds[5], (2, D), 0.3, 1.75, ((0, 2),))
    qkv_weight = noise(seeds[6], (2, D, 3 * D), D ** -0.5, 0.3125, ((0, 2),))
    qv_bias = noise(seeds[7], (2, 2 * D), 0.3, 1.75, ((0, 2),))
    mix_pre = noise(seeds[8], (HEADS, HEADS), HEADS ** -0.5, 2.0)
    mix_post = noise(seeds[9], (HEADS, HEADS), HEADS ** -0.5, 2.0)
    post_bias = noise(seeds[10], (HEADS,), 0.003, 0.015625)
    proj_weight = noise(seeds[11], (2, D, D), (max(D // 128, 1)) ** -0.5, 3.5, ((0, 2),))
    proj_bias = noise(seeds[12], (2, D), 0.3, 1.75, ((0, 2),))
    scale_attn = jnp.clip(0.3984375 + 0.796875 * jax.random.uniform(seeds[13], (2, D), jnp.float32) ** shard_levels(seeds[13], (2, D), ((0, 2),), -0.2, 0.2), 0.3984375, 1.1953125).astype(jnp.bfloat16)
    norm2_gain = jnp.clip(1.0 + 0.1 * jax.random.normal(seeds[14], (2, D), jnp.float32), 0.5, 1.5).astype(jnp.bfloat16)
    norm2_bias = noise(seeds[15], (2, D), 0.3, 1.75, ((0, 2),))
    fc1_weight = noise(seeds[16], (2, D, FF), D ** -0.5, 0.3125, ((0, 2),))
    fc1_bias = noise(seeds[17], (2, FF), 0.3, 1.75, ((0, 2),))
    fc2_weight = noise(seeds[18], (2, FF, D), FF ** -0.5, 0.15625, ((0, 2),))
    fc2_bias = noise(seeds[19], (2, D), 0.3, 1.75, ((0, 2),))
    scale_mlp = jnp.clip(0.3984375 + 0.796875 * jax.random.uniform(seeds[20], (2, D), jnp.float32) ** shard_levels(seeds[20], (2, D), ((0, 2),), -0.2, 0.2), 0.3984375, 1.1953125).astype(jnp.bfloat16)
    return dict(patches=patches, class_token=class_token, keep_mask=keep_mask, class_cotangent=class_cotangent, norm1_gain=norm1_gain, norm1_bias=norm1_bias, qkv_weight=qkv_weight, qv_bias=qv_bias, mix_pre=mix_pre, mix_post=mix_post, post_bias=post_bias, proj_weight=proj_weight, proj_bias=proj_bias, scale_attn=scale_attn, norm2_gain=norm2_gain, norm2_bias=norm2_bias, fc1_weight=fc1_weight, fc1_bias=fc1_bias, fc2_weight=fc2_weight, fc2_bias=fc2_bias, scale_mlp=scale_mlp)


@jax.custom_vjp
def low(v):
    return lax.optimization_barrier(v.astype(jnp.bfloat16)).astype(jnp.float32)

@jax.custom_vjp
def low_back(v):
    return v

def low_keep(v):
    return (low(v), None)

def low_pass(kept, grad):
    return (grad,)

def back_keep(v):
    return (v, None)

def back_low(kept, grad):
    return (low(grad),)
low.defvjp(low_keep, low_pass)
low_back.defvjp(back_keep, back_low)

def product(pattern, left_side, right_side):
    return jnp.einsum(pattern, left_side, right_side, precision=lax.Precision.HIGHEST)

def layer_norm(tokens, norm_gain, norm_bias):
    average = lax.optimization_barrier(jnp.mean(tokens, -1, keepdims=True))
    centred = tokens - average
    spread = lax.optimization_barrier(jnp.mean(centred * centred, -1, keepdims=True))
    return centred * lax.rsqrt(spread + 1e-06) * norm_gain + norm_bias

def feed_forward(section_params, tokens):
    hidden = low(layer_norm(tokens, section_params[7], section_params[8]))
    inner_rows = low_back(product('...d,df->...f', hidden, section_params[9]) + section_params[10])
    active = low(jax.nn.gelu(inner_rows, approximate=False))
    return low_back(product('...f,fd->...d', active, section_params[11]) + section_params[12])

def self_block(section_params, mixing, tokens, keep_rows):
    groups, length, model_width = tokens.shape
    head_dim = model_width // HEADS
    shape_heads = (groups, length, HEADS, head_dim)
    hidden = low(layer_norm(tokens, section_params[0], section_params[1]))
    joined = product('gpd,de->gpe', hidden, section_params[2])
    queries = low_back(low(joined[..., :model_width] + section_params[3][:model_width])).reshape(shape_heads)
    key_rows = low_back(low(joined[..., model_width:2 * model_width])).reshape(shape_heads)
    value_rows = low_back(low(joined[..., 2 * model_width:] + section_params[3][model_width:])).reshape(shape_heads)
    scores = low_back(product('gihe,gjhe->ghij', queries, key_rows)) * head_dim ** (-0.5)
    positions = jnp.arange(length)
    allowed = (keep_rows[:, None, None, :] > 0) | (positions[:, None] == positions[None, :])[None, None]
    mixed_scores = product('hc,gcij->ghij', mixing[0], scores)
    weights = jax.nn.softmax(jnp.where(allowed, mixed_scores, -1e+30), axis=-1)
    combined = low(product('hc,gcij->ghij', mixing[1], weights) + mixing[2][None, :, None, None] * allowed)
    attended = low_back(low(product('ghij,gjhe->gihe', combined, value_rows))).reshape(groups, length, model_width)
    result = tokens + section_params[6] * low_back(product('gpd,de->gpe', attended, section_params[4]) + section_params[5])
    result = result + section_params[13] * feed_forward(section_params, result)
    return low_back(low(result))

def class_block(section_params, class_rows, patch_rows, keep_rows):
    groups, length, model_width = patch_rows.shape
    head_dim = model_width // HEADS
    token_heads = (groups, length + 1, HEADS, head_dim)
    tokens = jnp.concatenate([class_rows[:, None, :], patch_rows], axis=1)
    hidden = low(layer_norm(tokens, section_params[0], section_params[1]))
    queries = low_back(low(product('gd,de->ge', hidden[:, 0], section_params[2][:, :model_width]) + section_params[3][:model_width])).reshape(groups, HEADS, head_dim)
    joined = product('gpd,de->gpe', hidden, section_params[2][:, model_width:])
    key_rows = low_back(low(joined[..., :model_width])).reshape(token_heads)
    value_rows = low_back(low(joined[..., model_width:] + section_params[3][model_width:])).reshape(token_heads)
    scores = low_back(product('ghe,gjhe->ghj', queries, key_rows)) * head_dim ** (-0.5)
    allowed = jnp.concatenate([jnp.ones((groups, 1), jnp.bool_), keep_rows > 0], axis=1)[:, None, :]
    weights = low(jax.nn.softmax(jnp.where(allowed, scores, -1e+30), axis=-1))
    attended = low_back(low(product('ghj,gjhe->ghe', weights, value_rows))).reshape(groups, model_width)
    result = class_rows + section_params[6] * low_back(product('gd,de->ge', attended, section_params[4]) + section_params[5])
    return result + section_params[13] * feed_forward(section_params, result)

def reference(patches, class_token, keep_mask, class_cotangent, norm1_gain, norm1_bias, qkv_weight, qv_bias, mix_pre, mix_post, post_bias, proj_weight, proj_bias, scale_attn, norm2_gain, norm2_bias, fc1_weight, fc1_bias, fc2_weight, fc2_bias, scale_mlp):
    stacked = (norm1_gain, norm1_bias, qkv_weight, qv_bias, proj_weight, proj_bias, scale_attn, norm2_gain, norm2_bias, fc1_weight, fc1_bias, fc2_weight, fc2_bias, scale_mlp)
    params = (tuple((member.astype(jnp.float32) for member in stacked)), (mix_pre.astype(jnp.float32), mix_post.astype(jnp.float32), post_bias.astype(jnp.float32)))
    groups = IMAGES // IMG_DEV

    def regroup(array):
        return array.reshape((groups, IMG_DEV) + array.shape[1:])

    def one_group(totals, inputs):
        patch_group, class_group, keep_group, cotangent_group = inputs

        def forward(params, patch_rows, class_rows):
            sections, mixing = params
            first_section = tuple((member[0] for member in sections))
            second_section = tuple((member[1] for member in sections))
            sent_rows = self_block(first_section, mixing, patch_rows, keep_group)
            return class_block(second_section, class_rows, sent_rows, keep_group)
        result, pullback = jax.vjp(forward, params, patch_group.astype(jnp.float32), class_group.astype(jnp.float32))
        gradients, patch_part, class_part = pullback(cotangent_group.astype(jnp.float32))
        totals = jax.tree.map(lambda left_part, right_part: left_part + right_part, totals, gradients)
        return (totals, (result.astype(jnp.bfloat16), patch_part, class_part.astype(jnp.bfloat16)))
    zero_totals = jax.tree.map(jnp.zeros_like, params)
    totals, outputs = lax.scan(one_group, zero_totals, (regroup(patches), regroup(class_token), regroup(keep_mask), regroup(class_cotangent)))
    class_output = outputs[0].reshape(IMAGES, D)
    patch_grad = outputs[1].reshape(IMAGES, PATCHES, D)
    class_grad = outputs[2].reshape(IMAGES, D)
    sections, mixing = totals
    return (class_output, patch_grad, class_grad, sections[0], sections[1], sections[2], sections[3], sections[4], sections[5], sections[6], sections[7], sections[8], sections[9], sections[10], sections[11], sections[12], sections[13], mixing[0], mixing[1], mixing[2])
```

```python
import jax
import jax.numpy as jnp
from jax import lax
from jax.experimental import pallas as pl
from jax.experimental.pallas import tpu as pltpu
from jax.sharding import PartitionSpec as P

HEADS = 8
IMGS = 2
VMEM_LIMIT = 48 * 1024 * 1024
LOG2E = 1.4426950408889634
F32 = jnp.float32
BF16 = jnp.bfloat16


def mm(left, right):
    return lax.dot_general(left, right, (((1,), (0,)), ((), ())), preferred_element_type=F32)


def mm_nt(left, right):
    return lax.dot_general(left, right, (((1,), (1,)), ((), ())), preferred_element_type=F32)


def mm_tn(left, right):
    return lax.dot_general(left, right, (((0,), (0,)), ((), ())), preferred_element_type=F32)


def normed(rows):
    centred = rows - jnp.mean(rows, -1, keepdims=True)
    scale = lax.rsqrt(jnp.mean(centred * centred, -1, keepdims=True) + 1e-06)
    return centred * scale, scale


def norm_back(normal, scale, grad):
    inner = jnp.mean(grad * normal, -1, keepdims=True)
    return (grad - jnp.mean(grad, -1, keepdims=True) - normal * inner) * scale


def col_sum(rows):
    return jnp.sum(rows, axis=0, keepdims=True)


def gelu_pair(rows):
    size = jnp.abs(rows)
    bell = jnp.exp2(rows * rows * (-0.5 * LOG2E))
    t = 1.0 / (1.0 + (0.3275911 * 0.7071067811865476) * size)
    poly = t * (0.254829592 + t * (-0.284496736 + t * (1.421413741 + t * (-1.453152027 + t * 1.061405429))))
    tail = 0.5 * poly * bell
    phi = jnp.where(rows < 0.0, tail, 1.0 - tail)
    return rows * phi, phi + rows * (bell * 0.3989422804014327)


def head_mask(rows, width):
    lane = lax.broadcasted_iota(jnp.int32, (rows, width), 1)
    head = lax.rem(lax.broadcasted_iota(jnp.int32, (rows, width), 0), HEADS)
    size = width // HEADS
    return (lane >= head * size) & (lane < head * size + size)


def chosen(is_first, first, other):
    return jnp.where(is_first, first, other)


def transposed(rows):
    return rows.T


def attention_forward(
    place, mix_pre, mix_post, rows_ref, keep_ref, vec_own, vec_got, w_own, w_got, bias_ref,
    att_ref, hid_ref, q_ref, k_ref, v_ref, pt_ref, w_ref, vs_ref,
):
    first = place[0] == 0
    width = rows_ref.shape[2]
    length = rows_ref.shape[1]
    lanes = q_ref.shape[1]
    size = width // HEADS

    @pl.when(first)
    def _():
        w_ref[...] = w_own[...]

    @pl.when(jnp.logical_not(first))
    def _():
        w_ref[...] = w_got[...]

    vec = chosen(first, vec_own[...].astype(F32), vec_got[...].astype(F32))
    scale = size ** (-0.5) * LOG2E
    pad_rows = jnp.zeros((lanes - length, width), BF16)
    same = lax.broadcasted_iota(jnp.int32, (length, lanes), 0) == lax.broadcasted_iota(jnp.int32, (length, lanes), 1)

    for b in range(IMGS):
        normal, _ = normed(rows_ref[b].astype(F32))
        hidden = (normal * vec[0:1] + vec[1:2]).astype(BF16)
        hid_ref[b] = hidden
        joined = mm(hidden, w_ref[...])
        queries = joined[:, :width] + vec[2:3]
        keys = joined[:, width : 2 * width]
        values = joined[:, 2 * width :] + vec[3:4]
        low_k = keys.astype(BF16)
        low_v = values.astype(BF16)
        q_ref[b, :length] = queries.astype(BF16)
        k_ref[b, :length] = low_k
        v_ref[b, :length] = low_v
        q_ref[b, length:] = pad_rows
        k_ref[b, length:] = pad_rows
        v_ref[b, length:] = pad_rows
        q_t = transposed(q_ref[b].astype(F32))
        v_t = transposed(v_ref[b].astype(F32))
        keep = keep_ref[b]
        allowed = (keep > 0.0) | same
        for h in range(HEADS):
            scaled_q = jnp.concatenate(
                [q_t[c * size : (c + 1) * size] * mix_pre[h, c] for c in range(HEADS)], axis=0
            ).astype(BF16)
            scores = jnp.where(allowed, mm(low_k, scaled_q) * scale, -1e30)
            top = jnp.max(scores, axis=0, keepdims=True)
            weights = jnp.exp2(scores - top)
            weights = weights * (1.0 / jnp.sum(weights, axis=0, keepdims=True))
            pt_ref[b, h * lanes : h * lanes + length] = weights.astype(BF16)
            pt_ref[b, h * lanes + length : (h + 1) * lanes] = jnp.zeros((lanes - length, lanes), BF16)
            vs_ref[:, h * lanes : (h + 1) * lanes] = jnp.concatenate(
                [v_t[c * size : (c + 1) * size] * mix_post[c, h] for c in range(HEADS)], axis=0
            ).astype(BF16)
        mixed = transposed(mm(vs_ref[...], pt_ref[b]))[:length]
        low_f = low_v.astype(F32)
        extra = bias_ref[...] * (col_sum(low_f * keep) + (1.0 - keep) * low_f)
        att_ref[b] = (mixed + extra).astype(BF16)


def block_copy(place, source, target, start, count):
    for n in range(count):
        at = position_block(place, start + n)
        target[n] = source[at]


def position_block(place, at):
    first_bit, second_bit = (at >> 3) & 1, (at >> 2) & 1
    rest = ((at >> 4) << 4) | ((at & 1) << 3) | (((at >> 1) & 1) << 2)
    x_first = rest | first_bit | (second_bit << 1)
    y_first = rest | second_bit | (first_bit << 1)
    flip = place[0] ^ (at >> 4)
    return jnp.where(flip == 0, x_first, y_first) ^ place[1]


def block_position(place, block):
    apart = block ^ place[1]
    x_bit, y_bit = apart & 1, (apart >> 1) & 1
    half = apart >> 4
    straight = (place[0] ^ half) == 0
    top = jnp.where(straight, (x_bit << 3) | (y_bit << 2), (y_bit << 3) | (x_bit << 2))
    return (half << 4) | top | (((apart >> 2) & 1) << 1) | ((apart >> 3) & 1)


def put_blocks(target, rows, start, wide):
    tall, across = 48, 384
    for rb in range(rows.shape[0] // tall):
        for cb in range(rows.shape[1] // across):
            block = rb * wide[0] + wide[1] + cb
            for k in range(3):
                piece = rows[rb * tall : (rb + 1) * tall, cb * across + k * 128 : cb * across + (k + 1) * 128]
                target[block, start + k * tall : start + (k + 1) * tall] = piece.astype(BF16)


def middle_kernel(
    place, att_ref, rows_ref, keep_rows, class_ref, cot_ref,
    vec_own, vec_got, p_own, p_got, f1_own, f1_got, f2_own, f2_got, w_own, w_got,
    send_ref, kept_ref, mg_ref, vec_out, vec_out1, class_out, factor_ref,
    p0_ref, f10, f20, p1_ref, f11, f21, w1_ref, act_ref, gp_ref, blocks,
):
    first = place[0] == 0
    length, width = rows_ref.shape[1], rows_ref.shape[2]
    flat = IMGS * length
    size = width // HEADS
    patches = 196

    @pl.when(first)
    def _():
        p0_ref[...] = p_own[...]
        f10[...] = f1_own[...]
        f20[...] = f2_own[...]
        p1_ref[...] = p_got[...]
        f11[...] = f1_got[...]
        f21[...] = f2_got[...]
        w1_ref[...] = w_got[...]

    @pl.when(jnp.logical_not(first))
    def _():
        p0_ref[...] = p_got[...]
        f10[...] = f1_got[...]
        f20[...] = f2_got[...]
        p1_ref[...] = p_own[...]
        f11[...] = f1_own[...]
        f21[...] = f2_own[...]
        w1_ref[...] = w_own[...]

    own, got = vec_own[...].astype(F32), vec_got[...].astype(F32)
    vec, vec1 = chosen(first, own, got), chosen(first, got, own)

    def wide_bias(v):
        return jnp.concatenate([v[8 + k : 9 + k] for k in range(4)], axis=1)

    branch = mm(att_ref[...].reshape(flat, width), p0_ref[...]) + vec[4:5]
    middle = rows_ref[...].reshape(flat, width).astype(F32) + vec[5:6] * branch
    normal, norm_scale = normed(middle)
    inner_low = (normal * vec[6:7] + vec[7:8]).astype(BF16)
    bias = wide_bias(vec)
    step = 384
    for k in range(4):
        cut = slice(k * step, (k + 1) * step)
        inner = mm(inner_low, f10[:, cut]) + bias[:, cut]
        active, slope = gelu_pair(inner)
        act_ref[:, cut] = active.astype(BF16)
        gp_ref[:, cut] = slope.astype(BF16)
    outer = mm(act_ref[...], f20[...]) + vec[12:13]
    sent = (middle + vec[13:14] * outer).astype(BF16).astype(F32)

    class_rows = class_ref[...].astype(F32)
    normal_c, _ = normed(class_rows)
    hidden_c = (normal_c * vec1[0:1] + vec1[1:2]).astype(BF16)
    query = (mm(hidden_c, w1_ref[:, :width]) + vec1[2:3]).astype(BF16).astype(F32)
    mask = head_mask(IMGS * HEADS, width)

    def spread(rows):
        both = jnp.concatenate(
            [jnp.broadcast_to(rows[b : b + 1], (HEADS, width)) for b in range(IMGS)], axis=0
        )
        return jnp.where(mask, both, 0.0)

    def gathered(rows):
        kept = jnp.where(mask, rows, 0.0)
        parts = [col_sum(kept[b * HEADS : (b + 1) * HEADS]) for b in range(IMGS)]
        return jnp.concatenate(parts + [jnp.zeros((8 - IMGS, width), F32)], axis=0)

    query_rows = mm_nt(spread(query).astype(BF16), w1_ref[:, width : 2 * width]).astype(BF16)
    at_row = lax.broadcasted_iota(jnp.int32, (length, width), 0)
    hiddens, normals, scales, probs, low_probs, sums, whs = [], [], [], [], [], [], []
    for b in range(IMGS):
        tokens = jnp.where(at_row == patches, class_rows[b : b + 1], sent[b * length : (b + 1) * length])
        n1, s1 = normed(tokens)
        h1 = (n1 * vec1[0:1] + vec1[1:2]).astype(BF16)
        scores = mm_nt(query_rows[b * HEADS : (b + 1) * HEADS], h1) * (size ** (-0.5) * LOG2E)
        scores = jnp.where(keep_rows[b : b + 1] > 0.0, scores, -1e30)
        weights = jnp.exp2(scores - jnp.max(scores, axis=-1, keepdims=True))
        weights = weights / jnp.sum(weights, axis=-1, keepdims=True)
        low = weights.astype(BF16)
        hiddens.append(h1)
        normals.append(n1)
        scales.append(s1)
        probs.append(weights)
        low_probs.append(low)
        sums.append(jnp.sum(low.astype(F32), axis=-1, keepdims=True))
        whs.append(mm(low, h1))
    wh = jnp.concatenate(whs, axis=0).astype(BF16)
    prob_sum = gathered(jnp.broadcast_to(jnp.concatenate(sums, axis=0), (IMGS * HEADS, width)))
    att1 = (gathered(mm(wh, w1_ref[:, 2 * width :])) + vec1[3:4] * prob_sum).astype(BF16)
    branch1 = mm(att1, p1_ref[...]) + vec1[4:5]
    middle1 = class_rows + vec1[5:6] * branch1
    normal2, scale2 = normed(middle1)
    inner1 = (normal2 * vec1[6:7] + vec1[7:8]).astype(BF16)
    active1, slope1 = gelu_pair(mm(inner1, f11[...]) + wide_bias(vec1))
    outer1 = mm(active1.astype(BF16), f21[...]) + vec1[12:13]
    class_result = middle1 + vec1[13:14] * outer1

    upper1 = cot_ref[...].astype(F32)
    og1 = (upper1 * vec1[13:14]).astype(BF16)
    ig1 = (mm_nt(og1, f21[...]) * slope1).astype(BF16)
    dh2 = mm_nt(ig1, f11[...])
    mg1 = upper1 + norm_back(normal2, scale2, dh2 * vec1[6:7])
    bg1 = (mg1 * vec1[5:6]).astype(BF16)
    da1 = mm_nt(bg1, p1_ref[...]).astype(BF16).astype(F32)
    value_rows = mm_nt(spread(da1).astype(BF16), w1_ref[:, 2 * width :]).astype(BF16)
    low_grads, gs = [], []
    for b in range(IMGS):
        part = slice(b * HEADS, (b + 1) * HEADS)
        dw = mm_nt(value_rows[part], hiddens[b])
        ds = probs[b] * (dw - jnp.sum(probs[b] * dw, axis=-1, keepdims=True))
        low = (ds * size ** (-0.5)).astype(BF16)
        low_grads.append(low)
        gs.append(mm(low, hiddens[b]))
    g_rows = jnp.concatenate(gs, axis=0).astype(BF16)
    dq1 = gathered(mm(g_rows, w1_ref[:, width : 2 * width])).astype(BF16)
    dclass = mm_nt(dq1, w1_ref[:, :width])
    uppers, class_grads = [], []
    n1g, n1b = jnp.zeros((1, width), F32), jnp.zeros((1, width), F32)
    for b in range(IMGS):
        part = slice(b * HEADS, (b + 1) * HEADS)
        left = jnp.concatenate([low_grads[b], low_probs[b]], axis=0)
        right = jnp.concatenate([query_rows[part], value_rows[part]], axis=0)
        dh1 = mm_tn(left, right)
        dh1 = jnp.where(at_row == patches, dh1 + dclass[b : b + 1], dh1)
        n1g = n1g + col_sum(dh1 * normals[b])
        n1b = n1b + col_sum(dh1)
        dtokens = norm_back(normals[b], scales[b], dh1 * vec1[0:1])
        class_grads.append(dtokens[patches : patches + 1] + mg1[b : b + 1])
        uppers.append(jnp.where(at_row < patches, dtokens, 0.0).astype(BF16).astype(F32))
    upper = jnp.concatenate(uppers, axis=0)
    blank = jnp.zeros((8 - IMGS, width), F32)
    class_out[0:8] = class_result
    class_out[8:16] = jnp.concatenate(class_grads + [blank], axis=0)
    ig1_sum = col_sum(ig1.astype(F32))
    vec_out1[...] = jnp.concatenate(
        [
            n1g,
            n1b,
            col_sum(dq1.astype(F32)),
            col_sum(da1 * prob_sum),
            col_sum(bg1.astype(F32)),
            col_sum(mg1 * branch1),
            col_sum(dh2 * normal2),
            col_sum(dh2),
        ]
        + [ig1_sum[:, k * width : (k + 1) * width] for k in range(4)]
        + [col_sum(og1.astype(F32)), col_sum(upper1 * outer1), jnp.zeros((2, width), F32)],
        axis=0,
    )
    pieces = [piece.astype(F32)[0:IMGS] for piece in (hidden_c, att1, bg1, inner1, og1)]
    vectors = jnp.concatenate(pieces + [jnp.zeros((16 - 5 * IMGS, width), F32)], axis=0).astype(BF16)
    for k in range(3):
        lanes = slice(k * 128, (k + 1) * 128)
        factor_ref[k * 48 : k * 48 + 16] = wh[:, lanes]
        factor_ref[k * 48 + 16 : k * 48 + 32] = g_rows[:, lanes]
        factor_ref[k * 48 + 32 : k * 48 + 48] = vectors[:, lanes]

    sm_grad = col_sum(upper * outer)
    og = (upper * vec[13:14]).astype(BF16)
    put_blocks(blocks, mm_tn(act_ref[...], og), 144, (1, 0))
    dh = jnp.zeros((flat, width), F32)
    fc1_sums = []
    for k in range(4):
        cut = slice(k * step, (k + 1) * step)
        ig = (mm_nt(og, f20[cut, :]) * gp_ref[:, cut].astype(F32)).astype(BF16)
        fc1_sums.append(col_sum(ig.astype(F32)))
        put_blocks(blocks, mm_tn(inner_low, ig), 0, (4, k))
        dh = dh + mm_nt(ig, f10[:, cut])
    mg = upper + norm_back(normal, norm_scale, dh * vec[6:7])
    mg_ref[...] = mg.reshape(IMGS, length, width)
    vec_out[...] = jnp.concatenate(
        [jnp.zeros((4, width), F32), jnp.zeros((1, width), F32), col_sum(mg * branch), col_sum(dh * normal), col_sum(dh)]
        + fc1_sums
        + [col_sum(og.astype(F32)), sm_grad, jnp.zeros((2, width), F32)],
        axis=0,
    )
    block_copy(place, blocks, kept_ref, 0, 16)
    block_copy(place, blocks, send_ref, 16, 16)


def attention_backward(
    place, mix_pre, mix_post, mg_ref, rows_ref, keep_ref, hid_ref, q_ref, k_ref, v_ref, pt_ref, att_ref,
    vec_in, vec_in1, vec_own, vec_got, w_own, w_got, p_own, p_got, bias_ref, pre_rows, post_rows,
    send_ref, kept_ref, own_half, other_half,
    w_ref, p_ref, dm_ref, ks_ref, da_ref, join_ref, bg_ref, blocks, tall_ref,
):
    first = place[0] == 0
    length, width = rows_ref.shape[1], rows_ref.shape[2]
    lanes = q_ref.shape[1]
    size = width // HEADS
    flat = IMGS * length
    root = size ** (-0.5)

    @pl.when(first)
    def _():
        w_ref[...] = w_own[...]
        p_ref[...] = p_own[...]

    @pl.when(jnp.logical_not(first))
    def _():
        w_ref[...] = w_got[...]
        p_ref[...] = p_got[...]

    vec = chosen(first, vec_own[...].astype(F32), vec_got[...].astype(F32))
    mg = mg_ref[...].reshape(flat, width)
    bg = (mg * vec[5:6]).astype(BF16)
    bg_ref[...] = bg
    pb_grad = col_sum(bg.astype(F32))
    put_blocks(blocks, mm_tn(att_ref[...].reshape(flat, width), bg), 0, (4, 3))
    pad_rows = jnp.zeros((lanes - length, width), BF16)
    pre_sum = jnp.zeros((HEADS, width), F32)
    post_sum = jnp.zeros((HEADS, width), F32)
    bias_sum = jnp.zeros((1, width), F32)
    for b in range(IMGS):
        da = mm_nt(bg_ref[b * length : (b + 1) * length], p_ref[...]).astype(BF16)
        da_ref[:length] = da
        da_ref[length:] = pad_rows
        da_t = transposed(da_ref[...].astype(F32))
        k_t = transposed(k_ref[b].astype(F32))
        low_v = v_ref[b, :length]
        val_f = low_v.astype(F32)
        key_f = k_ref[b, :length].astype(F32)
        da_f = da.astype(F32)
        keep = keep_ref[b]
        biased = da_f * bias_ref[...]
        dv = keep * col_sum(biased) + (1.0 - keep) * biased
        bias_sum = bias_sum + col_sum(da_f * (col_sum(val_f * keep) + (1.0 - keep) * val_f))
        post_parts = []
        for c in range(HEADS):
            scaled = jnp.concatenate(
                [da_t[h * size : (h + 1) * size] * mix_post[h, c] for h in range(HEADS)], axis=0
            ).astype(BF16)
            dp = mm(low_v, scaled)
            weights = pt_ref[b, c * lanes : c * lanes + length]
            w_f = weights.astype(F32)
            dm = w_f * (dp - col_sum(w_f * dp))
            dm_ref[c * lanes : c * lanes + length] = dm.astype(BF16)
            dm_ref[c * lanes + length : (c + 1) * lanes] = jnp.zeros((lanes - length, lanes), BF16)
            moved = mm(weights, da_ref[...])
            dv = dv + moved * post_rows[c : c + 1]
            post_parts.append(col_sum(moved * val_f))
            ks_ref[:, c * lanes : (c + 1) * lanes] = jnp.concatenate(
                [k_t[h * size : (h + 1) * size] * mix_pre[c, h] for h in range(HEADS)], axis=0
            ).astype(BF16)
        post_sum = post_sum + jnp.concatenate(post_parts, axis=0)
        dk = jnp.zeros((length, width), F32)
        pre_parts = []
        for h in range(HEADS):
            moved = mm(dm_ref[h * lanes : h * lanes + length], q_ref[b])
            dk = dk + moved * pre_rows[h : h + 1]
            pre_parts.append(col_sum(moved * key_f))
        pre_sum = pre_sum + jnp.concatenate(pre_parts, axis=0)
        dq = transposed(mm(ks_ref[...], dm_ref[...]))[:length] * root
        join_ref[b * length : (b + 1) * length, :width] = dq.astype(BF16)
        join_ref[b * length : (b + 1) * length, width : 2 * width] = (dk * root).astype(BF16)
        join_ref[b * length : (b + 1) * length, 2 * width :] = dv.astype(BF16)
    joined = join_ref[...]
    hidden = hid_ref[...].reshape(flat, width)
    for k in range(3):
        put_blocks(blocks, mm_tn(hidden, join_ref[:, k * width : (k + 1) * width]), 0, (4, k))
    dh = mm_nt(joined, w_ref[...])
    normal, norm_scale = normed(rows_ref[...].reshape(flat, width).astype(F32))
    patch = mg + norm_back(normal, norm_scale, dh * vec[0:1])
    half = width // 2
    low_half, high_half = patch[:, :half], patch[:, half:]
    own_half[...] = jnp.where(first, low_half, high_half).reshape(IMGS, length, half)
    other_half[...] = jnp.where(first, high_half, low_half).astype(BF16).reshape(IMGS, length, half)

    dq_sum = col_sum(join_ref[:, :width].astype(F32))
    dv_sum = col_sum(join_ref[:, 2 * width :].astype(F32))
    late = jnp.concatenate(
        [col_sum(dh * normal), col_sum(dh), dq_sum, dv_sum, pb_grad, jnp.zeros((11, width), F32)], axis=0
    )
    vec0 = vec_in[...] + late
    lane = lax.broadcasted_iota(jnp.int32, (width, 128), 1)
    feature = lax.broadcasted_iota(jnp.int32, (width, 128), 0)
    groups = jnp.where((feature >= lane * size) & (feature < lane * size + size), 1.0, 0.0)
    sums = jnp.concatenate([pre_sum * root, post_sum, bias_sum, jnp.zeros((7, width), F32)], axis=0)
    small = lax.dot_general(
        sums, groups, (((1,), (0,)), ((), ())), preferred_element_type=F32, precision=lax.Precision.HIGHEST
    )
    tall = jnp.concatenate(
        [vec0[:, k * 128 : (k + 1) * 128] for k in range(3)]
        + [vec_in1[:, k * 128 : (k + 1) * 128] for k in range(3)]
        + [small, jnp.zeros((8, 128), F32)],
        axis=0,
    )
    tall_ref[...] = tall
    filler = jnp.zeros((12, 128), F32)
    for n in range(32):
        blocks[n, 144:160] = jnp.concatenate([tall_ref[n * 4 : n * 4 + 4], filler], axis=0).astype(BF16)
    block_copy(place, blocks, kept_ref, 0, 16)
    block_copy(place, blocks, send_ref, 16, 16)


def unpack(place, mine, other, block, start):
    source = mine if block < 16 else other
    at = block_position(place, block) & 15
    return [source[at, start + k * 48 : start + (k + 1) * 48].astype(F32) for k in range(3)]


def fc_outputs(place, mine, other, factors, f1, f2, vec, fc1_out, fc2_out):
    width = f1.shape[0]

    @pl.when(place[0] == 0)
    def _():
        for block in range(32):
            rb, cb = block // 4, block % 4
            for k, piece in enumerate(unpack(place, mine, other, block, 0)):
                fc1_out[rb * 48 : (rb + 1) * 48, cb * 384 + k * 128 : cb * 384 + (k + 1) * 128] = piece
            for k, piece in enumerate(unpack(place, mine, other, block, 144)):
                fc2_out[block * 48 : (block + 1) * 48, k * 128 : (k + 1) * 128] = piece

    @pl.when(place[0] != 0)
    def _():
        bias = jnp.concatenate([vec[8 + k : 9 + k].astype(F32) for k in range(4)], axis=1)
        group = min(32, factors.shape[0])
        for n in range(factors.shape[0] // group):
            vectors = factor_rows(factors, slice(n * group, (n + 1) * group), 32, group)
            inner1, og1 = picked(vectors, 3, group), picked(vectors, 4, group)
            active, slope = gelu_pair(mm(inner1, f1[...]) + bias)
            ig1 = (mm_nt(og1, f2[...]) * slope).astype(BF16)
            fc1_part = mm_tn(inner1, ig1)
            fc2_part = mm_tn(active.astype(BF16), og1)
            fc1_out[...] = fc1_part if n == 0 else fc1_out[...] + fc1_part
            fc2_out[...] = fc2_part if n == 0 else fc2_out[...] + fc2_part


def factor_rows(factors, part, start, group):
    pieces = [factors[part, k * 48 + start : k * 48 + start + 16].reshape(group * 16, 128) for k in range(3)]
    return jnp.concatenate(pieces, axis=1)


def picked(vectors, kind, group):
    rows, cols = group * IMGS, group * 16
    row = lax.broadcasted_iota(jnp.int32, (rows, cols), 0)
    col = lax.broadcasted_iota(jnp.int32, (rows, cols), 1)
    wanted = (row >> 1) * 16 + kind * IMGS + (row & 1)
    return mm(jnp.where(col == wanted, 1.0, 0.0).astype(BF16), vectors).astype(BF16)


def qkv_outputs(place, mine, other, factors, w, p, vec, qkv_out, proj_out, vec_out, mix_out, tall_ref):
    width = p.shape[0]
    first = place[0] == 0
    for block in range(32):
        at = block_position(place, block) & 15
        here, there = mine[at, 144:160].astype(F32), other[at, 144:160].astype(F32)
        low = chosen(first, here, there) if block < 16 else chosen(first, there, here)
        tall_ref[block * 4 : block * 4 + 4] = low[0:4]
    for k in range(3):
        vec_out[:, k * 128 : (k + 1) * 128] = chosen(
            first, tall_ref[k * 16 : (k + 1) * 16], tall_ref[48 + k * 16 : 48 + (k + 1) * 16]
        )
    mix_out[...] = tall_ref[96:120]

    @pl.when(first)
    def _():
        for block in range(32):
            rb, cb = block // 4, block % 4
            for k, piece in enumerate(unpack(place, mine, other, block, 0)):
                rows = slice(rb * 48, (rb + 1) * 48)
                if cb < 3:
                    qkv_out[rows, cb * 384 + k * 128 : cb * 384 + (k + 1) * 128] = piece
                else:
                    proj_out[rows, k * 128 : (k + 1) * 128] = piece

    @pl.when(jnp.logical_not(first))
    def _():
        group = min(32, factors.shape[0])
        rows = group * IMGS * HEADS
        mask = head_mask(rows, width)
        spread = (
            lax.broadcasted_iota(jnp.int32, (rows, group * IMGS), 0) >> 3
            == lax.broadcasted_iota(jnp.int32, (rows, group * IMGS), 1)
        )
        spread = jnp.where(spread, 1.0, 0.0).astype(BF16)

        def expanded(vectors):
            return jnp.where(mask, mm(spread, vectors), 0.0).astype(BF16)

        for n in range(factors.shape[0] // group):
            part = slice(n * group, (n + 1) * group)
            wh, g, vectors = (factor_rows(factors, part, start, group) for start in (0, 16, 32))
            hidden_c, att1, bg1 = (picked(vectors, kind, group) for kind in range(3))
            query = (mm(hidden_c, w[:, :width]) + vec[2:3].astype(F32)).astype(BF16)
            da1 = mm_nt(bg1, p[...]).astype(BF16)
            chosen_g = jnp.where(mask, mm(g, w[:, width : 2 * width]), 0.0).astype(BF16)
            dq1 = mm_tn(spread, chosen_g).astype(BF16)
            parts = (mm_tn(hidden_c, dq1), mm_tn(g, expanded(query)), mm_tn(wh, expanded(da1)))
            for k, piece in enumerate(parts):
                cut = slice(k * width, (k + 1) * width)
                qkv_out[:, cut] = piece if n == 0 else qkv_out[:, cut] + piece
            piece = mm_tn(att1, bg1)
            proj_out[...] = piece if n == 0 else proj_out[...] + piece


VM = pl.BlockSpec(memory_space=pltpu.VMEM)
SM = pl.BlockSpec(memory_space=pltpu.SMEM)


def call(body, ins, outs, scratch, name, flops=0):
    specs = [SM if small else VM for small, _ in ins]
    return pl.pallas_call(
        body,
        out_shape=[jax.ShapeDtypeStruct(shape, kind) for shape, kind in outs],
        in_specs=specs,
        out_specs=[VM] * len(outs),
        scratch_shapes=[pltpu.VMEM(shape, kind) for shape, kind in scratch],
        compiler_params=pltpu.CompilerParams(vmem_limit_bytes=VMEM_LIMIT),
        cost_estimate=pl.CostEstimate(flops=flops, bytes_accessed=4000000, transcendentals=0),
        name=name,
    )(*[value for _, value in ins])


def swapped(array):
    return lax.ppermute(array, "pipe", [(0, 1), (1, 0)])


def core_pairs(dp, bits):
    return [
        (core * dp + i, core * dp + (i ^ bit)) for core, bit in enumerate(bits) for i in range(dp)
    ]


STEPS = ((1, 2), (2, 1), (4, 4), (8, 8))


def exchanged(array, bits):
    dp = lax.axis_size("dp")
    return lax.ppermute(array, ("pipe", "dp"), core_pairs(dp, bits))


def added(left, right):
    return (left.astype(F32) + right.astype(F32)).astype(BF16)


def scattered(kept, got):
    if lax.axis_size("dp") != 16:
        return lax.psum(added(kept, got).astype(F32), "dp").astype(BF16)
    count = kept.shape[0]
    for bits in STEPS:
        half = count // 2
        leaving = added(kept[half:count], got[half:count])
        kept = added(kept[:half], got[:half])
        got = exchanged(leaving, bits)
        count = half
    return added(kept, got)


def collected(blocks):
    if lax.axis_size("dp") != 16:
        return blocks
    for bits in STEPS[::-1]:
        blocks = jnp.concatenate([blocks, exchanged(blocks, bits)], axis=0)
    return blocks


def local(
    patches, class_token, keep_mask, class_cotangent, norm1_gain, norm1_bias, qkv_weight, qv_bias,
    mix_pre, mix_post, post_bias, proj_weight, proj_bias, scale_attn, norm2_gain, norm2_bias,
    fc1_weight, fc1_bias, fc2_weight, fc2_bias, scale_mlp,
):
    core = lax.axis_index("pipe")
    chip = lax.axis_index("dp")
    dp = lax.axis_size("dp")
    images, count, width = patches.shape
    hidden_width = fc1_weight.shape[2]
    length, lanes = 208, 256
    size = width // HEADS
    me = core * 16 + (chip if dp == 16 else 0)
    place = jnp.stack([core, me]).astype(jnp.int32)

    w_own, p_own, f1_own, f2_own = qkv_weight[0], proj_weight[0], fc1_weight[0], fc2_weight[0]
    w_got = swapped(w_own)
    vec_own = jnp.concatenate(
        [
            norm1_gain, norm1_bias, qv_bias.reshape(2, width), proj_bias, scale_attn, norm2_gain, norm2_bias,
            fc1_bias.reshape(4, width), fc2_bias, scale_mlp, jnp.zeros((2, width), BF16),
        ],
        axis=0,
    )
    vec_got = swapped(vec_own)
    p_got, f1_got, f2_got = swapped(p_own), swapped(f1_own), swapped(f2_own)

    def own_images(array):
        return lax.dynamic_slice_in_dim(array, core * IMGS, IMGS, 0)

    rows = jnp.pad(own_images(patches), ((0, 0), (0, length - count), (0, 0)))
    keep = own_images(keep_mask).astype(F32)
    keep_col = jnp.pad(keep, ((0, 0), (0, length - count)))[:, :, None]
    keep_row = jnp.pad(
        jnp.concatenate([keep, jnp.ones((IMGS, 1), F32)], axis=1), ((0, 8 - IMGS), (0, length - count - 1))
    )
    class_rows = jnp.pad(own_images(class_token), ((0, 8 - IMGS), (0, 0)))
    cot_rows = jnp.pad(own_images(class_cotangent), ((0, 8 - IMGS), (0, 0)))
    pre_f, post_f = mix_pre.astype(F32), mix_post.astype(F32)
    bias_row = jnp.repeat(post_bias.astype(F32), size)[None]
    pre_rows = jnp.repeat(pre_f, size, axis=1)
    post_rows = jnp.repeat(post_f.T, size, axis=1)

    token_shape = (IMGS, length, width)
    wide_shape = (IMGS, lanes, width)
    att, hid, queries, keys, values, probs = call(
        attention_forward,
        [(1, place), (1, pre_f), (1, post_f), (0, rows), (0, keep_col), (0, vec_own), (0, vec_got), (0, w_own),
         (0, w_got), (0, bias_row)],
        [(token_shape, BF16), (token_shape, BF16), (wide_shape, BF16), (wide_shape, BF16), (wide_shape, BF16),
         ((IMGS, HEADS * lanes, lanes), BF16)],
        [((width, 3 * width), BF16), ((width, HEADS * lanes), BF16)],
        "attention_forward",
    )
    flat = IMGS * length
    vec_shape = (16, width)
    send1, kept1, mg, vec0, vec1, class_out, factors = call(
        middle_kernel,
        [(1, place), (0, att), (0, rows), (0, keep_row), (0, class_rows), (0, cot_rows), (0, vec_own), (0, vec_got),
         (0, p_own), (0, p_got), (0, f1_own), (0, f1_got), (0, f2_own), (0, f2_got), (0, w_own), (0, w_got)],
        [((16, 288, 128), BF16), ((16, 288, 128), BF16), (token_shape, F32), (vec_shape, F32), (vec_shape, F32),
         ((16, width), F32), ((144, 128), BF16)],
        [((width, width), BF16), ((width, hidden_width), BF16), ((hidden_width, width), BF16),
         ((width, width), BF16), ((width, hidden_width), BF16), ((hidden_width, width), BF16),
         ((width, 3 * width), BF16), ((flat, hidden_width), BF16), ((flat, hidden_width), BF16),
         ((32, 288, 128), BF16)],
        "middle_kernel",
    )
    half = width // 2
    send2, kept2, own_half, other_half = call(
        attention_backward,
        [(1, place), (1, pre_f), (1, post_f), (0, mg), (0, rows), (0, keep_col), (0, hid), (0, queries), (0, keys),
         (0, values), (0, probs), (0, att), (0, vec0), (0, vec1), (0, vec_own), (0, vec_got), (0, w_own), (0, w_got),
         (0, p_own), (0, p_got), (0, bias_row), (0, pre_rows), (0, post_rows)],
        [((16, 160, 128), BF16), ((16, 160, 128), BF16), ((IMGS, length, half), F32), ((IMGS, length, half), BF16)],
        [((width, 3 * width), BF16), ((width, width), BF16), ((HEADS * lanes, lanes), BF16),
         ((width, HEADS * lanes), BF16), ((lanes, width), BF16), ((flat, 3 * width), BF16), ((flat, width), BF16),
         ((32, 160, 128), BF16), ((128, 128), F32)],
        "attention_backward",
    )

    class_low = class_out.astype(BF16)
    class_got = swapped(class_low)

    def halves(array):
        return jnp.where(core == 0, array[..., :half], array[..., half:])

    own_class, got_class = halves(class_low), halves(class_got)

    def image_order(own, got):
        return jnp.where(core == 0, jnp.concatenate([own, got], axis=0), jnp.concatenate([got, own], axis=0))

    class_result = image_order(own_class[0:IMGS], got_class[0:IMGS])
    class_grad = image_order(own_class[8 : 8 + IMGS], got_class[8 : 8 + IMGS])
    patch_out = image_order(own_half[:, :count], swapped(other_half)[:, :count].astype(F32))

    blocks1 = scattered(kept1, swapped(send1))
    if dp == 16:
        both = jnp.concatenate([blocks1, factors[None]], axis=1)
        both = collected(both)
        mine1, gathered_factors = both[:, :288], both[:, 288:]
    else:
        mine1, gathered_factors = blocks1, lax.all_gather(factors, "dp")
    other1 = swapped(mine1)
    all_factors = jnp.concatenate([gathered_factors, swapped(gathered_factors)], axis=0)
    mine2 = collected(scattered(kept2, swapped(send2)))
    other2 = swapped(mine2)

    fc1_out, fc2_out = call(
        fc_outputs,
        [(1, place), (0, mine1), (0, other1), (0, all_factors), (0, f1_own), (0, f2_own), (0, vec_own)],
        [((width, hidden_width), F32), ((hidden_width, width), F32)],
        [],
        "fc_outputs",
    )
    qkv_out, proj_out, vec_out, mix_out = call(
        qkv_outputs,
        [(1, place), (0, mine2), (0, other2), (0, all_factors), (0, w_own), (0, p_own), (0, vec_own)],
        [((width, 3 * width), F32), ((width, width), F32), (vec_shape, F32), ((24, 128), F32)],
        [((128, 128), F32)],
        "qkv_outputs",
    )
    return (
        class_result,
        patch_out,
        class_grad,
        vec_out[0:1],
        vec_out[1:2],
        qkv_out[None],
        vec_out[2:4].reshape(1, 2 * width),
        proj_out[None],
        vec_out[4:5],
        vec_out[5:6],
        vec_out[6:7],
        vec_out[7:8],
        fc1_out[None],
        vec_out[8:12].reshape(1, hidden_width),
        fc2_out[None],
        vec_out[12:13],
        vec_out[13:14],
        mix_out[0:8, 0:8],
        mix_out[8:16, 0:8].T,
        mix_out[16, 0:8],
    )


def solution(mesh):
    stacked = (P("pipe", None), P("pipe", None), P("pipe", None, None))
    row, _, cube = stacked
    return jax.shard_map(
        local,
        mesh=mesh,
        in_specs=(
            P("dp", None, None), P("dp", None), P("dp", None), P("dp", None),
            row, row, cube, row, P(), P(), P(), cube, row, row, row, row, cube, row, cube, row, row,
        ),
        out_specs=(
            P("dp", "pipe"), P("dp", None, "pipe"), P("dp", "pipe"),
            row, row, cube, row, cube, row, row, row, row, cube, row, cube, row, row, P(), P(), P(),
        ),
        check_vma=False,
    )
```

```python
import jax
import jax.numpy as jnp
from jax import lax
from jax.experimental import pallas as pl
from jax.experimental.pallas import tpu as pltpu
from jax.sharding import PartitionSpec as P

HEADS = 8
IMGS = 2
LIMIT_P, LIMIT_A, LIMIT_B, LIMIT_C, LIMIT_D, LIMIT_E = 60, 24, 24, 24, 24, 24
LOG2E = 1.4426950408889634
F32 = jnp.float32
BF16 = jnp.bfloat16


def mm(left, right):
    return lax.dot_general(left, right, (((1,), (0,)), ((), ())), preferred_element_type=F32)


def mm_nt(left, right):
    return lax.dot_general(left, right, (((1,), (1,)), ((), ())), preferred_element_type=F32)


def mm_tn(left, right):
    return lax.dot_general(left, right, (((0,), (0,)), ((), ())), preferred_element_type=F32)


def normed(rows):
    centred = rows - jnp.mean(rows, -1, keepdims=True)
    scale = lax.rsqrt(jnp.mean(centred * centred, -1, keepdims=True) + 1e-06)
    return centred * scale, scale


def norm_back(normal, scale, grad):
    inner = jnp.mean(grad * normal, -1, keepdims=True)
    return (grad - jnp.mean(grad, -1, keepdims=True) - normal * inner) * scale


def col_sum(rows):
    return jnp.sum(rows, axis=0, keepdims=True)


def gelu_pair(rows):
    phi = 0.5 + 0.5 * lax.erf(rows * 0.7071067811865476)
    return rows * phi, phi + rows * (jnp.exp2(rows * rows * (-0.5 * LOG2E)) * 0.3989422804014327)


def head_mask(rows, width):
    lane = lax.broadcasted_iota(jnp.int32, (rows, width), 1)
    head = lax.rem(lax.broadcasted_iota(jnp.int32, (rows, width), 0), HEADS)
    size = width // HEADS
    return (lane >= head * size) & (lane < head * size + size)


def chosen(is_first, first, other):
    return jnp.where(is_first, first, other)


def transposed(rows):
    return rows.T


def own_place():
    core = lax.axis_index("pipe")
    return core, core * 16 + (lax.axis_index("dp") if lax.axis_size("dp") == 16 else 0)


def fetch(first, own, got, target, sem):
    @pl.when(first)
    def _():
        pltpu.make_async_copy(own, target, sem).start()

    @pl.when(jnp.logical_not(first))
    def _():
        pltpu.make_async_copy(got, target, sem).start()

    return pltpu.make_async_copy(own, target, sem)


def own_images(first, rows):
    return chosen(first, rows[0:IMGS], rows[IMGS : 2 * IMGS])


def token_rows(rows_ref):
    rows = rows_ref[pl.ds(lax.axis_index("pipe") * IMGS, IMGS)]
    return rows.reshape(-1, rows.shape[2])


def keep_columns(first, mask_ref, scratch):
    scratch[...] = jnp.zeros_like(scratch)
    scratch[0:IMGS, 0 : mask_ref.shape[1]] = own_images(first, mask_ref[...].astype(F32))
    return scratch[...].T


def prepare(*refs):
    sources, (vec_ref, pre_ref, post_ref, bias_ref), held, sems = refs[:13], refs[13:17], refs[17:30], refs[30]
    copies = [pltpu.make_async_copy(*pair, sems.at[n]) for n, pair in enumerate(zip(sources, held))]
    for copy in copies:
        copy.start()
    for copy in copies:
        copy.wait()
    n1g, n1b, qvb, pb, sa, n2g, n2b, f1b, f2b, sm, pre, post, post_bias = held
    width = n1g.shape[1]
    rows = [n1g[...], n1b[...], qvb[:, :width], qvb[:, width:], pb[...], sa[...], n2g[...], n2b[...]]
    rows += [f1b[:, k * width : (k + 1) * width] for k in range(4)] + [f2b[...], sm[...]]
    rows = [row.astype(F32) for row in rows] + [jnp.zeros((2, width), F32)]
    vec_ref[...] = jnp.concatenate(rows, axis=0).astype(BF16)
    spread = jnp.where(head_mask(HEADS, width), 1.0, 0.0).astype(BF16)
    pre_ref[...] = mm(pre[...], spread)
    post_ref[...] = mm_tn(post[...], spread)
    bias_ref[...] = mm(post_bias[...], spread)


def attention_forward(
    mixing, rows_ref, mask_ref, vec_own, vec_got, w_own, w_got, bias_ref,
    att_ref, hid_ref, q_ref, k_ref, v_ref, pt_ref, w_ref, vs_ref, keep_ref, sems,
):
    first = lax.axis_index("pipe") == 0
    weights_copy = fetch(first, w_own, w_got, w_ref, sems.at[0])
    width = rows_ref.shape[2]
    length = rows_ref.shape[1]
    lanes = q_ref.shape[1]
    size = width // HEADS
    keeps = keep_columns(first, mask_ref, keep_ref)

    vec = chosen(first, vec_own[...].astype(F32), vec_got[...].astype(F32))
    scale = size ** (-0.5) * LOG2E
    pad_rows = jnp.zeros((lanes - length, width), BF16)
    same = lax.broadcasted_iota(jnp.int32, (length, lanes), 0) == lax.broadcasted_iota(jnp.int32, (length, lanes), 1)

    for b in range(IMGS):
        normal, _ = normed(rows_ref[lax.axis_index("pipe") * IMGS + b].astype(F32))
        hidden = (normal * vec[0:1] + vec[1:2]).astype(BF16)
        hid_ref[b] = hidden
        if b == 0:
            weights_copy.wait()
        joined = mm(hidden, w_ref[...])
        queries = joined[:, :width] + vec[2:3]
        keys = joined[:, width : 2 * width]
        values = joined[:, 2 * width :] + vec[3:4]
        low_k = keys.astype(BF16)
        low_v = values.astype(BF16)
        q_ref[b, :length] = queries.astype(BF16)
        k_ref[b, :length] = low_k
        v_ref[b, :length] = low_v
        q_ref[b, length:] = pad_rows
        k_ref[b, length:] = pad_rows
        v_ref[b, length:] = pad_rows
        q_t = transposed(q_ref[b].astype(F32))
        v_t = transposed(v_ref[b].astype(F32))
        keep = keeps[:length, b : b + 1]
        allowed = (keep > 0.0) | same
        for h in range(HEADS):
            scaled_q = jnp.concatenate(
                [q_t[c * size : (c + 1) * size] * mixing[0, h, c] for c in range(HEADS)], axis=0
            ).astype(BF16)
            scores = jnp.where(allowed, mm(low_k, scaled_q) * scale, -1e30)
            top = jnp.max(scores, axis=0, keepdims=True)
            weights = jnp.exp2(scores - top)
            weights = weights * (1.0 / jnp.sum(weights, axis=0, keepdims=True))
            pt_ref[b, h * lanes : h * lanes + length] = weights.astype(BF16)
            pt_ref[b, h * lanes + length : (h + 1) * lanes] = jnp.zeros((lanes - length, lanes), BF16)
            vs_ref[:, h * lanes : (h + 1) * lanes] = jnp.concatenate(
                [v_t[c * size : (c + 1) * size] * mixing[1, c, h] for c in range(HEADS)], axis=0
            ).astype(BF16)
        mixed = transposed(mm(vs_ref[...], pt_ref[b]))[:length]
        low_f = low_v.astype(F32)
        extra = bias_ref[...] * (col_sum(low_f * keep) + (1.0 - keep) * low_f)
        att_ref[b] = (mixed + extra).astype(BF16)


def block_copy(source, target, start, count):
    for n in range(count):
        target[n] = source[position_block(start + n)]


def position_block(at):
    core, me = own_place()
    first_bit, second_bit = (at >> 3) & 1, (at >> 2) & 1
    rest = ((at >> 4) << 4) | ((at & 1) << 3) | (((at >> 1) & 1) << 2)
    x_first = rest | first_bit | (second_bit << 1)
    y_first = rest | second_bit | (first_bit << 1)
    return jnp.where(core == (at >> 4), x_first, y_first) ^ me


def block_position(block):
    core, me = own_place()
    apart = block ^ me
    x_bit, y_bit = apart & 1, (apart >> 1) & 1
    half = apart >> 4
    top = jnp.where(core == half, (x_bit << 3) | (y_bit << 2), (y_bit << 3) | (x_bit << 2))
    return (half << 4) | top | (((apart >> 2) & 1) << 1) | ((apart >> 3) & 1)


def put_blocks(target, rows, start, wide):
    tall, across = 48, 384
    for rb in range(rows.shape[0] // tall):
        for cb in range(rows.shape[1] // across):
            block = rb * wide[0] + wide[1] + cb
            for k in range(3):
                piece = rows[rb * tall : (rb + 1) * tall, cb * across + k * 128 : cb * across + (k + 1) * 128]
                target[block, start + k * tall : start + (k + 1) * tall] = piece.astype(BF16)


def middle_kernel(
    att_ref, rows_ref, mask_ref, class_ref, cot_ref,
    vec_own, vec_got, p_own, p_got, f1_own, f1_got, f2_own, f2_got, w_own, w_got,
    send_ref, kept_ref, mg_ref, vec_out, vec_out1, class_own, class_other, factor_ref,
    p0_ref, f10, f20, p1_ref, f11, f21, w1_ref, act_ref, gp_ref, blocks, keep_ref, sems,
):
    first = lax.axis_index("pipe") == 0
    p0_copy = fetch(first, p_own, p_got, p0_ref, sems.at[0])
    f10_copy = fetch(first, f1_own, f1_got, f10, sems.at[1])
    f20_copy = fetch(first, f2_own, f2_got, f20, sems.at[2])
    w1_copy = fetch(first, w_got, w_own, w1_ref, sems.at[3])
    p1_copy = fetch(first, p_got, p_own, p1_ref, sems.at[4])
    f11_copy = fetch(first, f1_got, f1_own, f11, sems.at[5])
    f21_copy = fetch(first, f2_got, f2_own, f21, sems.at[6])
    length, width = rows_ref.shape[1], rows_ref.shape[2]
    flat = IMGS * length
    size = width // HEADS
    patches = mask_ref.shape[1]
    keep_ref[...] = jnp.zeros_like(keep_ref)
    keep_ref[0:IMGS, 0:patches] = own_images(first, mask_ref[...].astype(F32))
    keep_rows = keep_ref[0:IMGS, :length]
    keep_lane = lax.broadcasted_iota(jnp.int32, (IMGS, length), 1)
    keep_rows = jnp.where(keep_lane == patches, 1.0, keep_rows)

    own, got = vec_own[...].astype(F32), vec_got[...].astype(F32)
    vec, vec1 = chosen(first, own, got), chosen(first, got, own)

    def wide_bias(v):
        return jnp.concatenate([v[8 + k : 9 + k] for k in range(4)], axis=1)

    p0_copy.wait()
    branch = mm(att_ref[...].reshape(flat, width), p0_ref[...]) + vec[4:5]
    middle = token_rows(rows_ref).astype(F32) + vec[5:6] * branch
    normal, norm_scale = normed(middle)
    inner_low = (normal * vec[6:7] + vec[7:8]).astype(BF16)
    bias = wide_bias(vec)
    step = 384
    f10_copy.wait()
    for k in range(4):
        cut = slice(k * step, (k + 1) * step)
        inner = mm(inner_low, f10[:, cut]) + bias[:, cut]
        active, slope = gelu_pair(inner)
        act_ref[:, cut] = active.astype(BF16)
        gp_ref[:, cut] = slope.astype(BF16)
    f20_copy.wait()
    outer = mm(act_ref[...], f20[...]) + vec[12:13]
    sent = (middle + vec[13:14] * outer).astype(BF16).astype(F32)

    blank = jnp.zeros((8 - IMGS, width), F32)
    class_rows = jnp.concatenate([own_images(first, class_ref[...].astype(F32)), blank], axis=0)
    w1_copy.wait()
    normal_c, _ = normed(class_rows)
    hidden_c = (normal_c * vec1[0:1] + vec1[1:2]).astype(BF16)
    query = (mm(hidden_c, w1_ref[:, :width]) + vec1[2:3]).astype(BF16).astype(F32)
    mask = head_mask(IMGS * HEADS, width)

    def spread(rows):
        both = jnp.concatenate(
            [jnp.broadcast_to(rows[b : b + 1], (HEADS, width)) for b in range(IMGS)], axis=0
        )
        return jnp.where(mask, both, 0.0)

    def gathered(rows):
        kept = jnp.where(mask, rows, 0.0)
        parts = [col_sum(kept[b * HEADS : (b + 1) * HEADS]) for b in range(IMGS)]
        return jnp.concatenate(parts + [jnp.zeros((8 - IMGS, width), F32)], axis=0)

    query_rows = mm_nt(spread(query).astype(BF16), w1_ref[:, width : 2 * width]).astype(BF16)
    at_row = lax.broadcasted_iota(jnp.int32, (length, width), 0)
    hiddens, normals, scales, probs, low_probs, sums, whs = [], [], [], [], [], [], []
    for b in range(IMGS):
        tokens = jnp.where(at_row == patches, class_rows[b : b + 1], sent[b * length : (b + 1) * length])
        n1, s1 = normed(tokens)
        h1 = (n1 * vec1[0:1] + vec1[1:2]).astype(BF16)
        scores = mm_nt(query_rows[b * HEADS : (b + 1) * HEADS], h1) * (size ** (-0.5) * LOG2E)
        scores = jnp.where(keep_rows[b : b + 1] > 0.0, scores, -1e30)
        weights = jnp.exp2(scores - jnp.max(scores, axis=-1, keepdims=True))
        weights = weights / jnp.sum(weights, axis=-1, keepdims=True)
        low = weights.astype(BF16)
        hiddens.append(h1)
        normals.append(n1)
        scales.append(s1)
        probs.append(weights)
        low_probs.append(low)
        sums.append(jnp.sum(low.astype(F32), axis=-1, keepdims=True))
        whs.append(mm(low, h1))
    wh = jnp.concatenate(whs, axis=0).astype(BF16)
    prob_sum = gathered(jnp.broadcast_to(jnp.concatenate(sums, axis=0), (IMGS * HEADS, width)))
    att1 = (gathered(mm(wh, w1_ref[:, 2 * width :])) + vec1[3:4] * prob_sum).astype(BF16)
    p1_copy.wait()
    branch1 = mm(att1, p1_ref[...]) + vec1[4:5]
    middle1 = class_rows + vec1[5:6] * branch1
    normal2, scale2 = normed(middle1)
    inner1 = (normal2 * vec1[6:7] + vec1[7:8]).astype(BF16)
    f11_copy.wait()
    f21_copy.wait()
    active1, slope1 = gelu_pair(mm(inner1, f11[...]) + wide_bias(vec1))
    outer1 = mm(active1.astype(BF16), f21[...]) + vec1[12:13]
    class_result = middle1 + vec1[13:14] * outer1

    upper1 = jnp.concatenate([own_images(first, cot_ref[...].astype(F32)), blank], axis=0)
    og1 = (upper1 * vec1[13:14]).astype(BF16)
    ig1 = (mm_nt(og1, f21[...]) * slope1).astype(BF16)
    dh2 = mm_nt(ig1, f11[...])
    mg1 = upper1 + norm_back(normal2, scale2, dh2 * vec1[6:7])
    bg1 = (mg1 * vec1[5:6]).astype(BF16)
    da1 = mm_nt(bg1, p1_ref[...]).astype(BF16).astype(F32)
    value_rows = mm_nt(spread(da1).astype(BF16), w1_ref[:, 2 * width :]).astype(BF16)
    low_grads, gs = [], []
    for b in range(IMGS):
        part = slice(b * HEADS, (b + 1) * HEADS)
        dw = mm_nt(value_rows[part], hiddens[b])
        ds = probs[b] * (dw - jnp.sum(probs[b] * dw, axis=-1, keepdims=True))
        low = (ds * size ** (-0.5)).astype(BF16)
        low_grads.append(low)
        gs.append(mm(low, hiddens[b]))
    g_rows = jnp.concatenate(gs, axis=0).astype(BF16)
    dq1 = gathered(mm(g_rows, w1_ref[:, width : 2 * width])).astype(BF16)
    dclass = mm_nt(dq1, w1_ref[:, :width])
    uppers, class_grads = [], []
    n1g, n1b = jnp.zeros((1, width), F32), jnp.zeros((1, width), F32)
    for b in range(IMGS):
        part = slice(b * HEADS, (b + 1) * HEADS)
        left = jnp.concatenate([low_grads[b], low_probs[b]], axis=0)
        right = jnp.concatenate([query_rows[part], value_rows[part]], axis=0)
        dh1 = mm_tn(left, right)
        dh1 = jnp.where(at_row == patches, dh1 + dclass[b : b + 1], dh1)
        n1g = n1g + col_sum(dh1 * normals[b])
        n1b = n1b + col_sum(dh1)
        dtokens = norm_back(normals[b], scales[b], dh1 * vec1[0:1])
        class_grads.append(dtokens[patches : patches + 1] + mg1[b : b + 1])
        uppers.append(jnp.where(at_row < patches, dtokens, 0.0).astype(BF16).astype(F32))
    upper = jnp.concatenate(uppers, axis=0)
    class_rows = jnp.concatenate([class_result] + class_grads + [blank], axis=0)
    low_half, high_half = class_rows[:, : width // 2], class_rows[:, width // 2 :]
    class_own[...] = chosen(first, low_half, high_half).astype(BF16)
    class_other[...] = chosen(first, high_half, low_half).astype(BF16)
    ig1_sum = col_sum(ig1.astype(F32))
    vec_out1[...] = jnp.concatenate(
        [
            n1g,
            n1b,
            col_sum(dq1.astype(F32)),
            col_sum(da1 * prob_sum),
            col_sum(bg1.astype(F32)),
            col_sum(mg1 * branch1),
            col_sum(dh2 * normal2),
            col_sum(dh2),
        ]
        + [ig1_sum[:, k * width : (k + 1) * width] for k in range(4)]
        + [col_sum(og1.astype(F32)), col_sum(upper1 * outer1), jnp.zeros((2, width), F32)],
        axis=0,
    )
    pieces = [piece.astype(F32)[0:IMGS] for piece in (hidden_c, att1, bg1, inner1, og1)]
    vectors = jnp.concatenate(pieces + [jnp.zeros((16 - 5 * IMGS, width), F32)], axis=0).astype(BF16)
    for k in range(3):
        lanes = slice(k * 128, (k + 1) * 128)
        factor_ref[k * 48 : k * 48 + 16] = wh[:, lanes]
        factor_ref[k * 48 + 16 : k * 48 + 32] = g_rows[:, lanes]
        factor_ref[k * 48 + 32 : k * 48 + 48] = vectors[:, lanes]

    sm_grad = col_sum(upper * outer)
    og = (upper * vec[13:14]).astype(BF16)
    put_blocks(blocks, mm_tn(act_ref[...], og), 144, (1, 0))
    dh = jnp.zeros((flat, width), F32)
    fc1_sums = []
    for k in range(4):
        cut = slice(k * step, (k + 1) * step)
        ig = (mm_nt(og, f20[cut, :]) * gp_ref[:, cut].astype(F32)).astype(BF16)
        fc1_sums.append(col_sum(ig.astype(F32)))
        put_blocks(blocks, mm_tn(inner_low, ig), 0, (4, k))
        dh = dh + mm_nt(ig, f10[:, cut])
    mg = upper + norm_back(normal, norm_scale, dh * vec[6:7])
    mg_ref[...] = mg.reshape(IMGS, length, width)
    vec_out[...] = jnp.concatenate(
        [jnp.zeros((4, width), F32), jnp.zeros((1, width), F32), col_sum(mg * branch), col_sum(dh * normal), col_sum(dh)]
        + fc1_sums
        + [col_sum(og.astype(F32)), sm_grad, jnp.zeros((2, width), F32)],
        axis=0,
    )
    block_copy(blocks, kept_ref, 0, 16)
    block_copy(blocks, send_ref, 16, 16)


def attention_backward(
    b, mixing, mg_ref, mask_ref, q_ref, k_ref, v_ref, pt_ref, vec_own, vec_got, p_own, p_got, bias_ref,
    pre_rows, post_rows, join_ref, sum_ref, p_ref, dm_ref, ks_ref, da_ref, keep_ref, sems,
):
    first = lax.axis_index("pipe") == 0
    p_copy = fetch(first, p_own, p_got, p_ref, sems.at[0])
    length, width = mg_ref.shape[1], mg_ref.shape[2]
    lanes = q_ref.shape[1]
    size = width // HEADS
    root = size ** (-0.5)
    scale_row = chosen(first, vec_own[5:6].astype(F32), vec_got[5:6].astype(F32))
    bg = (mg_ref[b] * scale_row).astype(BF16)
    keep = keep_columns(first, mask_ref, keep_ref)[:length, b : b + 1]
    p_copy.wait()
    da = mm_nt(bg, p_ref[...]).astype(BF16)
    da_ref[:length] = da
    da_ref[length:] = jnp.zeros((lanes - length, width), BF16)
    da_t = transposed(da_ref[...].astype(F32))
    k_t = transposed(k_ref[b].astype(F32))
    low_v = v_ref[b, :length]
    val_f = low_v.astype(F32)
    key_f = k_ref[b, :length].astype(F32)
    da_f = da.astype(F32)
    biased = da_f * bias_ref[...]
    dv = keep * col_sum(biased) + (1.0 - keep) * biased
    bias_sum = col_sum(da_f * (col_sum(val_f * keep) + (1.0 - keep) * val_f))
    post_parts = []
    for c in range(HEADS):
        scaled = jnp.concatenate(
            [da_t[h * size : (h + 1) * size] * mixing[1, h, c] for h in range(HEADS)], axis=0
        ).astype(BF16)
        dp = mm(low_v, scaled)
        weights = pt_ref[b, c * lanes : c * lanes + length]
        w_f = weights.astype(F32)
        dm = w_f * (dp - col_sum(w_f * dp))
        dm_ref[c * lanes : c * lanes + length] = dm.astype(BF16)
        dm_ref[c * lanes + length : (c + 1) * lanes] = jnp.zeros((lanes - length, lanes), BF16)
        moved = mm(weights, da_ref[...])
        dv = dv + moved * post_rows[c : c + 1]
        post_parts.append(col_sum(moved * val_f))
        ks_ref[:, c * lanes : (c + 1) * lanes] = jnp.concatenate(
            [k_t[h * size : (h + 1) * size] * mixing[0, c, h] for h in range(HEADS)], axis=0
        ).astype(BF16)
    dk = jnp.zeros((length, width), F32)
    pre_parts = []
    for h in range(HEADS):
        moved = mm(dm_ref[h * lanes : h * lanes + length], q_ref[b])
        dk = dk + moved * pre_rows[h : h + 1]
        pre_parts.append(col_sum(moved * key_f))
    dq = transposed(mm(ks_ref[...], dm_ref[...]))[:length] * root
    join_ref[:, :width] = dq.astype(BF16)
    join_ref[:, width : 2 * width] = (dk * root).astype(BF16)
    join_ref[:, 2 * width :] = dv.astype(BF16)
    sum_ref[...] = jnp.concatenate(
        [part * root for part in pre_parts] + post_parts + [bias_sum, jnp.zeros((7, width), F32)], axis=0
    )


def input_gradients(
    mg_ref, rows_ref, hid_ref, att_ref, join0, join1, sum0, sum1, vec_in, vec_in1, vec_own, vec_got, w_own, w_got,
    class_other,
    send_ref, kept_ref, own_half, other_half, w_ref, join_ref, blocks, tall_ref, sems,
):
    first = lax.axis_index("pipe") == 0
    w_copy = fetch(first, w_own, w_got, w_ref, sems.at[0])
    length, width = rows_ref.shape[1], rows_ref.shape[2]
    size = width // HEADS
    flat = IMGS * length
    vec = chosen(first, vec_own[...].astype(F32), vec_got[...].astype(F32))
    mg = mg_ref[...].reshape(flat, width)
    bg = (mg * vec[5:6]).astype(BF16)
    pb_grad = col_sum(bg.astype(F32))
    put_blocks(blocks, mm_tn(att_ref[...].reshape(flat, width), bg), 0, (4, 3))
    join_ref[:length] = join0[...]
    join_ref[length:] = join1[...]
    hidden = hid_ref[...].reshape(flat, width)
    for k in range(3):
        put_blocks(blocks, mm_tn(hidden, join_ref[:, k * width : (k + 1) * width]), 0, (4, k))
    w_copy.wait()
    dh = mm_nt(join_ref[...], w_ref[...])
    normal, norm_scale = normed(token_rows(rows_ref).astype(F32))
    patch = mg + norm_back(normal, norm_scale, dh * vec[0:1])
    half = width // 2
    low_half, high_half = patch[:, :half], patch[:, half:]
    own_rows, other_rows = chosen(first, low_half, high_half), chosen(first, high_half, low_half)
    for b in range(IMGS):
        own_half[b] = transposed(own_rows[b * length : (b + 1) * length])
        other_half[b, :half] = transposed(other_rows[b * length : (b + 1) * length]).astype(BF16)
        other_half[b, half:] = jnp.zeros((16, length), BF16)
    other_half[0, half:, :half] = class_other[...]

    dq_sum = col_sum(join_ref[:, :width].astype(F32))
    dv_sum = col_sum(join_ref[:, 2 * width :].astype(F32))
    late = jnp.concatenate(
        [col_sum(dh * normal), col_sum(dh), dq_sum, dv_sum, pb_grad, jnp.zeros((11, width), F32)], axis=0
    )
    vec0 = vec_in[...] + late
    lane = lax.broadcasted_iota(jnp.int32, (width, 128), 1)
    feature = lax.broadcasted_iota(jnp.int32, (width, 128), 0)
    groups = jnp.where((feature >= lane * size) & (feature < lane * size + size), 1.0, 0.0)
    small = lax.dot_general(
        sum0[...] + sum1[...], groups, (((1,), (0,)), ((), ())),
        preferred_element_type=F32, precision=lax.Precision.HIGHEST,
    )
    tall_ref[...] = jnp.concatenate(
        [vec0[:, k * 128 : (k + 1) * 128] for k in range(3)]
        + [vec_in1[:, k * 128 : (k + 1) * 128] for k in range(3)]
        + [small, jnp.zeros((8, 128), F32)],
        axis=0,
    )
    filler = jnp.zeros((12, 128), F32)
    for n in range(32):
        blocks[n, 144:160] = jnp.concatenate([tall_ref[n * 4 : n * 4 + 4], filler], axis=0).astype(BF16)
    block_copy(blocks, kept_ref, 0, 16)
    block_copy(blocks, send_ref, 16, 16)


def assemble(own_half, half_got, class_own, patch_out, class_out, class_grad):
    first = lax.axis_index("pipe") == 0
    half, count = patch_out.shape[1:]
    for b in range(IMGS):
        mine, theirs = own_half[b, :, :count], half_got[b, :half, :count].astype(F32)
        patch_out[b] = chosen(first, mine, theirs)
        patch_out[IMGS + b] = chosen(first, theirs, mine)
    mine, theirs = class_own[...].astype(F32), half_got[0, half:, :half].astype(F32)
    for at, out in ((0, class_out), (8, class_grad)):
        pair = mine[at : at + IMGS], theirs[at : at + IMGS]
        rows = jnp.concatenate([chosen(first, *pair), chosen(first, *pair[::-1])], axis=0)
        out[...] = rows.astype(BF16)


def join_pieces(low, high, target):
    target[0:8] = low[:, : target.shape[1]]
    target[8:16] = high[:, : target.shape[1]]


def unpack(mine, other, block, start):
    source = mine if block < 16 else other
    at = block_position(block) & 15
    return [source[at, start + k * 48 : start + (k + 1) * 48].astype(F32) for k in range(3)]


def class_gradients(*refs):
    factor_refs = refs[:-19]
    w_in, p_in, f1_in, f2_in, vec, *outs = refs[-19:-10]
    w, p, f1, f2, factors, *held, sems = refs[-10:]
    width = p.shape[0]

    @pl.when(lax.axis_index("pipe") != 0)
    def _():
        copies = [
            pltpu.make_async_copy(source, target, sems.at[n])
            for n, (source, target) in enumerate(((f1_in, f1), (f2_in, f2), (w_in, w), (p_in, p)))
        ]
        for copy in copies:
            copy.start()
        join_factors(factor_refs, factors)
        group = min(32, factors.shape[0])
        rows = group * IMGS * HEADS
        mask = head_mask(rows, width)
        spread = (
            lax.broadcasted_iota(jnp.int32, (rows, group * IMGS), 0) >> 3
            == lax.broadcasted_iota(jnp.int32, (rows, group * IMGS), 1)
        )
        spread = jnp.where(spread, 1.0, 0.0).astype(BF16)
        bias = jnp.concatenate([vec[8 + k : 9 + k].astype(F32) for k in range(4)], axis=1)
        for copy in copies:
            copy.wait()

        def expanded(vectors):
            return jnp.where(mask, mm(spread, vectors), 0.0).astype(BF16)

        def put(n, at, target, cut, piece):
            target[:, cut] = piece if n == 0 else target[:, cut] + piece
            if n == factors.shape[0] // group - 1:
                done.append(pltpu.make_async_copy(target.at[:, cut], outs[at].at[:, cut], sems.at[4 + len(done)]))
                done[-1].start()

        done = []
        whole = slice(0, width)
        for n in range(factors.shape[0] // group):
            part = slice(n * group, (n + 1) * group)
            wh, g, vectors = (factor_rows(factors, part, start, group) for start in (0, 16, 32))
            hidden_c, att1, bg1, inner1, og1 = (picked(vectors, kind, group) for kind in range(5))
            active, slope = gelu_pair(mm(inner1, f1[...]) + bias)
            ig1 = (mm_nt(og1, f2[...]) * slope).astype(BF16)
            put(n, 3, held[3], whole, mm_tn(active.astype(BF16), og1))
            put(n, 2, held[2], slice(0, f1.shape[1]), mm_tn(inner1, ig1))
            query = (mm(hidden_c, w[:, :width]) + vec[2:3].astype(F32)).astype(BF16)
            da1 = mm_nt(bg1, p[...]).astype(BF16)
            chosen_g = jnp.where(mask, mm(g, w[:, width : 2 * width]), 0.0).astype(BF16)
            dq1 = mm_tn(spread, chosen_g).astype(BF16)
            put(n, 1, held[1], whole, mm_tn(att1, bg1))
            parts = (mm_tn(hidden_c, dq1), mm_tn(g, expanded(query)), mm_tn(wh, expanded(da1)))
            for k, piece in enumerate(parts):
                put(n, 0, held[0], slice(k * width, (k + 1) * width), piece)
        for copy in done:
            copy.wait()


def fc_outputs(mine_low, mine_high, other_low, other_high, fc1_in, fc2_in, fc1_out, fc2_out, mine, other, fc1, fc2, sems):
    del fc1_in, fc2_in

    @pl.when(lax.axis_index("pipe") == 0)
    def _():
        join_pieces(mine_low, mine_high, mine)
        join_pieces(other_low, other_high, other)
        copies = []
        for rb in range(8):
            for cb in range(4):
                block = rb * 4 + cb
                for k, piece in enumerate(unpack(mine, other, block, 0)):
                    fc1[rb * 48 : (rb + 1) * 48, cb * 384 + k * 128 : cb * 384 + (k + 1) * 128] = piece
                for k, piece in enumerate(unpack(mine, other, block, 144)):
                    fc2[block * 48 : (block + 1) * 48, k * 128 : (k + 1) * 128] = piece
            for n, (source, target, tall) in enumerate(((fc1, fc1_out, 48), (fc2, fc2_out, 192))):
                rows = pl.ds(rb * tall, tall)
                copies.append(pltpu.make_async_copy(source.at[rows], target.at[rows], sems.at[rb * 2 + n]))
                copies[-1].start()
        for copy in copies:
            copy.wait()


def join_factors(pieces, factors):
    at = 0
    for piece in pieces:
        count, start = piece.shape[0], piece.shape[1] - 144
        factors[at : at + count] = piece[:, start:]
        at += count


def factor_rows(factors, part, start, group):
    pieces = [factors[part, k * 48 + start : k * 48 + start + 16].reshape(group * 16, 128) for k in range(3)]
    return jnp.concatenate(pieces, axis=1)


def picked(vectors, kind, group):
    rows, cols = group * IMGS, group * 16
    row = lax.broadcasted_iota(jnp.int32, (rows, cols), 0)
    col = lax.broadcasted_iota(jnp.int32, (rows, cols), 1)
    wanted = (row >> 1) * 16 + kind * IMGS + (row & 1)
    return mm(jnp.where(col == wanted, 1.0, 0.0).astype(BF16), vectors).astype(BF16)


def qkv_outputs(mine_low, mine_high, other_low, other_high, qkv_in, proj_in, *refs):
    del qkv_in, proj_in
    qkv_out, proj_out = refs[:2]
    vec_outs, (pre_out, post_out, bias_out, mine, other, tall_ref, qkv, proj, sems) = refs[2:12], refs[12:]
    first = lax.axis_index("pipe") == 0
    width = proj_out.shape[0]
    join_pieces(mine_low, mine_high, mine)
    join_pieces(other_low, other_high, other)

    @pl.when(first)
    def _():
        for rb in range(8):
            rows = slice(rb * 48, (rb + 1) * 48)
            for cb in range(4):
                for k, piece in enumerate(unpack(mine, other, rb * 4 + cb, 0)):
                    if cb < 3:
                        qkv[rows, cb * 384 + k * 128 : cb * 384 + (k + 1) * 128] = piece
                    else:
                        proj[rows, k * 128 : (k + 1) * 128] = piece
            rows = pl.ds(rb * 48, 48)
            pltpu.make_async_copy(qkv.at[rows], qkv_out.at[rows], sems.at[rb]).start()
            pltpu.make_async_copy(proj.at[rows], proj_out.at[rows], sems.at[8 + rb]).start()

    for block in range(32):
        at = block_position(block) & 15
        here, there = mine[at, 144:160].astype(F32), other[at, 144:160].astype(F32)
        low = chosen(first, here, there) if block < 16 else chosen(first, there, here)
        tall_ref[block * 4 : block * 4 + 4] = low[0:4]
    rows = [
        chosen(first, tall_ref[k * 16 : (k + 1) * 16], tall_ref[48 + k * 16 : 48 + (k + 1) * 16]) for k in range(3)
    ]
    rows = jnp.concatenate(rows, axis=1)
    at = 0
    for out in vec_outs:
        for k in range(out.shape[1] // width):
            out[:, k * width : (k + 1) * width] = rows[at : at + 1]
            at += 1
    pre_out[...] = tall_ref[96:104, 0:HEADS]
    post_out[...] = tall_ref[104:112].T[0:HEADS]
    bias_out[...] = tall_ref[112:113, 0:HEADS]

    @pl.when(first)
    def _():
        for rb in range(8):
            rows = pl.ds(rb * 48, 48)
            pltpu.make_async_copy(qkv.at[rows], qkv_out.at[rows], sems.at[rb]).wait()
            pltpu.make_async_copy(proj.at[rows], proj_out.at[rows], sems.at[8 + rb]).wait()


VM = pl.BlockSpec(memory_space=pltpu.VMEM)
SM = pl.BlockSpec(memory_space=pltpu.SMEM)
HB = pl.BlockSpec(memory_space=pltpu.HBM)


def call(body, ins, outs, scratch, name, limit, sems=0, far=0, aliases=None):
    return pl.pallas_call(
        body,
        out_shape=[jax.ShapeDtypeStruct(shape, kind) for shape, kind in outs],
        in_specs=[spec for spec, _ in ins],
        out_specs=[HB] * far + [VM] * (len(outs) - far),
        scratch_shapes=[pltpu.VMEM(shape, kind) for shape, kind in scratch]
        + ([pltpu.SemaphoreType.DMA((sems,))] if sems else []),
        compiler_params=pltpu.CompilerParams(vmem_limit_bytes=limit * 1024 * 1024),
        cost_estimate=pl.CostEstimate(flops=0, bytes_accessed=1, transcendentals=0),
        input_output_aliases=aliases or {},
        name=name,
    )(*[value for _, value in ins])


def swapped(array):
    return lax.ppermute(array, "pipe", [(0, 1), (1, 0)])


def core_pairs(dp, bits):
    return [
        (core * dp + i, core * dp + (i ^ bit)) for core, bit in enumerate(bits) for i in range(dp)
    ]


def exchanged(array, bits):
    dp = lax.axis_size("dp")
    return lax.ppermute(array, ("pipe", "dp"), core_pairs(dp, bits))


def total(pieces, start, stop):
    parts = [piece[start:stop].astype(F32) for piece in pieces]
    return sum(parts[1:], parts[0]).astype(BF16)


def after(arrays, *others):
    return lax.optimization_barrier((arrays, others))[0]


NEAR, FAR = (4, 4), (8, 8)
LONG = (("halve", (1, 2)), ("halve", (2, 1)), ("halve", NEAR), ("swap", FAR), ("collect", NEAR), ("collect", (2, 1)), ("collect", (1, 2)))
SHORT = (("halve", (1, 2)), ("halve", (2, 1)), ("swap", NEAR), ("swap", FAR), ("collect", (2, 1)), ("collect", (1, 2)))
GATHER = (("collect", FAR), ("collect", NEAR), ("collect", (2, 1)), ("collect", (1, 2)))


class Stream:
    def __init__(self, pieces, steps):
        self.pieces, self.steps, self.at = list(pieces), steps, 0
        self.whole = lax.axis_size("dp") == 16
        self.leaving = self.pieces[0]

    def wait(self, *others):
        self.pieces = list(after(tuple(self.pieces), *others))

    def step(self):
        if not self.whole:
            return
        kind, bits = self.steps[self.at]
        self.at += 1
        count = min(piece.shape[0] for piece in self.pieces)
        if kind == "halve":
            self.leaving = total(self.pieces, count // 2, count)
            self.pieces = [piece[: count // 2] for piece in self.pieces] + [exchanged(self.leaving, bits)]
        elif kind == "swap":
            run = 1 if bits == FAR else 2
            starts = [at ^ run for at in range(0, count, run)]
            self.leaving = jnp.concatenate([total(self.pieces, at, at + run) for at in starts], axis=0)
            self.pieces = [total(self.pieces, 0, count), exchanged(self.leaving, bits)]
            if self.steps[self.at][0] == "collect":
                self.pieces = [total(self.pieces, 0, count)]
        else:
            self.leaving = jnp.concatenate(self.pieces, axis=0) if len(self.pieces) > 1 else self.pieces[0]
            self.pieces = [self.leaving, exchanged(self.leaving, bits)]

    def halves(self):
        if self.whole:
            return self.pieces
        whole = lax.psum(total(self.pieces, 0, 16).astype(F32), "dp").astype(BF16)
        return whole[:8], whole[8:]


def local(
    patches, class_token, keep_mask, class_cotangent, norm1_gain, norm1_bias, qkv_weight, qv_bias,
    mix_pre, mix_post, post_bias, proj_weight, proj_bias, scale_attn, norm2_gain, norm2_bias,
    fc1_weight, fc1_bias, fc2_weight, fc2_bias, scale_mlp,
):
    dp = lax.axis_size("dp")
    images, count, width = patches.shape
    hidden_width = fc1_weight.shape[2]
    length, lanes = 208, 256
    half = width // 2
    flat = IMGS * length

    w_own, p_own, f1_own, f2_own = qkv_weight[0], proj_weight[0], fc1_weight[0], fc2_weight[0]
    w_got = swapped(w_own)
    small = (
        norm1_gain, norm1_bias, qv_bias, proj_bias, scale_attn, norm2_gain, norm2_bias, fc1_bias, fc2_bias, scale_mlp,
        mix_pre, mix_post, post_bias[None],
    )
    vec_own, pre_rows, post_rows, bias_row = call(
        prepare,
        [(HB, array) for array in small],
        [((16, width), BF16), ((HEADS, width), F32), ((HEADS, width), F32), ((1, width), F32)],
        [(array.shape, BF16) for array in small],
        "prepare",
        LIMIT_P,
        sems=13,
    )
    vec_got = swapped(vec_own)
    p_late, f1_late, f2_late = after((p_own, f1_own, f2_own), w_got)
    p_got, f1_got, f2_got = swapped(p_late), swapped(f1_late), swapped(f2_late)
    mixing = jnp.stack([mix_pre, mix_post]).astype(F32)
    rows = jnp.pad(patches, ((0, 0), (0, length - count), (0, 0)))

    token_shape = (IMGS, length, width)
    wide_shape = (IMGS, lanes, width)
    keep_scratch = ((8, lanes), F32)
    att, hid, queries, keys, values, probs = call(
        attention_forward,
        [(SM, mixing), (VM, rows), (VM, keep_mask), (VM, vec_own), (VM, vec_got), (HB, w_own), (HB, w_got),
         (VM, bias_row)],
        [(token_shape, BF16), (token_shape, BF16), (wide_shape, BF16), (wide_shape, BF16), (wide_shape, BF16),
         ((IMGS, HEADS * lanes, lanes), BF16)],
        [((width, 3 * width), BF16), ((width, HEADS * lanes), BF16), keep_scratch],
        "attention_forward",
        LIMIT_A,
        sems=1,
    )
    vec_shape = (16, width)
    send1, kept1, mg, vec0, vec1, class_own, class_other, factors = call(
        middle_kernel,
        [(VM, att), (VM, rows), (VM, keep_mask), (VM, class_token), (VM, class_cotangent), (VM, vec_own),
         (VM, vec_got), (HB, p_own), (HB, p_got), (HB, f1_own), (HB, f1_got), (HB, f2_own), (HB, f2_got), (HB, w_own),
         (HB, w_got)],
        [((16, 288, 128), BF16), ((16, 288, 128), BF16), (token_shape, F32), (vec_shape, F32), (vec_shape, F32),
         ((16, half), BF16), ((16, half), BF16), ((144, 128), BF16)],
        [((width, width), BF16), ((width, hidden_width), BF16), ((hidden_width, width), BF16),
         ((width, width), BF16), ((width, hidden_width), BF16), ((hidden_width, width), BF16),
         ((width, 3 * width), BF16), ((flat, hidden_width), BF16), ((flat, hidden_width), BF16),
         ((32, 288, 128), BF16), keep_scratch],
        "middle_kernel",
        LIMIT_B,
        sems=7,
    )

    def image_backward(b, mg):
        return call(
            lambda *refs: attention_backward(b, *refs),
            [(SM, mixing), (VM, mg), (VM, keep_mask), (VM, queries), (VM, keys), (VM, values), (VM, probs),
             (VM, vec_own), (VM, vec_got), (HB, p_own), (HB, p_got), (VM, bias_row), (VM, pre_rows), (VM, post_rows)],
            [((length, 3 * width), BF16), ((24, width), F32)],
            [((width, width), BF16), ((HEADS * lanes, lanes), BF16), ((width, HEADS * lanes), BF16),
             ((lanes, width), BF16), keep_scratch],
            f"attention_backward_{b}",
            LIMIT_C,
            sems=1,
        )

    got1 = swapped(send1)
    stream1, shared = Stream((kept1, got1), LONG), Stream((factors[None],), GATHER)
    join0, sum0 = image_backward(0, mg)
    stream1.wait(join0)
    stream1.step()
    join1, sum1 = image_backward(1, after(mg, stream1.leaving))
    mg = after(mg, join1)
    send2, kept2, own_half, other_half = call(
        input_gradients,
        [(VM, mg), (VM, rows), (VM, hid), (VM, att), (VM, join0), (VM, join1), (VM, sum0), (VM, sum1), (VM, vec0),
         (VM, vec1), (VM, vec_own), (VM, vec_got), (HB, w_own), (HB, w_got), (VM, class_other)],
        [((16, 160, 128), BF16), ((16, 160, 128), BF16), ((IMGS, half, length), F32), ((IMGS, half + 16, length), BF16)],
        [((width, 3 * width), BF16), ((flat, 3 * width), BF16), ((32, 160, 128), BF16), ((128, 128), F32)],
        "input_gradients",
        LIMIT_C,
        sems=1,
    )
    got2, half_got = swapped(send2), swapped(other_half)
    patch_out, class_result, class_grad = call(
        assemble,
        [(VM, own_half), (VM, half_got), (VM, class_own)],
        [((2 * IMGS, half, count), F32), ((2 * IMGS, half), BF16), ((2 * IMGS, half), BF16)],
        [],
        "assemble",
        LIMIT_C,
    )

    def turn(*streams):
        for stream in streams:
            turn.last = stream.wait(*turn.last) or (stream.step(), stream.leaving)[1:]

    turn.last = (kept2,)
    stream2 = Stream((kept2, got2), SHORT)
    turn(stream1, stream2)
    stream1.wait(half_got)
    turn(stream1, stream2, shared, stream1, stream2, shared, stream1, stream2, shared, stream1, shared, stream2, stream1)
    stream2.wait(patch_out, class_result, class_grad)
    turn(stream2)
    if dp == 16:
        factor_parts = after(tuple(shared.pieces), stream2.leaving)
    else:
        factor_parts = (lax.all_gather(factors, "dp"),)
    factor_parts += tuple(swapped(part) for part in factor_parts)
    low1, high1 = stream1.halves()
    matrices = [((width, 3 * width), F32), ((width, width), F32), ((width, hidden_width), F32), ((hidden_width, width), F32)]
    qkv1, proj1, fc11, fc21 = call(
        class_gradients,
        [(VM, part) for part in factor_parts]
        + [(HB, w_own), (HB, p_own), (HB, f1_own), (HB, f2_own), (VM, vec_own)],
        matrices,
        [(shape, BF16) for shape, _ in matrices] + [((2 * dp, 144, 128), BF16)] + matrices,
        "class_gradients",
        LIMIT_E,
        sems=10,
        far=4,
    )
    low1_other, high1 = swapped(low1), after(high1, fc11)
    high1_other = swapped(high1)
    low2, high2 = stream2.halves()
    low2_other = swapped(low2)
    fc1_out, fc2_out = call(
        fc_outputs,
        [(VM, low1), (VM, high1), (VM, low1_other), (VM, high1_other), (HB, fc11), (HB, fc21)],
        matrices[2:],
        [((16, 288, 128), BF16), ((16, 288, 128), BF16)] + matrices[2:],
        "fc_outputs",
        LIMIT_D,
        sems=16,
        far=2,
        aliases={4: 0, 5: 1},
    )
    high2 = after(high2, fc1_out)
    high2_other = swapped(high2)
    qkv_out, proj_out, *small_outs = call(
        qkv_outputs,
        [(VM, low2), (VM, high2), (VM, low2_other), (VM, high2_other), (HB, qkv1), (HB, proj1)],
        matrices[:2]
        + [((1, size * width), F32) for size in (1, 1, 2, 1, 1, 1, 1, 4, 1, 1)]
        + [((HEADS, HEADS), F32), ((HEADS, HEADS), F32), ((1, HEADS), F32)],
        [((16, 160, 128), BF16), ((16, 160, 128), BF16), ((128, 128), F32)] + matrices[:2],
        "qkv_outputs",
        LIMIT_D,
        sems=16,
        far=2,
        aliases={4: 0, 5: 1},
    )
    n1g, n1b, qvb, pb, sa, n2g, n2b, f1b, f2b, sm, pre, post, bias = small_outs
    return (
        class_result, patch_out.transpose(0, 2, 1), class_grad, n1g, n1b, qkv_out[None], qvb, proj_out[None], pb, sa, n2g, n2b,
        fc1_out[None], f1b, fc2_out[None], f2b, sm, pre, post, bias[0],
    )


def solution(mesh):
    stacked = (P("pipe", None), P("pipe", None), P("pipe", None, None))
    row, _, cube = stacked
    return jax.shard_map(
        local,
        mesh=mesh,
        in_specs=(
            P("dp", None, None), P("dp", None), P("dp", None), P("dp", None),
            row, row, cube, row, P(), P(), P(), cube, row, row, row, row, cube, row, cube, row, row,
        ),
        out_specs=(
            P("dp", "pipe"), P("dp", None, "pipe"), P("dp", "pipe"),
            row, row, cube, row, cube, row, row, row, row, cube, row, cube, row, row, P(), P(), P(),
        ),
        check_vma=False,
    )
```

```python
import jax
import jax.numpy as jnp
from jax import lax
from jax.experimental import pallas as pl
from jax.experimental.pallas import tpu as pltpu
from jax.sharding import PartitionSpec as P

HEADS = 8
IMGS = 2
LIMIT_P, LIMIT_A, LIMIT_B, LIMIT_C, LIMIT_D, LIMIT_E = 60, 24, 24, 24, 24, 24
LOG2E = 1.4426950408889634
F32 = jnp.float32
BF16 = jnp.bfloat16


def mm(left, right):
    return lax.dot_general(left, right, (((1,), (0,)), ((), ())), preferred_element_type=F32)


def mm_nt(left, right):
    return lax.dot_general(left, right, (((1,), (1,)), ((), ())), preferred_element_type=F32)


def mm_tn(left, right):
    return lax.dot_general(left, right, (((0,), (0,)), ((), ())), preferred_element_type=F32)


def normed(rows):
    centred = rows - jnp.mean(rows, -1, keepdims=True)
    scale = lax.rsqrt(jnp.mean(centred * centred, -1, keepdims=True) + 1e-06)
    return centred * scale, scale


def norm_back(normal, scale, grad):
    inner = jnp.mean(grad * normal, -1, keepdims=True)
    return (grad - jnp.mean(grad, -1, keepdims=True) - normal * inner) * scale


def col_sum(rows):
    return jnp.sum(rows, axis=0, keepdims=True)


def gelu_pair(rows):
    phi = 0.5 + 0.5 * lax.erf(rows * 0.7071067811865476)
    return rows * phi, phi + rows * (jnp.exp2(rows * rows * (-0.5 * LOG2E)) * 0.3989422804014327)


def head_mask(rows, width):
    lane = lax.broadcasted_iota(jnp.int32, (rows, width), 1)
    head = lax.rem(lax.broadcasted_iota(jnp.int32, (rows, width), 0), HEADS)
    size = width // HEADS
    return (lane >= head * size) & (lane < head * size + size)


def chosen(is_first, first, other):
    return jnp.where(is_first, first, other)


def scaled_rows(rows, factors):
    size = rows.shape[0] // HEADS
    parts = []
    for head, factor in enumerate(factors):
        part = rows[head * size : (head + 1) * size]
        parts.append(part * jnp.full((1, rows.shape[1]), factor, F32).astype(BF16))
    return jnp.concatenate(parts, axis=0)


def transposed(rows):
    return rows.T


def own_place():
    core = lax.axis_index("pipe")
    return core, core * 16 + (lax.axis_index("dp") if lax.axis_size("dp") == 16 else 0)


def fetch(first, own, got, target, sem):
    @pl.when(first)
    def _():
        pltpu.make_async_copy(own, target, sem).start()

    @pl.when(jnp.logical_not(first))
    def _():
        pltpu.make_async_copy(got, target, sem).start()

    return pltpu.make_async_copy(own, target, sem)


def own_images(first, rows):
    return chosen(first, rows[0:IMGS], rows[IMGS : 2 * IMGS])


def token_rows(rows_ref):
    rows = rows_ref[pl.ds(lax.axis_index("pipe") * IMGS, IMGS)]
    return rows.reshape(-1, rows.shape[2])


def keep_columns(first, mask_ref, scratch):
    scratch[...] = jnp.zeros_like(scratch)
    scratch[0:IMGS, 0 : mask_ref.shape[1]] = own_images(first, mask_ref[...].astype(F32))
    return scratch[...].T


def prepare(*refs):
    sources, (vec_ref, pre_ref, post_ref, bias_ref), held, sems = refs[:13], refs[13:17], refs[17:30], refs[30]
    copies = [pltpu.make_async_copy(*pair, sems.at[n]) for n, pair in enumerate(zip(sources, held))]
    for copy in copies:
        copy.start()
    for copy in copies:
        copy.wait()
    n1g, n1b, qvb, pb, sa, n2g, n2b, f1b, f2b, sm, pre, post, post_bias = held
    width = n1g.shape[1]
    rows = [n1g[...], n1b[...], qvb[:, :width], qvb[:, width:], pb[...], sa[...], n2g[...], n2b[...]]
    rows += [f1b[:, k * width : (k + 1) * width] for k in range(4)] + [f2b[...], sm[...]]
    rows = [row.astype(F32) for row in rows] + [jnp.zeros((2, width), F32)]
    vec_ref[...] = jnp.concatenate(rows, axis=0).astype(BF16)
    spread = jnp.where(head_mask(HEADS, width), 1.0, 0.0).astype(BF16)
    pre_ref[...] = mm(pre[...], spread)
    post_ref[...] = mm_tn(post[...], spread)
    bias_ref[...] = mm(post_bias[...], spread)


def attention_forward(
    mixing, rows_ref, mask_ref, vec_own, vec_got, w_own, w_got, bias_ref,
    att_ref, hid_ref, q_ref, k_ref, v_ref, pt_ref, w_ref, vs_ref, keep_ref, sems,
):
    first = lax.axis_index("pipe") == 0
    weights_copy = fetch(first, w_own, w_got, w_ref, sems.at[0])
    width = rows_ref.shape[2]
    length = rows_ref.shape[1]
    lanes = q_ref.shape[1]
    size = width // HEADS
    keeps = keep_columns(first, mask_ref, keep_ref)

    vec = chosen(first, vec_own[...].astype(F32), vec_got[...].astype(F32))
    scale = size ** (-0.5) * LOG2E
    pad_rows = jnp.zeros((lanes - length, width), BF16)
    same = lax.broadcasted_iota(jnp.int32, (length, lanes), 0) == lax.broadcasted_iota(jnp.int32, (length, lanes), 1)

    for b in range(IMGS):
        normal, _ = normed(rows_ref[lax.axis_index("pipe") * IMGS + b].astype(F32))
        hidden = (normal * vec[0:1] + vec[1:2]).astype(BF16)
        hid_ref[b] = hidden
        if b == 0:
            weights_copy.wait()
        joined = mm(hidden, w_ref[...])
        queries = joined[:, :width] + vec[2:3]
        keys = joined[:, width : 2 * width]
        values = joined[:, 2 * width :] + vec[3:4]
        low_k = keys.astype(BF16)
        low_v = values.astype(BF16)
        q_ref[b, :length] = queries.astype(BF16)
        k_ref[b, :length] = low_k
        v_ref[b, :length] = low_v
        q_ref[b, length:] = pad_rows
        k_ref[b, length:] = pad_rows
        v_ref[b, length:] = pad_rows
        q_t = transposed(q_ref[b])
        v_t = transposed(v_ref[b])
        keep = keeps[:length, b : b + 1]
        allowed = (keep > 0.0) | same
        for h in range(HEADS):
            scaled_q = scaled_rows(q_t, [mixing[0, h, c] for c in range(HEADS)])
            scores = jnp.where(allowed, mm(low_k, scaled_q) * scale, -1e30)
            top = jnp.max(scores, axis=0, keepdims=True)
            weights = jnp.exp2(scores - top)
            weights = weights * (1.0 / jnp.sum(weights, axis=0, keepdims=True))
            pt_ref[b, h * lanes : h * lanes + length] = weights.astype(BF16)
            pt_ref[b, h * lanes + length : (h + 1) * lanes] = jnp.zeros((lanes - length, lanes), BF16)
            vs_ref[:, h * lanes : (h + 1) * lanes] = scaled_rows(v_t, [mixing[1, c, h] for c in range(HEADS)])
        mixed = transposed(mm(vs_ref[...], pt_ref[b]))[:length]
        low_f = low_v.astype(F32)
        extra = bias_ref[...] * (col_sum(low_f * keep) + (1.0 - keep) * low_f)
        att_ref[b] = (mixed + extra).astype(BF16)


def block_copy(source, target, start, count):
    for n in range(count):
        target[n] = source[position_block(start + n)]


def position_block(at):
    core, me = own_place()
    first_bit, second_bit = (at >> 3) & 1, (at >> 2) & 1
    rest = ((at >> 4) << 4) | ((at & 1) << 3) | (((at >> 1) & 1) << 2)
    x_first = rest | first_bit | (second_bit << 1)
    y_first = rest | second_bit | (first_bit << 1)
    return jnp.where(core == (at >> 4), x_first, y_first) ^ me


def block_position(block):
    core, me = own_place()
    apart = block ^ me
    x_bit, y_bit = apart & 1, (apart >> 1) & 1
    half = apart >> 4
    top = jnp.where(core == half, (x_bit << 3) | (y_bit << 2), (y_bit << 3) | (x_bit << 2))
    return (half << 4) | top | (((apart >> 2) & 1) << 1) | ((apart >> 3) & 1)


def put_blocks(target, rows, start, wide):
    tall, across = 48, 384
    for rb in range(rows.shape[0] // tall):
        for cb in range(rows.shape[1] // across):
            block = rb * wide[0] + wide[1] + cb
            for k in range(3):
                piece = rows[rb * tall : (rb + 1) * tall, cb * across + k * 128 : cb * across + (k + 1) * 128]
                target[block, start + k * tall : start + (k + 1) * tall] = piece.astype(BF16)


def middle_kernel(
    att_ref, rows_ref, mask_ref, class_ref, cot_ref,
    vec_own, vec_got, p_own, p_got, f1_own, f1_got, f2_own, f2_got, w_own, w_got,
    send_ref, kept_ref, mg_ref, vec_out, vec_out1, class_own, class_other, factor_ref,
    p0_ref, f10, f20, p1_ref, f11, f21, w1_ref, act_ref, gp_ref, blocks, keep_ref, sems,
):
    first = lax.axis_index("pipe") == 0
    p0_copy = fetch(first, p_own, p_got, p0_ref, sems.at[0])
    f10_copy = fetch(first, f1_own, f1_got, f10, sems.at[1])
    f20_copy = fetch(first, f2_own, f2_got, f20, sems.at[2])
    w1_copy = fetch(first, w_got, w_own, w1_ref, sems.at[3])
    p1_copy = fetch(first, p_got, p_own, p1_ref, sems.at[4])
    f11_copy = fetch(first, f1_got, f1_own, f11, sems.at[5])
    f21_copy = fetch(first, f2_got, f2_own, f21, sems.at[6])
    length, width = rows_ref.shape[1], rows_ref.shape[2]
    flat = IMGS * length
    size = width // HEADS
    patches = mask_ref.shape[1]
    keep_ref[...] = jnp.zeros_like(keep_ref)
    keep_ref[0:IMGS, 0:patches] = own_images(first, mask_ref[...].astype(F32))
    keep_rows = keep_ref[0:IMGS, :length]
    keep_lane = lax.broadcasted_iota(jnp.int32, (IMGS, length), 1)
    keep_rows = jnp.where(keep_lane == patches, 1.0, keep_rows)

    own, got = vec_own[...].astype(F32), vec_got[...].astype(F32)
    vec, vec1 = chosen(first, own, got), chosen(first, got, own)

    def wide_bias(v):
        return jnp.concatenate([v[8 + k : 9 + k] for k in range(4)], axis=1)

    p0_copy.wait()
    branch = mm(att_ref[...].reshape(flat, width), p0_ref[...]) + vec[4:5]
    middle = token_rows(rows_ref).astype(F32) + vec[5:6] * branch
    normal, norm_scale = normed(middle)
    inner_low = (normal * vec[6:7] + vec[7:8]).astype(BF16)
    bias = wide_bias(vec)
    step = 384
    f10_copy.wait()
    for k in range(4):
        cut = slice(k * step, (k + 1) * step)
        inner = mm(inner_low, f10[:, cut]) + bias[:, cut]
        active, slope = gelu_pair(inner)
        act_ref[:, cut] = active.astype(BF16)
        gp_ref[:, cut] = slope.astype(BF16)
    f20_copy.wait()
    outer = mm(act_ref[...], f20[...]) + vec[12:13]
    sent = (middle + vec[13:14] * outer).astype(BF16).astype(F32)

    blank = jnp.zeros((8 - IMGS, width), F32)
    class_rows = jnp.concatenate([own_images(first, class_ref[...].astype(F32)), blank], axis=0)
    w1_copy.wait()
    normal_c, _ = normed(class_rows)
    hidden_c = (normal_c * vec1[0:1] + vec1[1:2]).astype(BF16)
    query = (mm(hidden_c, w1_ref[:, :width]) + vec1[2:3]).astype(BF16).astype(F32)
    mask = head_mask(IMGS * HEADS, width)

    def spread(rows):
        both = jnp.concatenate(
            [jnp.broadcast_to(rows[b : b + 1], (HEADS, width)) for b in range(IMGS)], axis=0
        )
        return jnp.where(mask, both, 0.0)

    def gathered(rows):
        kept = jnp.where(mask, rows, 0.0)
        parts = [col_sum(kept[b * HEADS : (b + 1) * HEADS]) for b in range(IMGS)]
        return jnp.concatenate(parts + [jnp.zeros((8 - IMGS, width), F32)], axis=0)

    query_rows = mm_nt(spread(query).astype(BF16), w1_ref[:, width : 2 * width]).astype(BF16)
    at_row = lax.broadcasted_iota(jnp.int32, (length, width), 0)
    hiddens, normals, scales, probs, low_probs, sums, whs = [], [], [], [], [], [], []
    for b in range(IMGS):
        tokens = jnp.where(at_row == patches, class_rows[b : b + 1], sent[b * length : (b + 1) * length])
        n1, s1 = normed(tokens)
        h1 = (n1 * vec1[0:1] + vec1[1:2]).astype(BF16)
        scores = mm_nt(query_rows[b * HEADS : (b + 1) * HEADS], h1) * (size ** (-0.5) * LOG2E)
        scores = jnp.where(keep_rows[b : b + 1] > 0.0, scores, -1e30)
        weights = jnp.exp2(scores - jnp.max(scores, axis=-1, keepdims=True))
        weights = weights / jnp.sum(weights, axis=-1, keepdims=True)
        low = weights.astype(BF16)
        hiddens.append(h1)
        normals.append(n1)
        scales.append(s1)
        probs.append(weights)
        low_probs.append(low)
        sums.append(jnp.sum(low.astype(F32), axis=-1, keepdims=True))
        whs.append(mm(low, h1))
    wh = jnp.concatenate(whs, axis=0).astype(BF16)
    prob_sum = gathered(jnp.broadcast_to(jnp.concatenate(sums, axis=0), (IMGS * HEADS, width)))
    att1 = (gathered(mm(wh, w1_ref[:, 2 * width :])) + vec1[3:4] * prob_sum).astype(BF16)
    p1_copy.wait()
    branch1 = mm(att1, p1_ref[...]) + vec1[4:5]
    middle1 = class_rows + vec1[5:6] * branch1
    normal2, scale2 = normed(middle1)
    inner1 = (normal2 * vec1[6:7] + vec1[7:8]).astype(BF16)
    f11_copy.wait()
    f21_copy.wait()
    active1, slope1 = gelu_pair(mm(inner1, f11[...]) + wide_bias(vec1))
    outer1 = mm(active1.astype(BF16), f21[...]) + vec1[12:13]
    class_result = middle1 + vec1[13:14] * outer1

    upper1 = jnp.concatenate([own_images(first, cot_ref[...].astype(F32)), blank], axis=0)
    og1 = (upper1 * vec1[13:14]).astype(BF16)
    ig1 = (mm_nt(og1, f21[...]) * slope1).astype(BF16)
    dh2 = mm_nt(ig1, f11[...])
    mg1 = upper1 + norm_back(normal2, scale2, dh2 * vec1[6:7])
    bg1 = (mg1 * vec1[5:6]).astype(BF16)
    da1 = mm_nt(bg1, p1_ref[...]).astype(BF16).astype(F32)
    value_rows = mm_nt(spread(da1).astype(BF16), w1_ref[:, 2 * width :]).astype(BF16)
    low_grads, gs = [], []
    for b in range(IMGS):
        part = slice(b * HEADS, (b + 1) * HEADS)
        dw = mm_nt(value_rows[part], hiddens[b])
        ds = probs[b] * (dw - jnp.sum(probs[b] * dw, axis=-1, keepdims=True))
        low = (ds * size ** (-0.5)).astype(BF16)
        low_grads.append(low)
        gs.append(mm(low, hiddens[b]))
    g_rows = jnp.concatenate(gs, axis=0).astype(BF16)
    dq1 = gathered(mm(g_rows, w1_ref[:, width : 2 * width])).astype(BF16)
    dclass = mm_nt(dq1, w1_ref[:, :width])
    uppers, class_grads = [], []
    n1g, n1b = jnp.zeros((1, width), F32), jnp.zeros((1, width), F32)
    for b in range(IMGS):
        part = slice(b * HEADS, (b + 1) * HEADS)
        left = jnp.concatenate([low_grads[b], low_probs[b]], axis=0)
        right = jnp.concatenate([query_rows[part], value_rows[part]], axis=0)
        dh1 = mm_tn(left, right)
        dh1 = jnp.where(at_row == patches, dh1 + dclass[b : b + 1], dh1)
        n1g = n1g + col_sum(dh1 * normals[b])
        n1b = n1b + col_sum(dh1)
        dtokens = norm_back(normals[b], scales[b], dh1 * vec1[0:1])
        class_grads.append(dtokens[patches : patches + 1] + mg1[b : b + 1])
        uppers.append(jnp.where(at_row < patches, dtokens, 0.0).astype(BF16).astype(F32))
    upper = jnp.concatenate(uppers, axis=0)
    class_rows = jnp.concatenate([class_result] + class_grads + [blank], axis=0)
    low_half, high_half = class_rows[:, : width // 2], class_rows[:, width // 2 :]
    class_own[...] = chosen(first, low_half, high_half).astype(BF16)
    class_other[...] = chosen(first, high_half, low_half).astype(BF16)
    ig1_sum = col_sum(ig1.astype(F32))
    vec_out1[...] = jnp.concatenate(
        [
            n1g,
            n1b,
            col_sum(dq1.astype(F32)),
            col_sum(da1 * prob_sum),
            col_sum(bg1.astype(F32)),
            col_sum(mg1 * branch1),
            col_sum(dh2 * normal2),
            col_sum(dh2),
        ]
        + [ig1_sum[:, k * width : (k + 1) * width] for k in range(4)]
        + [col_sum(og1.astype(F32)), col_sum(upper1 * outer1), jnp.zeros((2, width), F32)],
        axis=0,
    )
    pieces = [piece.astype(F32)[0:IMGS] for piece in (hidden_c, att1, bg1, inner1, og1)]
    vectors = jnp.concatenate(pieces + [jnp.zeros((16 - 5 * IMGS, width), F32)], axis=0).astype(BF16)
    for k in range(3):
        lanes = slice(k * 128, (k + 1) * 128)
        factor_ref[k * 48 : k * 48 + 16] = wh[:, lanes]
        factor_ref[k * 48 + 16 : k * 48 + 32] = g_rows[:, lanes]
        factor_ref[k * 48 + 32 : k * 48 + 48] = vectors[:, lanes]

    sm_grad = col_sum(upper * outer)
    og = (upper * vec[13:14]).astype(BF16)
    put_blocks(blocks, mm_tn(act_ref[...], og), 144, (1, 0))
    dh = jnp.zeros((flat, width), F32)
    fc1_sums = []
    for k in range(4):
        cut = slice(k * step, (k + 1) * step)
        ig = (mm_nt(og, f20[cut, :]) * gp_ref[:, cut].astype(F32)).astype(BF16)
        fc1_sums.append(col_sum(ig.astype(F32)))
        put_blocks(blocks, mm_tn(inner_low, ig), 0, (4, k))
        dh = dh + mm_nt(ig, f10[:, cut])
    mg = upper + norm_back(normal, norm_scale, dh * vec[6:7])
    mg_ref[...] = mg.reshape(IMGS, length, width)
    vec_out[...] = jnp.concatenate(
        [jnp.zeros((4, width), F32), jnp.zeros((1, width), F32), col_sum(mg * branch), col_sum(dh * normal), col_sum(dh)]
        + fc1_sums
        + [col_sum(og.astype(F32)), sm_grad, jnp.zeros((2, width), F32)],
        axis=0,
    )
    block_copy(blocks, kept_ref, 0, 16)
    block_copy(blocks, send_ref, 16, 16)
    send_ref[16, 0:144] = factor_ref[...]
    send_ref[16, 144:288] = jnp.zeros((144, 128), BF16)


def attention_backward(
    b, mixing, mg_ref, mask_ref, q_ref, k_ref, v_ref, pt_ref, vec_own, vec_got, p_own, p_got, bias_ref,
    pre_rows, post_rows, join_ref, sum_ref, p_ref, dm_ref, ks_ref, da_ref, keep_ref, sems,
):
    first = lax.axis_index("pipe") == 0
    p_copy = fetch(first, p_own, p_got, p_ref, sems.at[0])
    length, width = mg_ref.shape[1], mg_ref.shape[2]
    lanes = q_ref.shape[1]
    size = width // HEADS
    root = size ** (-0.5)
    scale_row = chosen(first, vec_own[5:6].astype(F32), vec_got[5:6].astype(F32))
    bg = (mg_ref[b] * scale_row).astype(BF16)
    keep = keep_columns(first, mask_ref, keep_ref)[:length, b : b + 1]
    p_copy.wait()
    da = mm_nt(bg, p_ref[...]).astype(BF16)
    da_ref[:length] = da
    da_ref[length:] = jnp.zeros((lanes - length, width), BF16)
    da_t = transposed(da_ref[...])
    k_t = transposed(k_ref[b])
    low_v = v_ref[b, :length]
    val_f = low_v.astype(F32)
    key_f = k_ref[b, :length].astype(F32)
    da_f = da.astype(F32)
    biased = da_f * bias_ref[...]
    dv = keep * col_sum(biased) + (1.0 - keep) * biased
    bias_sum = col_sum(da_f * (col_sum(val_f * keep) + (1.0 - keep) * val_f))
    post_parts = []
    for c in range(HEADS):
        scaled = scaled_rows(da_t, [mixing[1, h, c] for h in range(HEADS)])
        dp = mm(low_v, scaled)
        weights = pt_ref[b, c * lanes : c * lanes + length]
        w_f = weights.astype(F32)
        dm = w_f * (dp - col_sum(w_f * dp))
        dm_ref[c * lanes : c * lanes + length] = dm.astype(BF16)
        dm_ref[c * lanes + length : (c + 1) * lanes] = jnp.zeros((lanes - length, lanes), BF16)
        moved = mm(weights, da_ref[...])
        dv = dv + moved * post_rows[c : c + 1]
        post_parts.append(col_sum(moved * val_f))
        ks_ref[:, c * lanes : (c + 1) * lanes] = scaled_rows(k_t, [mixing[0, c, h] for h in range(HEADS)])
    dk = jnp.zeros((length, width), F32)
    pre_parts = []
    for h in range(HEADS):
        moved = mm(dm_ref[h * lanes : h * lanes + length], q_ref[b])
        dk = dk + moved * pre_rows[h : h + 1]
        pre_parts.append(col_sum(moved * key_f))
    dq = transposed(mm(ks_ref[...], dm_ref[...]))[:length] * root
    join_ref[:, :width] = dq.astype(BF16)
    join_ref[:, width : 2 * width] = (dk * root).astype(BF16)
    join_ref[:, 2 * width :] = dv.astype(BF16)
    sum_ref[...] = jnp.concatenate(
        [part * root for part in pre_parts] + post_parts + [bias_sum, jnp.zeros((7, width), F32)], axis=0
    )


def input_gradients(
    mg_ref, rows_ref, hid_ref, att_ref, join0, join1, sum0, sum1, vec_in, vec_in1, vec_own, vec_got, w_own, w_got,
    class_other,
    send_ref, kept_ref, own_half, other_half, w_ref, join_ref, blocks, tall_ref, sems,
):
    first = lax.axis_index("pipe") == 0
    w_copy = fetch(first, w_own, w_got, w_ref, sems.at[0])
    length, width = rows_ref.shape[1], rows_ref.shape[2]
    size = width // HEADS
    flat = IMGS * length
    vec = chosen(first, vec_own[...].astype(F32), vec_got[...].astype(F32))
    mg = mg_ref[...].reshape(flat, width)
    bg = (mg * vec[5:6]).astype(BF16)
    pb_grad = col_sum(bg.astype(F32))
    put_blocks(blocks, mm_tn(att_ref[...].reshape(flat, width), bg), 0, (4, 3))
    join_ref[:length] = join0[...]
    join_ref[length:] = join1[...]
    hidden = hid_ref[...].reshape(flat, width)
    for k in range(3):
        put_blocks(blocks, mm_tn(hidden, join_ref[:, k * width : (k + 1) * width]), 0, (4, k))
    w_copy.wait()
    dh = mm_nt(join_ref[...], w_ref[...])
    normal, norm_scale = normed(token_rows(rows_ref).astype(F32))
    patch = mg + norm_back(normal, norm_scale, dh * vec[0:1])
    half = width // 2
    low_half, high_half = patch[:, :half], patch[:, half:]
    own_rows, other_rows = chosen(first, low_half, high_half), chosen(first, high_half, low_half)
    for b in range(IMGS):
        own_half[b] = transposed(own_rows[b * length : (b + 1) * length])
        other_half[b, :half] = transposed(other_rows[b * length : (b + 1) * length]).astype(BF16)
        other_half[b, half:] = jnp.zeros((16, length), BF16)
    other_half[0, half:, :half] = class_other[...]

    dq_sum = col_sum(join_ref[:, :width].astype(F32))
    dv_sum = col_sum(join_ref[:, 2 * width :].astype(F32))
    late = jnp.concatenate(
        [col_sum(dh * normal), col_sum(dh), dq_sum, dv_sum, pb_grad, jnp.zeros((11, width), F32)], axis=0
    )
    vec0 = vec_in[...] + late
    lane = lax.broadcasted_iota(jnp.int32, (width, 128), 1)
    feature = lax.broadcasted_iota(jnp.int32, (width, 128), 0)
    groups = jnp.where((feature >= lane * size) & (feature < lane * size + size), 1.0, 0.0)
    small = lax.dot_general(
        sum0[...] + sum1[...], groups, (((1,), (0,)), ((), ())),
        preferred_element_type=F32, precision=lax.Precision.HIGHEST,
    )
    tall_ref[...] = jnp.concatenate(
        [vec0[:, k * 128 : (k + 1) * 128] for k in range(3)]
        + [vec_in1[:, k * 128 : (k + 1) * 128] for k in range(3)]
        + [small, jnp.zeros((8, 128), F32)],
        axis=0,
    )
    filler = jnp.zeros((12, 128), F32)
    for n in range(32):
        blocks[n, 144:160] = jnp.concatenate([tall_ref[n * 4 : n * 4 + 4], filler], axis=0).astype(BF16)
    block_copy(blocks, kept_ref, 0, 16)
    block_copy(blocks, send_ref, 16, 16)


def assemble(own_half, half_got, class_own, patch_out, class_out, class_grad):
    first = lax.axis_index("pipe") == 0
    half, count = patch_out.shape[1:]
    for b in range(IMGS):
        mine, theirs = own_half[b, :, :count], half_got[b, :half, :count].astype(F32)
        patch_out[b] = chosen(first, mine, theirs)
        patch_out[IMGS + b] = chosen(first, theirs, mine)
    mine, theirs = class_own[...].astype(F32), half_got[0, half:, :half].astype(F32)
    for at, out in ((0, class_out), (8, class_grad)):
        pair = mine[at : at + IMGS], theirs[at : at + IMGS]
        rows = jnp.concatenate([chosen(first, *pair), chosen(first, *pair[::-1])], axis=0)
        out[...] = rows.astype(BF16)


def place_blocks(start, pieces, outs, held, sems):
    qkv_out, proj_out, fc1_out, fc2_out = outs
    for half in range(2):
        for n in range(8):
            block = position_block(half * 16 + start + n)
            slot = (half * 8 + n) * 3
            for at in range(3):
                source = pieces[0 if at < 2 else 1][half]
                for k in range(3):
                    rows = slice(k * 48 + (144 if at == 1 else 0), (k + 1) * 48 + (144 if at == 1 else 0))
                    held[slot + at, :, k * 128 : (k + 1) * 128] = source[n, rows].astype(F32)
            down = pl.ds(pl.multiple_of((block >> 2) * 48, 48), 48)
            along = pl.ds(pl.multiple_of((block & 3) * 384, 384), 384)
            rows = pl.ds(pl.multiple_of(block * 48, 48), 48)
            pltpu.make_async_copy(held.at[slot], fc1_out.at[down, along], sems.at[slot]).start()
            pltpu.make_async_copy(held.at[slot + 1], fc2_out.at[rows], sems.at[slot + 1]).start()
            last = (block & 3) == 3

            @pl.when(last)
            def _():
                pltpu.make_async_copy(held.at[slot + 2], proj_out.at[down], sems.at[slot + 2]).start()

            @pl.when(jnp.logical_not(last))
            def _():
                pltpu.make_async_copy(held.at[slot + 2], qkv_out.at[down, along], sems.at[slot + 2]).start()


def wait_blocks(outs, held, sems):
    for slot in range(48):
        pltpu.make_async_copy(held.at[slot], outs[3].at[pl.ds(0, 48)], sems.at[slot]).wait()


def first_outputs(*refs):
    pieces, outs, (held, sems) = refs[:4], refs[8:12], refs[12:]

    @pl.when(lax.axis_index("pipe") == 0)
    def _():
        place_blocks(0, (pieces[0:2], pieces[2:4]), outs, held, sems)
        wait_blocks(outs, held, sems)


def last_outputs(*refs):
    pieces, lows, outs, vec_outs = refs[:4], refs[4:6], refs[10:14], refs[14:24]
    pre_out, post_out, bias_out, held, vec_held, tall_ref, sems = refs[24:]
    first = lax.axis_index("pipe") == 0
    width = outs[1].shape[0]

    @pl.when(first)
    def _():
        place_blocks(8, (pieces[0:2], pieces[2:4]), outs, held, sems)

    for half in range(2):
        vec_held[half * 16 : half * 16 + 8] = lows[half][:, 144:160].astype(F32)
        vec_held[half * 16 + 8 : half * 16 + 16] = pieces[2 + half][:, 144:160].astype(F32)
    for block in range(32):
        tall_ref[block * 4 : block * 4 + 4] = vec_held[block_position(block)][0:4]
    rows = [
        chosen(first, tall_ref[k * 16 : (k + 1) * 16], tall_ref[48 + k * 16 : 48 + (k + 1) * 16]) for k in range(3)
    ]
    rows = jnp.concatenate(rows, axis=1)
    at = 0
    for out in vec_outs:
        for k in range(out.shape[1] // width):
            out[:, k * width : (k + 1) * width] = rows[at : at + 1]
            at += 1
    pre_out[...] = tall_ref[96:104, 0:HEADS]
    post_out[...] = tall_ref[104:112].T[0:HEADS]
    bias_out[...] = tall_ref[112:113, 0:HEADS]

    @pl.when(first)
    def _():
        wait_blocks(outs, held, sems)


def class_gradients(*refs):
    factor_refs = refs[:-19]
    w_in, p_in, f1_in, f2_in, vec, *outs = refs[-19:-10]
    w, p, f1, f2, factors, *held, sems = refs[-10:]
    width = p.shape[0]

    @pl.when(lax.axis_index("pipe") != 0)
    def _():
        copies = [
            pltpu.make_async_copy(source, target, sems.at[n])
            for n, (source, target) in enumerate(((f1_in, f1), (f2_in, f2), (w_in, w), (p_in, p)))
        ]
        for copy in copies:
            copy.start()
        join_factors(factor_refs, factors)
        group = min(32, factors.shape[0])
        rows = group * IMGS * HEADS
        mask = head_mask(rows, width)
        spread = (
            lax.broadcasted_iota(jnp.int32, (rows, group * IMGS), 0) >> 3
            == lax.broadcasted_iota(jnp.int32, (rows, group * IMGS), 1)
        )
        spread = jnp.where(spread, 1.0, 0.0).astype(BF16)
        bias = jnp.concatenate([vec[8 + k : 9 + k].astype(F32) for k in range(4)], axis=1)
        for copy in copies:
            copy.wait()

        def expanded(vectors):
            return jnp.where(mask, mm(spread, vectors), 0.0).astype(BF16)

        def put(n, at, target, cut, piece):
            target[:, cut] = piece if n == 0 else target[:, cut] + piece
            if n == factors.shape[0] // group - 1:
                done.append(pltpu.make_async_copy(target.at[:, cut], outs[at].at[:, cut], sems.at[4 + len(done)]))
                done[-1].start()

        done = []
        whole = slice(0, width)
        for n in range(factors.shape[0] // group):
            part = slice(n * group, (n + 1) * group)
            wh, g, vectors = (factor_rows(factors, part, start, group) for start in (0, 16, 32))
            hidden_c, att1, bg1, inner1, og1 = (picked(vectors, kind, group) for kind in range(5))
            active, slope = gelu_pair(mm(inner1, f1[...]) + bias)
            ig1 = (mm_nt(og1, f2[...]) * slope).astype(BF16)
            put(n, 3, held[3], whole, mm_tn(active.astype(BF16), og1))
            put(n, 2, held[2], slice(0, f1.shape[1]), mm_tn(inner1, ig1))
            query = (mm(hidden_c, w[:, :width]) + vec[2:3].astype(F32)).astype(BF16)
            da1 = mm_nt(bg1, p[...]).astype(BF16)
            chosen_g = jnp.where(mask, mm(g, w[:, width : 2 * width]), 0.0).astype(BF16)
            dq1 = mm_tn(spread, chosen_g).astype(BF16)
            put(n, 1, held[1], whole, mm_tn(att1, bg1))
            parts = (mm_tn(hidden_c, dq1), mm_tn(g, expanded(query)), mm_tn(wh, expanded(da1)))
            for k, piece in enumerate(parts):
                put(n, 0, held[0], slice(k * width, (k + 1) * width), piece)
        for copy in done:
            copy.wait()


def join_factors(pieces, factors):
    at = 0
    for piece in pieces:
        factors[at : at + piece.shape[0]] = piece[...]
        at += piece.shape[0]


def factor_rows(factors, part, start, group):
    pieces = [factors[part, k * 48 + start : k * 48 + start + 16].reshape(group * 16, 128) for k in range(3)]
    return jnp.concatenate(pieces, axis=1)


def picked(vectors, kind, group):
    rows, cols = group * IMGS, group * 16
    row = lax.broadcasted_iota(jnp.int32, (rows, cols), 0)
    col = lax.broadcasted_iota(jnp.int32, (rows, cols), 1)
    wanted = (row >> 1) * 16 + kind * IMGS + (row & 1)
    return mm(jnp.where(col == wanted, 1.0, 0.0).astype(BF16), vectors).astype(BF16)


VM = pl.BlockSpec(memory_space=pltpu.VMEM)
SM = pl.BlockSpec(memory_space=pltpu.SMEM)
HB = pl.BlockSpec(memory_space=pltpu.HBM)


def call(body, ins, outs, scratch, name, limit, sems=0, far=0, aliases=None):
    return pl.pallas_call(
        body,
        out_shape=[jax.ShapeDtypeStruct(shape, kind) for shape, kind in outs],
        in_specs=[spec for spec, _ in ins],
        out_specs=[HB] * far + [VM] * (len(outs) - far),
        scratch_shapes=[pltpu.VMEM(shape, kind) for shape, kind in scratch]
        + ([pltpu.SemaphoreType.DMA((sems,))] if sems else []),
        compiler_params=pltpu.CompilerParams(vmem_limit_bytes=limit * 1024 * 1024),
        cost_estimate=pl.CostEstimate(flops=0, bytes_accessed=1, transcendentals=0),
        input_output_aliases=aliases or {},
        name=name,
    )(*[value for _, value in ins])


def swapped(array):
    return lax.ppermute(array, "pipe", [(0, 1), (1, 0)])


def exchanged(array, bits, cores=(0, 1)):
    dp = lax.axis_size("dp")
    pairs = [(core * dp + i, core * dp + (i ^ bits[core])) for core in cores for i in range(dp)]
    return lax.ppermute(array, ("pipe", "dp"), pairs)


def total(pieces, start, stop):
    parts = [piece[start:stop].astype(F32) for piece in pieces]
    return sum(parts[1:], parts[0]).astype(BF16)


def after(arrays, *others):
    return lax.optimization_barrier((arrays, others))[0]


NEAR, FAR = (4, 4), (8, 8)
LONG = (("halve", (1, 2)), ("halve", (2, 1)), ("halve", NEAR), ("swap", FAR), ("collect", NEAR), ("collect", (2, 1)), ("collect", (1, 2)))
SHORT = (("halve", (1, 2)), ("halve", (2, 1)), ("swap", NEAR), ("swap", FAR), ("collect", (2, 1)), ("collect", (1, 2)))


GATHER = (("gather", FAR), ("gather", NEAR), ("gather", (2, 1)), ("gather", (1, 2)))


class Stream:
    def __init__(self, pieces, steps):
        self.pieces, self.steps, self.at = list(pieces), steps, 0
        self.whole = lax.axis_size("dp") == 16
        self.leaving = self.pieces[0]

    def wait(self, *others):
        self.pieces = list(after(tuple(self.pieces), *others))

    def step(self):
        if not self.whole:
            return
        kind, bits = self.steps[self.at]
        self.at += 1
        count = min(piece.shape[0] for piece in self.pieces)
        if kind == "halve":
            self.leaving = total(self.pieces, count // 2, count)
            self.pieces = [piece[: count // 2] for piece in self.pieces] + [exchanged(self.leaving, bits)]
        elif kind == "swap":
            run = 1 if bits == FAR else 2
            mid = total(self.pieces, 0, count)
            self.leaving = jnp.concatenate([total(self.pieces, at ^ run, (at ^ run) + run) for at in range(0, count, run)])
            got = exchanged(self.leaving, bits)
            self.pieces = [mid, got]
            if self.steps[self.at][0] == "collect":
                self.pieces = [total([mid, got[:count]], 0, count)]
        else:
            self.leaving = jnp.concatenate(self.pieces, axis=0) if len(self.pieces) > 1 else self.pieces[0]
            self.pieces = [self.leaving, exchanged(self.leaving, bits, (1,) if kind == "gather" else (0, 1))]

    def halves(self):
        if self.whole:
            return self.pieces
        whole = lax.psum(total(self.pieces, 0, 16).astype(F32), "dp").astype(BF16)
        return whole[:8], whole[8:]


def local(
    patches, class_token, keep_mask, class_cotangent, norm1_gain, norm1_bias, qkv_weight, qv_bias,
    mix_pre, mix_post, post_bias, proj_weight, proj_bias, scale_attn, norm2_gain, norm2_bias,
    fc1_weight, fc1_bias, fc2_weight, fc2_bias, scale_mlp,
):
    dp = lax.axis_size("dp")
    images, count, width = patches.shape
    hidden_width = fc1_weight.shape[2]
    length, lanes = 208, 256
    half = width // 2
    flat = IMGS * length

    w_own, p_own, f1_own, f2_own = qkv_weight[0], proj_weight[0], fc1_weight[0], fc2_weight[0]
    w_got = swapped(w_own)
    small = (
        norm1_gain, norm1_bias, qv_bias, proj_bias, scale_attn, norm2_gain, norm2_bias, fc1_bias, fc2_bias, scale_mlp,
        mix_pre, mix_post, post_bias[None],
    )
    vec_own, pre_rows, post_rows, bias_row = call(
        prepare,
        [(HB, array) for array in small],
        [((16, width), BF16), ((HEADS, width), F32), ((HEADS, width), F32), ((1, width), F32)],
        [(array.shape, BF16) for array in small],
        "prepare",
        LIMIT_P,
        sems=13,
    )
    vec_got = swapped(vec_own)
    mixing = jnp.stack([mix_pre, mix_post]).astype(F32)
    rows = jnp.pad(patches, ((0, 0), (0, length - count), (0, 0)))
    p_late, f1_late, f2_late = after((p_own, f1_own, f2_own), w_got, vec_got, rows)
    p_got, f1_got, f2_got = swapped(p_late), swapped(f1_late), swapped(f2_late)

    token_shape = (IMGS, length, width)
    wide_shape = (IMGS, lanes, width)
    keep_scratch = ((8, lanes), F32)
    att, hid, queries, keys, values, probs = call(
        attention_forward,
        [(SM, mixing), (VM, rows), (VM, keep_mask), (VM, vec_own), (VM, vec_got), (HB, w_own), (HB, w_got),
         (VM, bias_row)],
        [(token_shape, BF16), (token_shape, BF16), (wide_shape, BF16), (wide_shape, BF16), (wide_shape, BF16),
         ((IMGS, HEADS * lanes, lanes), BF16)],
        [((width, 3 * width), BF16), ((width, HEADS * lanes), BF16), keep_scratch],
        "attention_forward",
        LIMIT_A,
        sems=1,
    )
    vec_shape = (16, width)
    send1, kept1, mg, vec0, vec1, class_own, class_other, factors = call(
        middle_kernel,
        [(VM, att), (VM, rows), (VM, keep_mask), (VM, class_token), (VM, class_cotangent), (VM, vec_own),
         (VM, vec_got), (HB, p_own), (HB, p_got), (HB, f1_own), (HB, f1_got), (HB, f2_own), (HB, f2_got), (HB, w_own),
         (HB, w_got)],
        [((17, 288, 128), BF16), ((16, 288, 128), BF16), (token_shape, F32), (vec_shape, F32), (vec_shape, F32),
         ((16, half), BF16), ((16, half), BF16), ((144, 128), BF16)],
        [((width, width), BF16), ((width, hidden_width), BF16), ((hidden_width, width), BF16),
         ((width, width), BF16), ((width, hidden_width), BF16), ((hidden_width, width), BF16),
         ((width, 3 * width), BF16), ((flat, hidden_width), BF16), ((flat, hidden_width), BF16),
         ((32, 288, 128), BF16), keep_scratch],
        "middle_kernel",
        LIMIT_B,
        sems=7,
    )

    def image_backward(b, mg):
        return call(
            lambda *refs: attention_backward(b, *refs),
            [(SM, mixing), (VM, mg), (VM, keep_mask), (VM, queries), (VM, keys), (VM, values), (VM, probs),
             (VM, vec_own), (VM, vec_got), (HB, p_own), (HB, p_got), (VM, bias_row), (VM, pre_rows), (VM, post_rows)],
            [((length, 3 * width), BF16), ((24, width), F32)],
            [((width, width), BF16), ((HEADS * lanes, lanes), BF16), ((width, HEADS * lanes), BF16),
             ((lanes, width), BF16), keep_scratch],
            f"attention_backward_{b}",
            LIMIT_C,
            sems=1,
        )

    got1 = swapped(send1)
    factors_got = got1[16, :144]
    stream1, shared = Stream((kept1, got1), LONG), Stream((factors[None], factors_got[None]), GATHER)
    join0, sum0 = image_backward(0, mg)
    stream1.wait(join0)
    stream1.step()
    join1, sum1 = image_backward(1, after(mg, stream1.leaving))
    mg = after(mg, join1)
    send2, kept2, own_half, other_half = call(
        input_gradients,
        [(VM, mg), (VM, rows), (VM, hid), (VM, att), (VM, join0), (VM, join1), (VM, sum0), (VM, sum1), (VM, vec0),
         (VM, vec1), (VM, vec_own), (VM, vec_got), (HB, w_own), (HB, w_got), (VM, class_other)],
        [((16, 160, 128), BF16), ((16, 160, 128), BF16), ((IMGS, half, length), F32), ((IMGS, half + 16, length), BF16)],
        [((width, 3 * width), BF16), ((flat, 3 * width), BF16), ((32, 160, 128), BF16), ((128, 128), F32)],
        "input_gradients",
        LIMIT_C,
        sems=1,
    )
    got2, half_got = swapped(send2), swapped(other_half)
    stream2 = Stream((kept2, got2), SHORT)
    patch_out, class_result, class_grad = call(
        assemble,
        [(VM, own_half), (VM, half_got), (VM, class_own)],
        [((2 * IMGS, half, count), F32), ((2 * IMGS, half), BF16), ((2 * IMGS, half), BF16)],
        [],
        "assemble",
        LIMIT_C,
    )

    def turn(*streams):
        for stream in streams:
            turn.last = stream.wait(*turn.last) or (stream.step(), stream.leaving)[1:]

    turn.last = (kept2,)
    turn(stream1, stream2)
    turn.last += (half_got,)
    turn(shared, stream1, stream2, shared, stream1, stream2, shared, shared, stream1, stream2, stream1)
    turn.last += tuple(shared.pieces)
    turn(stream2)
    turn.last += (patch_out, class_result, class_grad)
    turn(stream1, stream2)
    if dp == 16:
        factor_parts = after(tuple(shared.pieces), stream2.leaving)
    else:
        factor_parts = tuple(lax.all_gather(part, "dp") for part in (factors, factors_got))
    matrices = [((width, 3 * width), F32), ((width, width), F32), ((width, hidden_width), F32), ((hidden_width, width), F32)]
    outs = call(
        class_gradients,
        [(VM, part) for part in factor_parts]
        + [(HB, w_own), (HB, p_own), (HB, f1_own), (HB, f2_own), (VM, vec_own)],
        matrices,
        [(shape, BF16) for shape, _ in matrices] + [((2 * dp, 144, 128), BF16)] + matrices,
        "class_gradients",
        LIMIT_E,
        sems=10,
        far=4,
    )
    (low1, high1), (low2, high2) = stream1.halves(), stream2.halves()
    low1_other, low2_other = swapped(low1), swapped(low2)
    held_blocks = ((48, 48, width), F32)
    outs = call(
        first_outputs,
        [(VM, low1), (VM, low1_other), (VM, low2), (VM, low2_other)] + [(HB, out) for out in outs],
        matrices,
        [held_blocks],
        "first_outputs",
        LIMIT_D,
        sems=48,
        far=4,
        aliases={4 + n: n for n in range(4)},
    )
    high1, high2 = after((high1, high2), outs[0])
    high1_other, high2_other = swapped(high1), swapped(high2)
    qkv_out, proj_out, fc1_out, fc2_out, *small_outs = call(
        last_outputs,
        [(VM, high1), (VM, high1_other), (VM, high2), (VM, high2_other), (VM, low2), (VM, low2_other)]
        + [(HB, out) for out in outs],
        matrices
        + [((1, size * width), F32) for size in (1, 1, 2, 1, 1, 1, 1, 4, 1, 1)]
        + [((HEADS, HEADS), F32), ((HEADS, HEADS), F32), ((1, HEADS), F32)],
        [held_blocks, ((32, 16, 128), F32), ((128, 128), F32)],
        "last_outputs",
        LIMIT_D,
        sems=48,
        far=4,
        aliases={6 + n: n for n in range(4)},
    )
    n1g, n1b, qvb, pb, sa, n2g, n2b, f1b, f2b, sm, pre, post, bias = small_outs
    return (
        class_result, patch_out.transpose(0, 2, 1), class_grad, n1g, n1b, qkv_out[None], qvb, proj_out[None], pb, sa, n2g, n2b,
        fc1_out[None], f1b, fc2_out[None], f2b, sm, pre, post, bias[0],
    )


def solution(mesh):
    stacked = (P("pipe", None), P("pipe", None), P("pipe", None, None))
    row, _, cube = stacked
    return jax.shard_map(
        local,
        mesh=mesh,
        in_specs=(
            P("dp", None, None), P("dp", None), P("dp", None), P("dp", None),
            row, row, cube, row, P(), P(), P(), cube, row, row, row, row, cube, row, cube, row, row,
        ),
        out_specs=(
            P("dp", "pipe"), P("dp", None, "pipe"), P("dp", "pipe"),
            row, row, cube, row, cube, row, row, row, row, cube, row, cube, row, row, P(), P(), P(),
        ),
        check_vma=False,
    )
```

```python
import jax
import jax.numpy as jnp
from jax import lax
from jax.experimental import pallas as pl
from jax.experimental.pallas import tpu as pltpu
from jax.sharding import PartitionSpec as P

HEADS = 8
IMGS = 2
LIMIT_P, LIMIT_A, LIMIT_B, LIMIT_C, LIMIT_D, LIMIT_E = 60, 24, 24, 24, 24, 24
LOG2E = 1.4426950408889634
F32 = jnp.float32
BF16 = jnp.bfloat16


def mm(left, right):
    return lax.dot_general(left, right, (((1,), (0,)), ((), ())), preferred_element_type=F32)


def mm_nt(left, right):
    return lax.dot_general(left, right, (((1,), (1,)), ((), ())), preferred_element_type=F32)


def mm_tn(left, right):
    return lax.dot_general(left, right, (((0,), (0,)), ((), ())), preferred_element_type=F32)


def normed(rows):
    centred = rows - jnp.mean(rows, -1, keepdims=True)
    scale = lax.rsqrt(jnp.mean(centred * centred, -1, keepdims=True) + 1e-06)
    return centred * scale, scale


def norm_back(normal, scale, grad):
    inner = jnp.mean(grad * normal, -1, keepdims=True)
    return (grad - jnp.mean(grad, -1, keepdims=True) - normal * inner) * scale


def col_sum(rows):
    return jnp.sum(rows, axis=0, keepdims=True)


def gelu_pair(rows):
    phi = 0.5 + 0.5 * lax.erf(rows * 0.7071067811865476)
    return rows * phi, phi + rows * (jnp.exp2(rows * rows * (-0.5 * LOG2E)) * 0.3989422804014327)


def head_mask(rows, width):
    lane = lax.broadcasted_iota(jnp.int32, (rows, width), 1)
    head = lax.rem(lax.broadcasted_iota(jnp.int32, (rows, width), 0), HEADS)
    size = width // HEADS
    return (lane >= head * size) & (lane < head * size + size)


def chosen(is_first, first, other):
    return jnp.where(is_first, first, other)


def scaled_rows(rows, factors):
    size = rows.shape[0] // HEADS
    parts = []
    for head, factor in enumerate(factors):
        part = rows[head * size : (head + 1) * size]
        parts.append(part * jnp.full((1, rows.shape[1]), factor, F32).astype(BF16))
    return jnp.concatenate(parts, axis=0)


def transposed(rows):
    return rows.T


def own_place():
    core = lax.axis_index("pipe")
    return core, core * 16 + (lax.axis_index("dp") if lax.axis_size("dp") == 16 else 0)


def fetch(first, own, got, target, sem):
    @pl.when(first)
    def _():
        pltpu.make_async_copy(own, target, sem).start()

    @pl.when(jnp.logical_not(first))
    def _():
        pltpu.make_async_copy(got, target, sem).start()

    return pltpu.make_async_copy(own, target, sem)


def own_images(first, rows):
    return chosen(first, rows[0:IMGS], rows[IMGS : 2 * IMGS])


def token_rows(rows_ref):
    rows = rows_ref[pl.ds(lax.axis_index("pipe") * IMGS, IMGS)]
    return rows.reshape(-1, rows.shape[2])


def keep_columns(first, mask_ref, scratch):
    scratch[...] = jnp.zeros_like(scratch)
    scratch[0:IMGS, 0 : mask_ref.shape[1]] = own_images(first, mask_ref[...].astype(F32))
    return scratch[...].T


def prepare(*refs):
    sources, (vec_ref, pre_ref, post_ref, bias_ref), held, sems = refs[:13], refs[13:17], refs[17:30], refs[30]
    copies = [pltpu.make_async_copy(*pair, sems.at[n]) for n, pair in enumerate(zip(sources, held))]
    for copy in copies:
        copy.start()
    for copy in copies:
        copy.wait()
    n1g, n1b, qvb, pb, sa, n2g, n2b, f1b, f2b, sm, pre, post, post_bias = held
    width = n1g.shape[1]
    rows = [n1g[...], n1b[...], qvb[:, :width], qvb[:, width:], pb[...], sa[...], n2g[...], n2b[...]]
    rows += [f1b[:, k * width : (k + 1) * width] for k in range(4)] + [f2b[...], sm[...]]
    rows = [row.astype(F32) for row in rows] + [jnp.zeros((2, width), F32)]
    vec_ref[...] = jnp.concatenate(rows, axis=0).astype(BF16)
    spread = jnp.where(head_mask(HEADS, width), 1.0, 0.0).astype(BF16)
    pre_ref[...] = mm(pre[...], spread)
    post_ref[...] = mm_tn(post[...], spread)
    bias_ref[...] = mm(post_bias[...], spread)


def attention_forward(
    mixing, rows_ref, mask_ref, vec_own, vec_got, w_own, w_got, bias_ref,
    att_ref, hid_ref, q_ref, k_ref, v_ref, pt_ref, w_ref, vs_ref, keep_ref, sems,
):
    first = lax.axis_index("pipe") == 0
    weights_copy = fetch(first, w_own, w_got, w_ref, sems.at[0])
    width = rows_ref.shape[2]
    length = rows_ref.shape[1]
    lanes = q_ref.shape[1]
    size = width // HEADS
    keeps = keep_columns(first, mask_ref, keep_ref)

    vec = chosen(first, vec_own[...].astype(F32), vec_got[...].astype(F32))
    scale = size ** (-0.5) * LOG2E
    pad_rows = jnp.zeros((lanes - length, width), BF16)
    same = lax.broadcasted_iota(jnp.int32, (length, lanes), 0) == lax.broadcasted_iota(jnp.int32, (length, lanes), 1)

    for b in range(IMGS):
        normal, _ = normed(rows_ref[lax.axis_index("pipe") * IMGS + b].astype(F32))
        hidden = (normal * vec[0:1] + vec[1:2]).astype(BF16)
        hid_ref[b] = hidden
        if b == 0:
            weights_copy.wait()
        joined = mm(hidden, w_ref[...])
        queries = joined[:, :width] + vec[2:3]
        keys = joined[:, width : 2 * width]
        values = joined[:, 2 * width :] + vec[3:4]
        low_k = keys.astype(BF16)
        low_v = values.astype(BF16)
        q_ref[b, :length] = queries.astype(BF16)
        k_ref[b, :length] = low_k
        v_ref[b, :length] = low_v
        q_ref[b, length:] = pad_rows
        k_ref[b, length:] = pad_rows
        v_ref[b, length:] = pad_rows
        q_t = transposed(q_ref[b])
        v_t = transposed(v_ref[b])
        keep = keeps[:length, b : b + 1]
        allowed = (keep > 0.0) | same
        for h in range(HEADS):
            scaled_q = scaled_rows(q_t, [mixing[0, h, c] for c in range(HEADS)])
            scores = jnp.where(allowed, mm(low_k, scaled_q) * scale, -1e30)
            top = jnp.max(scores, axis=0, keepdims=True)
            weights = jnp.exp2(scores - top)
            weights = weights * (1.0 / jnp.sum(weights, axis=0, keepdims=True))
            pt_ref[b, h * lanes : h * lanes + length] = weights.astype(BF16)
            pt_ref[b, h * lanes + length : (h + 1) * lanes] = jnp.zeros((lanes - length, lanes), BF16)
            vs_ref[:, h * lanes : (h + 1) * lanes] = scaled_rows(v_t, [mixing[1, c, h] for c in range(HEADS)])
        mixed = transposed(mm(vs_ref[...], pt_ref[b]))[:length]
        low_f = low_v.astype(F32)
        extra = bias_ref[...] * (col_sum(low_f * keep) + (1.0 - keep) * low_f)
        att_ref[b] = (mixed + extra).astype(BF16)


def block_copy(source, target, start, count):
    for n in range(count):
        target[n] = source[position_block(start + n)]


def position_block(at):
    core, me = own_place()
    first_bit, second_bit = (at >> 3) & 1, (at >> 2) & 1
    rest = ((at >> 4) << 4) | ((at & 1) << 3) | (((at >> 1) & 1) << 2)
    x_first = rest | first_bit | (second_bit << 1)
    y_first = rest | second_bit | (first_bit << 1)
    return jnp.where(core == (at >> 4), x_first, y_first) ^ me


def block_position(block):
    core, me = own_place()
    apart = block ^ me
    x_bit, y_bit = apart & 1, (apart >> 1) & 1
    half = apart >> 4
    top = jnp.where(core == half, (x_bit << 3) | (y_bit << 2), (y_bit << 3) | (x_bit << 2))
    return (half << 4) | top | (((apart >> 2) & 1) << 1) | ((apart >> 3) & 1)


def put_blocks(target, rows, start, wide):
    tall, across = 48, 384
    for rb in range(rows.shape[0] // tall):
        for cb in range(rows.shape[1] // across):
            block = rb * wide[0] + wide[1] + cb
            for k in range(3):
                piece = rows[rb * tall : (rb + 1) * tall, cb * across + k * 128 : cb * across + (k + 1) * 128]
                target[block, start + k * tall : start + (k + 1) * tall] = piece.astype(BF16)


def middle_kernel(
    att_ref, rows_ref, mask_ref, class_ref, cot_ref,
    vec_own, vec_got, p_own, p_got, f1_own, f1_got, f2_own, f2_got, w_own, w_got,
    send_ref, kept_ref, mg_ref, vec_out, vec_out1, class_own, class_other, factor_ref,
    p0_ref, f10, f20, p1_ref, f11, f21, w1_ref, act_ref, gp_ref, blocks, keep_ref, sems,
):
    first = lax.axis_index("pipe") == 0
    p0_copy = fetch(first, p_own, p_got, p0_ref, sems.at[0])
    w1_copy = fetch(first, w_got, w_own, w1_ref, sems.at[3])
    f10_copy = fetch(first, f1_own, f1_got, f10, sems.at[1])
    f20_copy = fetch(first, f2_own, f2_got, f20, sems.at[2])
    p1_copy = fetch(first, p_got, p_own, p1_ref, sems.at[4])
    f11_copy = fetch(first, f1_got, f1_own, f11, sems.at[5])
    f21_copy = fetch(first, f2_got, f2_own, f21, sems.at[6])
    length, width = rows_ref.shape[1], rows_ref.shape[2]
    flat = IMGS * length
    size = width // HEADS
    patches = mask_ref.shape[1]
    keep_ref[...] = jnp.zeros_like(keep_ref)
    keep_ref[0:IMGS, 0:patches] = own_images(first, mask_ref[...].astype(F32))
    keep_rows = keep_ref[0:IMGS, :length]
    keep_lane = lax.broadcasted_iota(jnp.int32, (IMGS, length), 1)
    keep_rows = jnp.where(keep_lane == patches, 1.0, keep_rows)

    own, got = vec_own[...].astype(F32), vec_got[...].astype(F32)
    vec, vec1 = chosen(first, own, got), chosen(first, got, own)

    def wide_bias(v):
        return jnp.concatenate([v[8 + k : 9 + k] for k in range(4)], axis=1)

    blank = jnp.zeros((8 - IMGS, width), F32)
    class_rows = jnp.concatenate([own_images(first, class_ref[...].astype(F32)), blank], axis=0)
    w1_copy.wait()
    normal_c, _ = normed(class_rows)
    hidden_c = (normal_c * vec1[0:1] + vec1[1:2]).astype(BF16)
    query = (mm(hidden_c, w1_ref[:, :width]) + vec1[2:3]).astype(BF16).astype(F32)
    mask = head_mask(IMGS * HEADS, width)

    def spread(rows):
        both = jnp.concatenate(
            [jnp.broadcast_to(rows[b : b + 1], (HEADS, width)) for b in range(IMGS)], axis=0
        )
        return jnp.where(mask, both, 0.0)

    def gathered(rows):
        kept = jnp.where(mask, rows, 0.0)
        parts = [col_sum(kept[b * HEADS : (b + 1) * HEADS]) for b in range(IMGS)]
        return jnp.concatenate(parts + [jnp.zeros((8 - IMGS, width), F32)], axis=0)

    query_rows = mm_nt(spread(query).astype(BF16), w1_ref[:, width : 2 * width]).astype(BF16)

    p0_copy.wait()
    branch = mm(att_ref[...].reshape(flat, width), p0_ref[...]) + vec[4:5]
    middle = token_rows(rows_ref).astype(F32) + vec[5:6] * branch
    normal, norm_scale = normed(middle)
    inner_low = (normal * vec[6:7] + vec[7:8]).astype(BF16)
    f10_copy.wait()
    bias = wide_bias(vec)
    step = f10.shape[1] // 2
    for k in range(2):
        cut = slice(k * step, (k + 1) * step)
        inner = mm(inner_low, f10[:, cut]) + bias[:, cut]
        active, slope = gelu_pair(inner)
        act_ref[:, cut] = active.astype(BF16)
        gp_ref[:, cut] = slope.astype(BF16)
    f20_copy.wait()
    outer = mm(act_ref[...], f20[...]) + vec[12:13]
    sent = (middle + vec[13:14] * outer).astype(BF16).astype(F32)

    upper1 = jnp.concatenate([own_images(first, cot_ref[...].astype(F32)), blank], axis=0)
    og1 = (upper1 * vec1[13:14]).astype(BF16)
    f21_copy.wait()
    dact1 = mm_nt(og1, f21[...])
    at_row = lax.broadcasted_iota(jnp.int32, (length, width), 0)
    hiddens, normals, scales, probs, low_probs, sums, whs = [], [], [], [], [], [], []
    for b in range(IMGS):
        tokens = jnp.where(at_row == patches, class_rows[b : b + 1], sent[b * length : (b + 1) * length])
        n1, s1 = normed(tokens)
        h1 = (n1 * vec1[0:1] + vec1[1:2]).astype(BF16)
        scores = mm_nt(query_rows[b * HEADS : (b + 1) * HEADS], h1) * (size ** (-0.5) * LOG2E)
        scores = jnp.where(keep_rows[b : b + 1] > 0.0, scores, -1e30)
        weights = jnp.exp2(scores - jnp.max(scores, axis=-1, keepdims=True))
        weights = weights / jnp.sum(weights, axis=-1, keepdims=True)
        low = weights.astype(BF16)
        hiddens.append(h1)
        normals.append(n1)
        scales.append(s1)
        probs.append(weights)
        low_probs.append(low)
        sums.append(jnp.sum(low.astype(F32), axis=-1, keepdims=True))
        whs.append(mm(low, h1))
    wh = jnp.concatenate(whs, axis=0).astype(BF16)
    prob_sum = gathered(jnp.broadcast_to(jnp.concatenate(sums, axis=0), (IMGS * HEADS, width)))
    att1 = (gathered(mm(wh, w1_ref[:, 2 * width :])) + vec1[3:4] * prob_sum).astype(BF16)
    p1_copy.wait()
    branch1 = mm(att1, p1_ref[...]) + vec1[4:5]
    middle1 = class_rows + vec1[5:6] * branch1
    normal2, scale2 = normed(middle1)
    inner1 = (normal2 * vec1[6:7] + vec1[7:8]).astype(BF16)
    f11_copy.wait()
    active1, slope1 = gelu_pair(mm(inner1, f11[...]) + wide_bias(vec1))
    outer1 = mm(active1.astype(BF16), f21[...]) + vec1[12:13]
    class_result = middle1 + vec1[13:14] * outer1

    ig1 = (dact1 * slope1).astype(BF16)
    dh2 = mm_nt(ig1, f11[...])
    mg1 = upper1 + norm_back(normal2, scale2, dh2 * vec1[6:7])
    bg1 = (mg1 * vec1[5:6]).astype(BF16)
    da1 = mm_nt(bg1, p1_ref[...]).astype(BF16).astype(F32)
    value_rows = mm_nt(spread(da1).astype(BF16), w1_ref[:, 2 * width :]).astype(BF16)
    low_grads, gs = [], []
    for b in range(IMGS):
        part = slice(b * HEADS, (b + 1) * HEADS)
        dw = mm_nt(value_rows[part], hiddens[b])
        ds = probs[b] * (dw - jnp.sum(probs[b] * dw, axis=-1, keepdims=True))
        low = (ds * size ** (-0.5)).astype(BF16)
        low_grads.append(low)
        gs.append(mm(low, hiddens[b]))
    g_rows = jnp.concatenate(gs, axis=0).astype(BF16)
    dq1 = gathered(mm(g_rows, w1_ref[:, width : 2 * width])).astype(BF16)
    dclass = mm_nt(dq1, w1_ref[:, :width])
    uppers, grads = [], []
    n1g, n1b = jnp.zeros((1, width), F32), jnp.zeros((1, width), F32)
    for b in range(IMGS):
        part = slice(b * HEADS, (b + 1) * HEADS)
        left = jnp.concatenate([low_grads[b], low_probs[b]], axis=0)
        right = jnp.concatenate([query_rows[part], value_rows[part]], axis=0)
        dh1 = mm_tn(left, right)
        grads.append(dh1)
        n1g = n1g + col_sum(dh1 * normals[b])
        n1b = n1b + col_sum(dh1)
        dtokens = norm_back(normals[b], scales[b], dh1 * vec1[0:1])
        uppers.append(jnp.where(at_row < patches, dtokens, 0.0).astype(BF16).astype(F32))

    def class_row(arrays):
        return jnp.concatenate([array[patches : patches + 1] for array in arrays], axis=0)

    dclass = dclass[0:IMGS]
    class_normal = class_row(normals)
    n1g = n1g + col_sum(dclass * class_normal)
    n1b = n1b + col_sum(dclass)
    class_grads = [
        mg1[0:IMGS] + norm_back(class_normal, class_row(scales), (class_row(grads) + dclass) * vec1[0:1])
    ]
    upper = jnp.concatenate(uppers, axis=0)
    class_rows = jnp.concatenate([class_result] + class_grads + [blank], axis=0)
    low_half, high_half = class_rows[:, : width // 2], class_rows[:, width // 2 :]
    class_own[...] = chosen(first, low_half, high_half).astype(BF16)
    class_other[...] = chosen(first, high_half, low_half).astype(BF16)
    ig1_sum = col_sum(ig1.astype(F32))
    vec_out1[...] = jnp.concatenate(
        [
            n1g,
            n1b,
            col_sum(dq1.astype(F32)),
            col_sum(da1 * prob_sum),
            col_sum(bg1.astype(F32)),
            col_sum(mg1 * branch1),
            col_sum(dh2 * normal2),
            col_sum(dh2),
        ]
        + [ig1_sum[:, k * width : (k + 1) * width] for k in range(4)]
        + [col_sum(og1.astype(F32)), col_sum(upper1 * outer1), jnp.zeros((2, width), F32)],
        axis=0,
    )
    pieces = [piece.astype(F32)[0:IMGS] for piece in (hidden_c, att1, bg1, inner1, og1)]
    vectors = jnp.concatenate(pieces + [jnp.zeros((16 - 5 * IMGS, width), F32)], axis=0).astype(BF16)
    for k in range(3):
        lanes = slice(k * 128, (k + 1) * 128)
        factor_ref[k * 48 : k * 48 + 16] = wh[:, lanes]
        factor_ref[k * 48 + 16 : k * 48 + 32] = g_rows[:, lanes]
        factor_ref[k * 48 + 32 : k * 48 + 48] = vectors[:, lanes]

    sm_grad = col_sum(upper * outer)
    og = (upper * vec[13:14]).astype(BF16)
    put_blocks(blocks, mm_tn(act_ref[...], og), 144, (1, 0))
    dh = jnp.zeros((flat, width), F32)
    fc1_sums = []
    step = f10.shape[1] // 1
    for k in range(1):
        cut = slice(k * step, (k + 1) * step)
        ig = (mm_nt(og, f20[cut, :]) * gp_ref[:, cut].astype(F32)).astype(BF16)
        ig_sum = col_sum(ig.astype(F32))
        fc1_sums += [ig_sum[:, at : at + width] for at in range(0, step, width)]
        put_blocks(blocks, mm_tn(inner_low, ig), 0, (4, k * step // width))
        dh = dh + mm_nt(ig, f10[:, cut])
    mg = upper + norm_back(normal, norm_scale, dh * vec[6:7])
    mg_ref[...] = mg.reshape(IMGS, length, width)
    vec_out[...] = jnp.concatenate(
        [jnp.zeros((4, width), F32), jnp.zeros((1, width), F32), col_sum(mg * branch), col_sum(dh * normal), col_sum(dh)]
        + fc1_sums
        + [col_sum(og.astype(F32)), sm_grad, jnp.zeros((2, width), F32)],
        axis=0,
    )
    block_copy(blocks, kept_ref, 0, 16)
    block_copy(blocks, send_ref, 16, 16)
    send_ref[16, 0:144] = factor_ref[...]
    send_ref[16, 144:288] = jnp.zeros((144, 128), BF16)


def attention_backward(
    b, mixing, mg_ref, mask_ref, q_ref, k_ref, v_ref, pt_ref, vec_own, vec_got, p_own, p_got, bias_ref,
    pre_rows, post_rows, join_ref, sum_ref, p_ref, dm_ref, ks_ref, da_ref, keep_ref, sems,
):
    first = lax.axis_index("pipe") == 0
    p_copy = fetch(first, p_own, p_got, p_ref, sems.at[0])
    length, width = mg_ref.shape[1], mg_ref.shape[2]
    lanes = q_ref.shape[1]
    size = width // HEADS
    root = size ** (-0.5)
    scale_row = chosen(first, vec_own[5:6].astype(F32), vec_got[5:6].astype(F32))
    bg = (mg_ref[b] * scale_row).astype(BF16)
    keep = keep_columns(first, mask_ref, keep_ref)[:length, b : b + 1]
    p_copy.wait()
    da = mm_nt(bg, p_ref[...]).astype(BF16)
    da_ref[:length] = da
    da_ref[length:] = jnp.zeros((lanes - length, width), BF16)
    da_t = transposed(da_ref[...])
    k_t = transposed(k_ref[b])
    low_v = v_ref[b, :length]
    val_f = low_v.astype(F32)
    key_f = k_ref[b, :length].astype(F32)
    da_f = da.astype(F32)
    biased = da_f * bias_ref[...]
    dv = keep * col_sum(biased) + (1.0 - keep) * biased
    bias_sum = col_sum(da_f * (col_sum(val_f * keep) + (1.0 - keep) * val_f))
    post_parts = []
    for c in range(HEADS):
        scaled = scaled_rows(da_t, [mixing[1, h, c] for h in range(HEADS)])
        dp = mm(low_v, scaled)
        weights = pt_ref[b, c * lanes : c * lanes + length]
        w_f = weights.astype(F32)
        dm = w_f * (dp - col_sum(w_f * dp))
        dm_ref[c * lanes : c * lanes + length] = dm.astype(BF16)
        dm_ref[c * lanes + length : (c + 1) * lanes] = jnp.zeros((lanes - length, lanes), BF16)
        moved = mm(weights, da_ref[...])
        dv = dv + moved * post_rows[c : c + 1]
        post_parts.append(col_sum(moved * val_f))
        ks_ref[:, c * lanes : (c + 1) * lanes] = scaled_rows(k_t, [mixing[0, c, h] for h in range(HEADS)])
    dk = jnp.zeros((length, width), F32)
    pre_parts = []
    for h in range(HEADS):
        moved = mm(dm_ref[h * lanes : h * lanes + length], q_ref[b])
        dk = dk + moved * pre_rows[h : h + 1]
        pre_parts.append(col_sum(moved * key_f))
    dq = transposed(mm(ks_ref[...], dm_ref[...]))[:length] * root
    join_ref[:, :width] = dq.astype(BF16)
    join_ref[:, width : 2 * width] = (dk * root).astype(BF16)
    join_ref[:, 2 * width :] = dv.astype(BF16)
    sum_ref[...] = jnp.concatenate(
        [part * root for part in pre_parts] + post_parts + [bias_sum, jnp.zeros((7, width), F32)], axis=0
    )


def input_gradients(
    mg_ref, rows_ref, hid_ref, att_ref, join0, join1, sum0, sum1, vec_in, vec_in1, vec_own, vec_got, w_own, w_got,
    class_other,
    send_ref, kept_ref, vec_part, own_half, other_half, w_ref, join_ref, blocks, sems,
):
    first = lax.axis_index("pipe") == 0
    w_copy = fetch(first, w_own, w_got, w_ref, sems.at[0])
    length, width = rows_ref.shape[1], rows_ref.shape[2]
    size = width // HEADS
    flat = IMGS * length
    vec = chosen(first, vec_own[...].astype(F32), vec_got[...].astype(F32))
    mg = mg_ref[...].reshape(flat, width)
    bg = (mg * vec[5:6]).astype(BF16)
    pb_grad = col_sum(bg.astype(F32))
    put_blocks(blocks, mm_tn(att_ref[...].reshape(flat, width), bg), 0, (4, 3))
    join_ref[:length] = join0[...]
    join_ref[length:] = join1[...]
    hidden = hid_ref[...].reshape(flat, width)
    put_blocks(blocks, mm_tn(hidden, join_ref[...]), 0, (4, 0))
    w_copy.wait()
    dh = mm_nt(join_ref[...], w_ref[...])
    normal, norm_scale = normed(token_rows(rows_ref).astype(F32))
    patch = mg + norm_back(normal, norm_scale, dh * vec[0:1])
    half = width // 2
    low_half, high_half = patch[:, :half], patch[:, half:]
    own_rows, other_rows = chosen(first, low_half, high_half), chosen(first, high_half, low_half)
    for b in range(IMGS):
        own_half[b] = transposed(own_rows[b * length : (b + 1) * length])
        other_half[b, :half] = transposed(other_rows[b * length : (b + 1) * length]).astype(BF16)
        other_half[b, half:] = jnp.zeros((16, length), BF16)
    other_half[0, half:, :half] = class_other[...]

    dq_sum = col_sum(join_ref[:, :width].astype(F32))
    dv_sum = col_sum(join_ref[:, 2 * width :].astype(F32))
    late = jnp.concatenate(
        [col_sum(dh * normal), col_sum(dh), dq_sum, dv_sum, pb_grad, jnp.zeros((11, width), F32)], axis=0
    )
    vec0 = vec_in[...] + late
    lane = lax.broadcasted_iota(jnp.int32, (width, 128), 1)
    feature = lax.broadcasted_iota(jnp.int32, (width, 128), 0)
    groups = jnp.where((feature >= lane * size) & (feature < lane * size + size), 1.0, 0.0)
    small = lax.dot_general(
        sum0[...] + sum1[...], groups, (((1,), (0,)), ((), ())),
        preferred_element_type=F32, precision=lax.Precision.HIGHEST,
    )
    tall = jnp.concatenate(
        [vec0[:, k * 128 : (k + 1) * 128] for k in range(3)]
        + [vec_in1[:, k * 128 : (k + 1) * 128] for k in range(3)]
        + [small, jnp.zeros((24, 128), F32)],
        axis=0,
    )
    vec_part[0] = tall.astype(BF16)
    send_ref[16] = tall.astype(BF16)
    block_copy(blocks, kept_ref, 0, 16)
    block_copy(blocks, send_ref, 16, 16)


def assemble(own_half, half_got, class_own, patch_out, class_out, class_grad):
    first = lax.axis_index("pipe") == 0
    half, count = patch_out.shape[1:]
    for b in range(IMGS):
        mine, theirs = own_half[b, :, :count], half_got[b, :half, :count].astype(F32)
        patch_out[b] = chosen(first, mine, theirs)
        patch_out[IMGS + b] = chosen(first, theirs, mine)
    mine, theirs = class_own[...].astype(F32), half_got[0, half:, :half].astype(F32)
    for at, out in ((0, class_out), (8, class_grad)):
        pair = mine[at : at + IMGS], theirs[at : at + IMGS]
        rows = jnp.concatenate([chosen(first, *pair), chosen(first, *pair[::-1])], axis=0)
        out[...] = rows.astype(BF16)


def place_blocks(plan, *refs):
    count = 2 * len(plan)
    pieces, (qkv_out, proj_out, fc1_out, fc2_out), (held, sems) = refs[:count], refs[count + 4 : count + 8], refs[count + 8 :]

    def put(at, source, n, first, target):
        for k in range(3):
            held[at, :, k * 128 : (k + 1) * 128] = source[n, first + k * 48 : first + (k + 1) * 48].astype(F32)
        pltpu.make_async_copy(held.at[at], target, sems.at[at]).start()

    @pl.when(lax.axis_index("pipe") == 0)
    def _():
        slot = 0
        for which, source in enumerate(pieces):
            stream, start = plan[which // 2]
            for n in range(source.shape[0]):
                block = position_block((which % 2) * 16 + start + n)
                down = pl.ds(pl.multiple_of((block >> 2) * 48, 48), 48)
                along = pl.ds(pl.multiple_of((block & 3) * 384, 384), 384)
                if stream == 0:
                    put(slot, source, n, 0, fc1_out.at[down, along])
                    put(slot + 1, source, n, 144, fc2_out.at[pl.ds(pl.multiple_of(block * 48, 48), 48)])
                    slot += 2
                else:
                    last = (block & 3) == 3

                    @pl.when(last)
                    def _():
                        put(slot, source, n, 0, proj_out.at[down])

                    @pl.when(jnp.logical_not(last))
                    def _():
                        put(slot, source, n, 0, qkv_out.at[down, along])

                    slot += 1
        for at in range(slot):
            pltpu.make_async_copy(held.at[at], fc2_out.at[pl.ds(0, 48)], sems.at[at]).wait()


def vector_outputs(part, *refs):
    vec_outs, (pre_out, post_out, bias_out) = refs[:10], refs[10:]
    first = lax.axis_index("pipe") == 0
    width = vec_outs[0].shape[1]
    tall = part[0].astype(F32)
    rows = [chosen(first, tall[k * 16 : (k + 1) * 16], tall[48 + k * 16 : 48 + (k + 1) * 16]) for k in range(3)]
    rows = jnp.concatenate(rows, axis=1)
    at = 0
    for out in vec_outs:
        for k in range(out.shape[1] // width):
            out[:, k * width : (k + 1) * width] = rows[at : at + 1]
            at += 1
    pre_out[...] = tall[96:104, 0:HEADS]
    post_out[...] = tall[104:112].T[0:HEADS]
    bias_out[...] = tall[112:113, 0:HEADS]


def class_gradients(*refs):
    factor_refs = refs[:-19]
    w_in, p_in, f1_in, f2_in, vec, *outs = refs[-19:-10]
    w, p, f1, f2, factors, *held, sems = refs[-10:]
    width = p.shape[0]

    @pl.when(lax.axis_index("pipe") != 0)
    def _():
        copies = [
            pltpu.make_async_copy(source, target, sems.at[n])
            for n, (source, target) in enumerate(((f1_in, f1), (f2_in, f2), (w_in, w), (p_in, p)))
        ]
        for copy in copies:
            copy.start()
        join_factors(factor_refs, factors)
        group = min(32, factors.shape[0])
        rows = group * IMGS * HEADS
        mask = head_mask(rows, width)
        spread = (
            lax.broadcasted_iota(jnp.int32, (rows, group * IMGS), 0) >> 3
            == lax.broadcasted_iota(jnp.int32, (rows, group * IMGS), 1)
        )
        spread = jnp.where(spread, 1.0, 0.0).astype(BF16)
        bias = jnp.concatenate([vec[8 + k : 9 + k].astype(F32) for k in range(4)], axis=1)
        for copy in copies:
            copy.wait()

        def expanded(vectors):
            return jnp.where(mask, mm(spread, vectors), 0.0).astype(BF16)

        def put(n, at, target, cut, piece):
            target[:, cut] = piece if n == 0 else target[:, cut] + piece
            if n == factors.shape[0] // group - 1:
                done.append(pltpu.make_async_copy(target.at[:, cut], outs[at].at[:, cut], sems.at[4 + len(done)]))
                done[-1].start()

        done = []
        whole = slice(0, width)
        for n in range(factors.shape[0] // group):
            part = slice(n * group, (n + 1) * group)
            wh, g, vectors = (factor_rows(factors, part, start, group) for start in (0, 16, 32))
            hidden_c, att1, bg1, inner1, og1 = (picked(vectors, kind, group) for kind in range(5))
            active, slope = gelu_pair(mm(inner1, f1[...]) + bias)
            ig1 = (mm_nt(og1, f2[...]) * slope).astype(BF16)
            put(n, 3, held[3], whole, mm_tn(active.astype(BF16), og1))
            put(n, 2, held[2], slice(0, f1.shape[1]), mm_tn(inner1, ig1))
            query = (mm(hidden_c, w[:, :width]) + vec[2:3].astype(F32)).astype(BF16)
            da1 = mm_nt(bg1, p[...]).astype(BF16)
            chosen_g = jnp.where(mask, mm(g, w[:, width : 2 * width]), 0.0).astype(BF16)
            dq1 = mm_tn(spread, chosen_g).astype(BF16)
            put(n, 1, held[1], whole, mm_tn(att1, bg1))
            parts = (mm_tn(hidden_c, dq1), mm_tn(g, expanded(query)), mm_tn(wh, expanded(da1)))
            for k, piece in enumerate(parts):
                put(n, 0, held[0], slice(k * width, (k + 1) * width), piece)
        for copy in done:
            copy.wait()


def join_factors(pieces, factors):
    at = 0
    for piece in pieces:
        factors[at : at + piece.shape[0]] = piece[...]
        at += piece.shape[0]


def factor_rows(factors, part, start, group):
    pieces = [factors[part, k * 48 + start : k * 48 + start + 16].reshape(group * 16, 128) for k in range(3)]
    return jnp.concatenate(pieces, axis=1)


def picked(vectors, kind, group):
    rows, cols = group * IMGS, group * 16
    row = lax.broadcasted_iota(jnp.int32, (rows, cols), 0)
    col = lax.broadcasted_iota(jnp.int32, (rows, cols), 1)
    wanted = (row >> 1) * 16 + kind * IMGS + (row & 1)
    return mm(jnp.where(col == wanted, 1.0, 0.0).astype(BF16), vectors).astype(BF16)


VM = pl.BlockSpec(memory_space=pltpu.VMEM)
SM = pl.BlockSpec(memory_space=pltpu.SMEM)
HB = pl.BlockSpec(memory_space=pltpu.HBM)


def call(body, ins, outs, scratch, name, limit, sems=0, far=0, aliases=None):
    return pl.pallas_call(
        body,
        out_shape=[jax.ShapeDtypeStruct(shape, kind) for shape, kind in outs],
        in_specs=[spec for spec, _ in ins],
        out_specs=[HB] * far + [VM] * (len(outs) - far),
        scratch_shapes=[pltpu.VMEM(shape, kind) for shape, kind in scratch]
        + ([pltpu.SemaphoreType.DMA((sems,))] if sems else []),
        compiler_params=pltpu.CompilerParams(vmem_limit_bytes=limit * 1024 * 1024),
        cost_estimate=pl.CostEstimate(flops=0, bytes_accessed=1, transcendentals=0),
        input_output_aliases=aliases or {},
        name=name,
    )(*[value for _, value in ins])


def swapped(array):
    return lax.ppermute(array, "pipe", [(0, 1), (1, 0)])


def exchanged(array, bits, cores=(0, 1)):
    dp = lax.axis_size("dp")
    pairs = [(core * dp + i, core * dp + (i ^ bits[core])) for core in cores for i in range(dp)]
    return lax.ppermute(array, ("pipe", "dp"), pairs)


def total(pieces, start, stop):
    parts = [piece[start:stop].astype(F32) for piece in pieces]
    return sum(parts[1:], parts[0]).astype(BF16)


def after(arrays, *others):
    return lax.optimization_barrier((arrays, others))[0]


NEAR, FAR = (4, 4), (8, 8)
LONG = (("halve", (1, 2)), ("halve", (2, 1)), ("halve", NEAR), ("swap", FAR), ("collect", NEAR), ("pair", (2, 1)), ("last", (1, 2)))
SHORT = (("halve", (1, 2)), ("halve", (2, 1)), ("swap", NEAR), ("swap", FAR), ("collect", (2, 1)), ("collect", (1, 2)))
GATHER = (("gather", FAR), ("gather", NEAR), ("gather", (2, 1)), ("gather", (1, 2)))


class Stream:
    def __init__(self, pieces, steps, rider=None):
        self.pieces, self.steps, self.rider, self.at = list(pieces), steps, rider, 0
        self.whole = lax.axis_size("dp") == 16
        self.leaving, self.count = self.pieces[0], 16 if steps is not GATHER else 1

    def wait(self, *others):
        self.pieces = list(after(tuple(self.pieces), *others))

    def swap(self, message, bits):
        count = message.shape[0]
        self.leaving = message if self.rider is None else jnp.concatenate([message, self.rider])
        got = exchanged(self.leaving, bits)
        if self.rider is not None:
            self.rider = total([self.rider, got[count:]], 0, 1)
        return got

    def step(self):
        if not self.whole:
            return
        kind, bits = self.steps[self.at]
        self.at += 1
        count = self.count
        if kind == "halve":
            got = self.swap(total(self.pieces, count // 2, count), bits)
            self.pieces, self.count = self.pieces + [got], count // 2
        elif kind == "swap":
            run = 1 if bits == FAR else 2
            mid = total(self.pieces, 0, count)
            turned = [total(self.pieces, at ^ run, (at ^ run) + run) for at in range(0, count, run)]
            self.pieces = [mid, self.swap(jnp.concatenate(turned), bits)]
            if self.steps[self.at][0] in ("collect", "pair"):
                self.pieces = [total(self.pieces, 0, count)]
        elif kind == "last":
            self.leaving = self.pieces[1]
            self.pieces = self.pieces + [exchanged(self.leaving, bits)]
        else:
            self.leaving = jnp.concatenate(self.pieces, axis=0) if len(self.pieces) > 1 else self.pieces[0]
            if kind == "pair":
                later = self.steps[self.at][1]
                self.pieces = [self.leaving, exchanged(self.leaving, bits), exchanged(self.leaving, later)]
                return
            self.pieces = [self.leaving, exchanged(self.leaving, bits, (1,) if kind == "gather" else (0, 1))]

    def parts(self):
        if self.whole:
            return self.pieces
        whole = lax.psum(total(self.pieces, 0, 16).astype(F32), "dp").astype(BF16)
        return [whole[at : at + 4] for at in range(0, 16, 4)]

    def ridden(self):
        if self.whole:
            return self.rider
        return lax.psum(self.rider.astype(F32), "dp").astype(BF16)


def local(
    patches, class_token, keep_mask, class_cotangent, norm1_gain, norm1_bias, qkv_weight, qv_bias,
    mix_pre, mix_post, post_bias, proj_weight, proj_bias, scale_attn, norm2_gain, norm2_bias,
    fc1_weight, fc1_bias, fc2_weight, fc2_bias, scale_mlp,
):
    dp = lax.axis_size("dp")
    images, count, width = patches.shape
    hidden_width = fc1_weight.shape[2]
    length, lanes = 208, 256
    half = width // 2
    flat = IMGS * length

    w_own, p_own, f1_own, f2_own = qkv_weight[0], proj_weight[0], fc1_weight[0], fc2_weight[0]
    w_got = swapped(w_own)
    small = (
        norm1_gain, norm1_bias, qv_bias, proj_bias, scale_attn, norm2_gain, norm2_bias, fc1_bias, fc2_bias, scale_mlp,
        mix_pre, mix_post, post_bias[None],
    )
    vec_own, pre_rows, post_rows, bias_row = call(
        prepare,
        [(HB, array) for array in small],
        [((16, width), BF16), ((HEADS, width), F32), ((HEADS, width), F32), ((1, width), F32)],
        [(array.shape, BF16) for array in small],
        "prepare",
        LIMIT_P,
        sems=13,
    )
    vec_got = swapped(vec_own)
    mixing = jnp.stack([mix_pre, mix_post]).astype(F32)
    rows = jnp.pad(patches, ((0, 0), (0, length - count), (0, 0)))
    p_late, f1_late, f2_late = after((p_own, f1_own, f2_own), w_got, vec_got, rows)
    p_got, f1_got, f2_got = swapped(p_late), swapped(f1_late), swapped(f2_late)

    token_shape = (IMGS, length, width)
    wide_shape = (IMGS, lanes, width)
    keep_scratch = ((8, lanes), F32)
    att, hid, queries, keys, values, probs = call(
        attention_forward,
        [(SM, mixing), (VM, rows), (VM, keep_mask), (VM, vec_own), (VM, vec_got), (HB, w_own), (HB, w_got),
         (VM, bias_row)],
        [(token_shape, BF16), (token_shape, BF16), (wide_shape, BF16), (wide_shape, BF16), (wide_shape, BF16),
         ((IMGS, HEADS * lanes, lanes), BF16)],
        [((width, 3 * width), BF16), ((width, HEADS * lanes), BF16), keep_scratch],
        "attention_forward",
        LIMIT_A,
        sems=1,
    )
    vec_shape = (16, width)
    send1, kept1, mg, vec0, vec1, class_own, class_other, factors = call(
        middle_kernel,
        [(VM, att), (VM, rows), (VM, keep_mask), (VM, class_token), (VM, class_cotangent), (VM, vec_own),
         (VM, vec_got), (HB, p_own), (HB, p_got), (HB, f1_own), (HB, f1_got), (HB, f2_own), (HB, f2_got), (HB, w_own),
         (HB, w_got)],
        [((17, 288, 128), BF16), ((16, 288, 128), BF16), (token_shape, F32), (vec_shape, F32), (vec_shape, F32),
         ((16, half), BF16), ((16, half), BF16), ((144, 128), BF16)],
        [((width, width), BF16), ((width, hidden_width), BF16), ((hidden_width, width), BF16),
         ((width, width), BF16), ((width, hidden_width), BF16), ((hidden_width, width), BF16),
         ((width, 3 * width), BF16), ((flat, hidden_width), BF16), ((flat, hidden_width), BF16),
         ((32, 288, 128), BF16), keep_scratch],
        "middle_kernel",
        LIMIT_B,
        sems=7,
    )

    def image_backward(b, mg):
        return call(
            lambda *refs: attention_backward(b, *refs),
            [(SM, mixing), (VM, mg), (VM, keep_mask), (VM, queries), (VM, keys), (VM, values), (VM, probs),
             (VM, vec_own), (VM, vec_got), (HB, p_own), (HB, p_got), (VM, bias_row), (VM, pre_rows), (VM, post_rows)],
            [((length, 3 * width), BF16), ((24, width), F32)],
            [((width, width), BF16), ((HEADS * lanes, lanes), BF16), ((width, HEADS * lanes), BF16),
             ((lanes, width), BF16), keep_scratch],
            f"attention_backward_{b}",
            LIMIT_C,
            sems=1,
        )

    got1 = swapped(send1)
    factors_got = got1[16, :144]
    stream1, shared = Stream((kept1, got1), LONG), Stream((factors[None], factors_got[None]), GATHER)
    join0, sum0 = image_backward(0, mg)
    stream1.wait(join0)
    stream1.step()
    join1, sum1 = image_backward(1, after(mg, stream1.leaving))
    mg = after(mg, join1)
    send2, kept2, vec_part, own_half, other_half = call(
        input_gradients,
        [(VM, mg), (VM, rows), (VM, hid), (VM, att), (VM, join0), (VM, join1), (VM, sum0), (VM, sum1), (VM, vec0),
         (VM, vec1), (VM, vec_own), (VM, vec_got), (HB, w_own), (HB, w_got), (VM, class_other)],
        [((17, 144, 128), BF16), ((16, 144, 128), BF16), ((1, 144, 128), BF16), ((IMGS, half, length), F32), ((IMGS, half + 16, length), BF16)],
        [((width, 3 * width), BF16), ((flat, 3 * width), BF16), ((32, 144, 128), BF16)],
        "input_gradients",
        LIMIT_C,
        sems=1,
    )
    got2, half_got = swapped(send2), swapped(other_half)
    stream2 = Stream((kept2, got2), SHORT, total([vec_part, got2[16:]], 0, 1))
    def turn(*streams):
        for stream in streams:
            turn.last = stream.wait(*turn.last) or (stream.step(), stream.leaving)[1:]

    turn.last = (kept2,)
    turn(stream1, stream2)
    turn.last += (half_got,)
    turn(shared, stream1, stream2, shared, stream1, stream2, shared, shared, stream1, stream2, stream1)
    patch_out, class_result, class_grad = call(
        assemble,
        [(VM, part) for part in after((own_half, half_got, class_own), stream1.leaving)],
        [((2 * IMGS, half, count), F32), ((2 * IMGS, half), BF16), ((2 * IMGS, half), BF16)],
        [],
        "assemble",
        LIMIT_C,
    )
    turn.last += tuple(shared.pieces)
    turn(stream2)
    small_outs = call(
        vector_outputs,
        [(VM, stream2.ridden())],
        [((1, size * width), F32) for size in (1, 1, 2, 1, 1, 1, 1, 4, 1, 1)]
        + [((HEADS, HEADS), F32), ((HEADS, HEADS), F32), ((1, HEADS), F32)],
        [],
        "vector_outputs",
        LIMIT_C,
    )
    turn.last += (patch_out, class_result, class_grad, small_outs)
    turn(stream1, stream2)
    if dp == 16:
        factor_parts = after(tuple(shared.pieces), stream2.leaving)
    else:
        factor_parts = tuple(lax.all_gather(part, "dp") for part in (factors, factors_got))
    matrices = [((width, 3 * width), F32), ((width, width), F32), ((width, hidden_width), F32), ((hidden_width, width), F32)]
    outs = call(
        class_gradients,
        [(VM, part) for part in factor_parts]
        + [(HB, w_own), (HB, p_own), (HB, f1_own), (HB, f2_own), (VM, vec_own)],
        matrices,
        [(shape, BF16) for shape, _ in matrices] + [((2 * dp, 144, 128), BF16)] + matrices,
        "class_gradients",
        LIMIT_E,
        sems=10,
        far=4,
    )
    parts = [], []
    for at, stream in enumerate((stream1, stream2)):
        start = 0
        for part in stream.parts():
            parts[at].append((at, start, part))
            start += part.shape[0]
    for name in ("first_outputs", "last_outputs"):
        chosen_parts = [part for group in parts for part in group if (part[1] < 8 or part[2].shape[0] == 4 and part[1] < 12) == (name == "first_outputs")]
        if name == "last_outputs":
            chosen_parts = [(at, start, after(part, outs[0])) for at, start, part in chosen_parts]
        plan = [(at, start) for at, start, _ in chosen_parts]
        slots = sum(2 * part.shape[0] * (2 - at) for at, _, part in chosen_parts)
        arrays = [(VM, array) for _, _, part in chosen_parts for array in (part, swapped(part))]
        outs = call(
            lambda *refs: place_blocks(plan, *refs),
            arrays + [(HB, out) for out in outs],
            matrices,
            [((slots, 48, width), F32)],
            name,
            LIMIT_D,
            sems=slots,
            far=4,
            aliases={len(arrays) + n: n for n in range(4)},
        )
    qkv_out, proj_out, fc1_out, fc2_out = outs
    n1g, n1b, qvb, pb, sa, n2g, n2b, f1b, f2b, sm, pre, post, bias = small_outs
    return (
        class_result, patch_out.transpose(0, 2, 1), class_grad, n1g, n1b, qkv_out[None], qvb, proj_out[None], pb, sa, n2g, n2b,
        fc1_out[None], f1b, fc2_out[None], f2b, sm, pre, post, bias[0],
    )


def solution(mesh):
    stacked = (P("pipe", None), P("pipe", None), P("pipe", None, None))
    row, _, cube = stacked
    return jax.shard_map(
        local,
        mesh=mesh,
        in_specs=(
            P("dp", None, None), P("dp", None), P("dp", None), P("dp", None),
            row, row, cube, row, P(), P(), P(), cube, row, row, row, row, cube, row, cube, row, row,
        ),
        out_specs=(
            P("dp", "pipe"), P("dp", None, "pipe"), P("dp", "pipe"),
            row, row, cube, row, cube, row, row, row, row, cube, row, cube, row, row, P(), P(), P(),
        ),
        check_vma=False,
    )
```

```python
import jax
import jax.numpy as jnp
from jax import lax
from jax.experimental import pallas as pl
from jax.experimental.pallas import tpu as pltpu
from jax.sharding import PartitionSpec as P

HEADS = 8
IMGS = 2
LIMIT_P, LIMIT_A, LIMIT_B, LIMIT_C, LIMIT_D, LIMIT_E = 60, 24, 24, 24, 24, 24
LOG2E = 1.4426950408889634
F32 = jnp.float32
BF16 = jnp.bfloat16


def mm(left, right):
    return lax.dot_general(left, right, (((1,), (0,)), ((), ())), preferred_element_type=F32)


def mm_nt(left, right):
    return lax.dot_general(left, right, (((1,), (1,)), ((), ())), preferred_element_type=F32)


def mm_tn(left, right):
    return lax.dot_general(left, right, (((0,), (0,)), ((), ())), preferred_element_type=F32)


def normed(rows):
    centred = rows - jnp.mean(rows, -1, keepdims=True)
    scale = lax.rsqrt(jnp.mean(centred * centred, -1, keepdims=True) + 1e-06)
    return centred * scale, scale


def norm_back(normal, scale, grad):
    inner = jnp.mean(grad * normal, -1, keepdims=True)
    return (grad - jnp.mean(grad, -1, keepdims=True) - normal * inner) * scale


def col_sum(rows):
    return jnp.sum(rows, axis=0, keepdims=True)


def gelu_pair(rows):
    phi = 0.5 + 0.5 * lax.erf(rows * 0.7071067811865476)
    return rows * phi, phi + rows * (jnp.exp2(rows * rows * (-0.5 * LOG2E)) * 0.3989422804014327)


def head_mask(rows, width):
    lane = lax.broadcasted_iota(jnp.int32, (rows, width), 1)
    head = lax.rem(lax.broadcasted_iota(jnp.int32, (rows, width), 0), HEADS)
    size = width // HEADS
    return (lane >= head * size) & (lane < head * size + size)


def chosen(is_first, first, other):
    return jnp.where(is_first, first, other)


def scaled_rows(rows, factors):
    size = rows.shape[0] // HEADS
    parts = []
    for head, factor in enumerate(factors):
        part = rows[head * size : (head + 1) * size]
        parts.append(part * jnp.full((1, rows.shape[1]), factor, F32).astype(BF16))
    return jnp.concatenate(parts, axis=0)


def transposed(rows):
    return rows.T


def own_place():
    core = lax.axis_index("pipe")
    return core, core * 16 + (lax.axis_index("dp") if lax.axis_size("dp") == 16 else 0)


def fetch(first, own, got, target, sem):
    @pl.when(first)
    def _():
        pltpu.make_async_copy(own, target, sem).start()

    @pl.when(jnp.logical_not(first))
    def _():
        pltpu.make_async_copy(got, target, sem).start()

    return pltpu.make_async_copy(own, target, sem)


def own_images(first, rows):
    return chosen(first, rows[0:IMGS], rows[IMGS : 2 * IMGS])


def token_rows(rows_ref):
    rows = rows_ref[pl.ds(lax.axis_index("pipe") * IMGS, IMGS)]
    return rows.reshape(-1, rows.shape[2])


def keep_columns(first, mask_ref, scratch):
    scratch[...] = jnp.zeros_like(scratch)
    scratch[0:IMGS, 0 : mask_ref.shape[1]] = own_images(first, mask_ref[...].astype(F32))
    return scratch[...].T


def prepare(*refs):
    sources, (vec_ref, pre_ref, post_ref, bias_ref), held, sems = refs[:13], refs[13:17], refs[17:30], refs[30]
    copies = [pltpu.make_async_copy(*pair, sems.at[n]) for n, pair in enumerate(zip(sources, held))]
    for copy in copies:
        copy.start()
    for copy in copies:
        copy.wait()
    n1g, n1b, qvb, pb, sa, n2g, n2b, f1b, f2b, sm, pre, post, post_bias = held
    width = n1g.shape[1]
    rows = [n1g[...], n1b[...], qvb[:, :width], qvb[:, width:], pb[...], sa[...], n2g[...], n2b[...]]
    rows += [f1b[:, k * width : (k + 1) * width] for k in range(4)] + [f2b[...], sm[...]]
    rows = [row.astype(F32) for row in rows] + [jnp.zeros((2, width), F32)]
    vec_ref[...] = jnp.concatenate(rows, axis=0).astype(BF16)
    spread = jnp.where(head_mask(HEADS, width), 1.0, 0.0).astype(BF16)
    pre_ref[...] = mm(pre[...], spread)
    post_ref[...] = mm_tn(post[...], spread)
    bias_ref[...] = mm(post_bias[...], spread)


def attention_forward(
    mixing, rows_ref, mask_ref, vec_own, vec_got, w_own, w_got, bias_ref,
    att_ref, hid_ref, q_ref, k_ref, v_ref, pt_ref, w_ref, vs_ref, keep_ref, sems,
):
    first = lax.axis_index("pipe") == 0
    weights_copy = fetch(first, w_own, w_got, w_ref, sems.at[0])
    width = rows_ref.shape[2]
    length = rows_ref.shape[1]
    lanes = q_ref.shape[1]
    size = width // HEADS
    keeps = keep_columns(first, mask_ref, keep_ref)

    vec = chosen(first, vec_own[...].astype(F32), vec_got[...].astype(F32))
    scale = size ** (-0.5) * LOG2E
    pad_rows = jnp.zeros((lanes - length, width), BF16)
    same = lax.broadcasted_iota(jnp.int32, (length, lanes), 0) == lax.broadcasted_iota(jnp.int32, (length, lanes), 1)

    for b in range(IMGS):
        normal, _ = normed(rows_ref[lax.axis_index("pipe") * IMGS + b].astype(F32))
        hidden = (normal * vec[0:1] + vec[1:2]).astype(BF16)
        hid_ref[b] = hidden
        if b == 0:
            weights_copy.wait()
        joined = mm(hidden, w_ref[...])
        queries = joined[:, :width] + vec[2:3]
        keys = joined[:, width : 2 * width]
        values = joined[:, 2 * width :] + vec[3:4]
        low_k = keys.astype(BF16)
        low_v = values.astype(BF16)
        q_ref[b, :length] = queries.astype(BF16)
        k_ref[b, :length] = low_k
        v_ref[b, :length] = low_v
        q_ref[b, length:] = pad_rows
        k_ref[b, length:] = pad_rows
        v_ref[b, length:] = pad_rows
        q_t = transposed(q_ref[b])
        v_t = transposed(v_ref[b])
        keep = keeps[:length, b : b + 1]
        allowed = (keep > 0.0) | same
        for h in range(HEADS):
            scaled_q = scaled_rows(q_t, [mixing[0, h, c] for c in range(HEADS)])
            scores = jnp.where(allowed, mm(low_k, scaled_q) * scale, -1e30)
            top = jnp.max(scores, axis=0, keepdims=True)
            weights = jnp.exp2(scores - top)
            weights = weights * (1.0 / jnp.sum(weights, axis=0, keepdims=True))
            pt_ref[b, h * lanes : h * lanes + length] = weights.astype(BF16)
            pt_ref[b, h * lanes + length : (h + 1) * lanes] = jnp.zeros((lanes - length, lanes), BF16)
            vs_ref[:, h * lanes : (h + 1) * lanes] = scaled_rows(v_t, [mixing[1, c, h] for c in range(HEADS)])
        mixed = transposed(mm(vs_ref[...], pt_ref[b]))[:length]
        low_f = low_v.astype(F32)
        extra = bias_ref[...] * (col_sum(low_f * keep) + (1.0 - keep) * low_f)
        att_ref[b] = (mixed + extra).astype(BF16)


def block_copy(source, target, start, count):
    for n in range(count):
        target[n] = source[position_block(start + n)]


def position_block(at):
    core, me = own_place()
    first_bit, second_bit = (at >> 3) & 1, (at >> 2) & 1
    rest = ((at >> 4) << 4) | ((at & 1) << 3) | (((at >> 1) & 1) << 2)
    x_first = rest | first_bit | (second_bit << 1)
    y_first = rest | second_bit | (first_bit << 1)
    return jnp.where(core == (at >> 4), x_first, y_first) ^ me


def block_position(block):
    core, me = own_place()
    apart = block ^ me
    x_bit, y_bit = apart & 1, (apart >> 1) & 1
    half = apart >> 4
    top = jnp.where(core == half, (x_bit << 3) | (y_bit << 2), (y_bit << 3) | (x_bit << 2))
    return (half << 4) | top | (((apart >> 2) & 1) << 1) | ((apart >> 3) & 1)


def put_blocks(target, rows, start, wide):
    tall, across = 48, 384
    for rb in range(rows.shape[0] // tall):
        for cb in range(rows.shape[1] // across):
            block = rb * wide[0] + wide[1] + cb
            for k in range(3):
                piece = rows[rb * tall : (rb + 1) * tall, cb * across + k * 128 : cb * across + (k + 1) * 128]
                target[block, start + k * tall : start + (k + 1) * tall] = piece.astype(BF16)


def middle_kernel(
    att_ref, rows_ref, mask_ref, class_ref, cot_ref,
    vec_own, vec_got, p_own, p_got, f1_own, f1_got, f2_own, f2_got, w_own, w_got,
    send_ref, kept_ref, mg_ref, vec_out, vec_out1, class_own, class_other, factor_ref,
    p0_ref, f10, f20, p1_ref, f11, f21, w1_ref, act_ref, gp_ref, blocks, keep_ref, sems,
):
    first = lax.axis_index("pipe") == 0
    p0_copy = fetch(first, p_own, p_got, p0_ref, sems.at[0])
    w1_copy = fetch(first, w_got, w_own, w1_ref, sems.at[3])
    f10_copy = fetch(first, f1_own, f1_got, f10, sems.at[1])
    f20_copy = fetch(first, f2_own, f2_got, f20, sems.at[2])
    p1_copy = fetch(first, p_got, p_own, p1_ref, sems.at[4])
    f11_copy = fetch(first, f1_got, f1_own, f11, sems.at[5])
    f21_copy = fetch(first, f2_got, f2_own, f21, sems.at[6])
    length, width = rows_ref.shape[1], rows_ref.shape[2]
    flat = IMGS * length
    size = width // HEADS
    patches = mask_ref.shape[1]
    keep_ref[...] = jnp.zeros_like(keep_ref)
    keep_ref[0:IMGS, 0:patches] = own_images(first, mask_ref[...].astype(F32))
    keep_rows = keep_ref[0:IMGS, :length]
    keep_lane = lax.broadcasted_iota(jnp.int32, (IMGS, length), 1)
    keep_rows = jnp.where(keep_lane == patches, 1.0, keep_rows)

    own, got = vec_own[...].astype(F32), vec_got[...].astype(F32)
    vec, vec1 = chosen(first, own, got), chosen(first, got, own)

    def wide_bias(v):
        return jnp.concatenate([v[8 + k : 9 + k] for k in range(4)], axis=1)

    blank = jnp.zeros((8 - IMGS, width), F32)
    class_rows = jnp.concatenate([own_images(first, class_ref[...].astype(F32)), blank], axis=0)
    w1_copy.wait()
    normal_c, _ = normed(class_rows)
    hidden_c = (normal_c * vec1[0:1] + vec1[1:2]).astype(BF16)
    query = (mm(hidden_c, w1_ref[:, :width]) + vec1[2:3]).astype(BF16).astype(F32)
    mask = head_mask(IMGS * HEADS, width)

    def spread(rows):
        both = jnp.concatenate(
            [jnp.broadcast_to(rows[b : b + 1], (HEADS, width)) for b in range(IMGS)], axis=0
        )
        return jnp.where(mask, both, 0.0)

    def gathered(rows):
        kept = jnp.where(mask, rows, 0.0)
        parts = [col_sum(kept[b * HEADS : (b + 1) * HEADS]) for b in range(IMGS)]
        return jnp.concatenate(parts + [jnp.zeros((8 - IMGS, width), F32)], axis=0)

    query_rows = mm_nt(spread(query).astype(BF16), w1_ref[:, width : 2 * width]).astype(BF16)

    p0_copy.wait()
    branch = mm(att_ref[...].reshape(flat, width), p0_ref[...]) + vec[4:5]
    middle = token_rows(rows_ref).astype(F32) + vec[5:6] * branch
    normal, norm_scale = normed(middle)
    inner_low = (normal * vec[6:7] + vec[7:8]).astype(BF16)
    f10_copy.wait()
    bias = wide_bias(vec)
    step = f10.shape[1] // 2
    for k in range(2):
        cut = slice(k * step, (k + 1) * step)
        inner = mm(inner_low, f10[:, cut]) + bias[:, cut]
        active, slope = gelu_pair(inner)
        act_ref[:, cut] = active.astype(BF16)
        gp_ref[:, cut] = slope.astype(BF16)
    f20_copy.wait()
    outer = mm(act_ref[...], f20[...]) + vec[12:13]
    sent = (middle + vec[13:14] * outer).astype(BF16).astype(F32)

    upper1 = jnp.concatenate([own_images(first, cot_ref[...].astype(F32)), blank], axis=0)
    og1 = (upper1 * vec1[13:14]).astype(BF16)
    f21_copy.wait()
    dact1 = mm_nt(og1, f21[...])
    at_row = lax.broadcasted_iota(jnp.int32, (length, width), 0)
    hiddens, normals, scales, probs, low_probs, sums, whs = [], [], [], [], [], [], []
    for b in range(IMGS):
        tokens = jnp.where(at_row == patches, class_rows[b : b + 1], sent[b * length : (b + 1) * length])
        n1, s1 = normed(tokens)
        h1 = (n1 * vec1[0:1] + vec1[1:2]).astype(BF16)
        scores = mm_nt(query_rows[b * HEADS : (b + 1) * HEADS], h1) * (size ** (-0.5) * LOG2E)
        scores = jnp.where(keep_rows[b : b + 1] > 0.0, scores, -1e30)
        weights = jnp.exp2(scores - jnp.max(scores, axis=-1, keepdims=True))
        weights = weights / jnp.sum(weights, axis=-1, keepdims=True)
        low = weights.astype(BF16)
        hiddens.append(h1)
        normals.append(n1)
        scales.append(s1)
        probs.append(weights)
        low_probs.append(low)
        sums.append(jnp.sum(low.astype(F32), axis=-1, keepdims=True))
        whs.append(mm(low, h1))
    wh = jnp.concatenate(whs, axis=0).astype(BF16)
    prob_sum = gathered(jnp.broadcast_to(jnp.concatenate(sums, axis=0), (IMGS * HEADS, width)))
    att1 = (gathered(mm(wh, w1_ref[:, 2 * width :])) + vec1[3:4] * prob_sum).astype(BF16)
    p1_copy.wait()
    branch1 = mm(att1, p1_ref[...]) + vec1[4:5]
    middle1 = class_rows + vec1[5:6] * branch1
    normal2, scale2 = normed(middle1)
    inner1 = (normal2 * vec1[6:7] + vec1[7:8]).astype(BF16)
    f11_copy.wait()
    active1, slope1 = gelu_pair(mm(inner1, f11[...]) + wide_bias(vec1))
    outer1 = mm(active1.astype(BF16), f21[...]) + vec1[12:13]
    class_result = middle1 + vec1[13:14] * outer1

    ig1 = (dact1 * slope1).astype(BF16)
    dh2 = mm_nt(ig1, f11[...])
    mg1 = upper1 + norm_back(normal2, scale2, dh2 * vec1[6:7])
    bg1 = (mg1 * vec1[5:6]).astype(BF16)
    da1 = mm_nt(bg1, p1_ref[...]).astype(BF16).astype(F32)
    value_rows = mm_nt(spread(da1).astype(BF16), w1_ref[:, 2 * width :]).astype(BF16)
    low_grads, gs = [], []
    for b in range(IMGS):
        part = slice(b * HEADS, (b + 1) * HEADS)
        dw = mm_nt(value_rows[part], hiddens[b])
        ds = probs[b] * (dw - jnp.sum(probs[b] * dw, axis=-1, keepdims=True))
        low = (ds * size ** (-0.5)).astype(BF16)
        low_grads.append(low)
        gs.append(mm(low, hiddens[b]))
    g_rows = jnp.concatenate(gs, axis=0).astype(BF16)
    dq1 = gathered(mm(g_rows, w1_ref[:, width : 2 * width])).astype(BF16)
    dclass = mm_nt(dq1, w1_ref[:, :width])
    uppers, grads = [], []
    n1g, n1b = jnp.zeros((1, width), F32), jnp.zeros((1, width), F32)
    for b in range(IMGS):
        part = slice(b * HEADS, (b + 1) * HEADS)
        left = jnp.concatenate([low_grads[b], low_probs[b]], axis=0)
        right = jnp.concatenate([query_rows[part], value_rows[part]], axis=0)
        dh1 = mm_tn(left, right)
        grads.append(dh1)
        n1g = n1g + col_sum(dh1 * normals[b])
        n1b = n1b + col_sum(dh1)
        dtokens = norm_back(normals[b], scales[b], dh1 * vec1[0:1])
        uppers.append(jnp.where(at_row < patches, dtokens, 0.0).astype(BF16).astype(F32))

    def class_row(arrays):
        return jnp.concatenate([array[patches : patches + 1] for array in arrays], axis=0)

    dclass = dclass[0:IMGS]
    class_normal = class_row(normals)
    n1g = n1g + col_sum(dclass * class_normal)
    n1b = n1b + col_sum(dclass)
    class_grads = [
        mg1[0:IMGS] + norm_back(class_normal, class_row(scales), (class_row(grads) + dclass) * vec1[0:1])
    ]
    upper = jnp.concatenate(uppers, axis=0)
    class_rows = jnp.concatenate([class_result] + class_grads + [blank], axis=0)
    low_half, high_half = class_rows[:, : width // 2], class_rows[:, width // 2 :]
    class_own[...] = chosen(first, low_half, high_half).astype(BF16)
    class_other[...] = chosen(first, high_half, low_half).astype(BF16)
    ig1_sum = col_sum(ig1.astype(F32))
    vec_out1[...] = jnp.concatenate(
        [
            n1g,
            n1b,
            col_sum(dq1.astype(F32)),
            col_sum(da1 * prob_sum),
            col_sum(bg1.astype(F32)),
            col_sum(mg1 * branch1),
            col_sum(dh2 * normal2),
            col_sum(dh2),
        ]
        + [ig1_sum[:, k * width : (k + 1) * width] for k in range(4)]
        + [col_sum(og1.astype(F32)), col_sum(upper1 * outer1), jnp.zeros((2, width), F32)],
        axis=0,
    )
    pieces = [piece.astype(F32)[0:IMGS] for piece in (hidden_c, att1, bg1, inner1, og1)]
    vectors = jnp.concatenate(pieces + [jnp.zeros((16 - 5 * IMGS, width), F32)], axis=0).astype(BF16)
    for k in range(3):
        lanes = slice(k * 128, (k + 1) * 128)
        factor_ref[k * 48 : k * 48 + 16] = wh[:, lanes]
        factor_ref[k * 48 + 16 : k * 48 + 32] = g_rows[:, lanes]
        factor_ref[k * 48 + 32 : k * 48 + 48] = vectors[:, lanes]

    sm_grad = col_sum(upper * outer)
    og = (upper * vec[13:14]).astype(BF16)
    put_blocks(blocks, mm_tn(act_ref[...], og), 144, (1, 0))
    dh = jnp.zeros((flat, width), F32)
    fc1_sums = []
    step = f10.shape[1] // 1
    for k in range(1):
        cut = slice(k * step, (k + 1) * step)
        ig = (mm_nt(og, f20[cut, :]) * gp_ref[:, cut].astype(F32)).astype(BF16)
        ig_sum = col_sum(ig.astype(F32))
        fc1_sums += [ig_sum[:, at : at + width] for at in range(0, step, width)]
        put_blocks(blocks, mm_tn(inner_low, ig), 0, (4, k * step // width))
        dh = dh + mm_nt(ig, f10[:, cut])
    mg = upper + norm_back(normal, norm_scale, dh * vec[6:7])
    mg_ref[...] = mg.reshape(IMGS, length, width)
    vec_out[...] = jnp.concatenate(
        [jnp.zeros((4, width), F32), jnp.zeros((1, width), F32), col_sum(mg * branch), col_sum(dh * normal), col_sum(dh)]
        + fc1_sums
        + [col_sum(og.astype(F32)), sm_grad, jnp.zeros((2, width), F32)],
        axis=0,
    )
    block_copy(blocks, kept_ref, 0, 16)
    block_copy(blocks, send_ref, 16, 16)
    send_ref[16, 0:144] = factor_ref[...]
    send_ref[16, 144:288] = jnp.zeros((144, 128), BF16)


def attention_backward(
    b, mixing, mg_ref, mask_ref, q_ref, k_ref, v_ref, pt_ref, vec_own, vec_got, p_own, p_got, bias_ref,
    pre_rows, post_rows, join_ref, sum_ref, p_ref, dm_ref, ks_ref, da_ref, keep_ref, sems,
):
    first = lax.axis_index("pipe") == 0
    p_copy = fetch(first, p_own, p_got, p_ref, sems.at[0])
    length, width = mg_ref.shape[1], mg_ref.shape[2]
    lanes = q_ref.shape[1]
    size = width // HEADS
    root = size ** (-0.5)
    scale_row = chosen(first, vec_own[5:6].astype(F32), vec_got[5:6].astype(F32))
    bg = (mg_ref[b] * scale_row).astype(BF16)
    keep = keep_columns(first, mask_ref, keep_ref)[:length, b : b + 1]
    p_copy.wait()
    da = mm_nt(bg, p_ref[...]).astype(BF16)
    da_ref[:length] = da
    da_ref[length:] = jnp.zeros((lanes - length, width), BF16)
    da_t = transposed(da_ref[...])
    k_t = transposed(k_ref[b])
    low_v = v_ref[b, :length]
    val_f = low_v.astype(F32)
    key_f = k_ref[b, :length].astype(F32)
    da_f = da.astype(F32)
    biased = da_f * bias_ref[...]
    dv = keep * col_sum(biased) + (1.0 - keep) * biased
    bias_sum = col_sum(da_f * (col_sum(val_f * keep) + (1.0 - keep) * val_f))
    post_parts = []
    for c in range(HEADS):
        scaled = scaled_rows(da_t, [mixing[1, h, c] for h in range(HEADS)])
        dp = mm(low_v, scaled)
        weights = pt_ref[b, c * lanes : c * lanes + length]
        w_f = weights.astype(F32)
        dm = w_f * (dp - col_sum(w_f * dp))
        dm_ref[c * lanes : c * lanes + length] = dm.astype(BF16)
        dm_ref[c * lanes + length : (c + 1) * lanes] = jnp.zeros((lanes - length, lanes), BF16)
        moved = mm(weights, da_ref[...])
        dv = dv + moved * post_rows[c : c + 1]
        post_parts.append(col_sum(moved * val_f))
        ks_ref[:, c * lanes : (c + 1) * lanes] = scaled_rows(k_t, [mixing[0, c, h] for h in range(HEADS)])
    dk = jnp.zeros((length, width), F32)
    pre_parts = []
    for h in range(HEADS):
        moved = mm(dm_ref[h * lanes : h * lanes + length], q_ref[b])
        dk = dk + moved * pre_rows[h : h + 1]
        pre_parts.append(col_sum(moved * key_f))
    dq = transposed(mm(ks_ref[...], dm_ref[...]))[:length] * root
    join_ref[:, :width] = dq.astype(BF16)
    join_ref[:, width : 2 * width] = (dk * root).astype(BF16)
    join_ref[:, 2 * width :] = dv.astype(BF16)
    sum_ref[...] = jnp.concatenate(
        [part * root for part in pre_parts] + post_parts + [bias_sum, jnp.zeros((7, width), F32)], axis=0
    )


def input_gradients(
    mg_ref, rows_ref, hid_ref, att_ref, join0, join1, sum0, sum1, vec_in, vec_in1, vec_own, vec_got, w_own, w_got,
    class_other,
    send_ref, kept_ref, vec_part, own_half, other_half, w_ref, join_ref, blocks, sems,
):
    first = lax.axis_index("pipe") == 0
    w_copy = fetch(first, w_own, w_got, w_ref, sems.at[0])
    length, width = rows_ref.shape[1], rows_ref.shape[2]
    size = width // HEADS
    flat = IMGS * length
    vec = chosen(first, vec_own[...].astype(F32), vec_got[...].astype(F32))
    mg = mg_ref[...].reshape(flat, width)
    bg = (mg * vec[5:6]).astype(BF16)
    pb_grad = col_sum(bg.astype(F32))
    put_blocks(blocks, mm_tn(att_ref[...].reshape(flat, width), bg), 0, (4, 3))
    join_ref[:length] = join0[...]
    join_ref[length:] = join1[...]
    hidden = hid_ref[...].reshape(flat, width)
    put_blocks(blocks, mm_tn(hidden, join_ref[...]), 0, (4, 0))
    w_copy.wait()
    dh = mm_nt(join_ref[...], w_ref[...])
    normal, norm_scale = normed(token_rows(rows_ref).astype(F32))
    patch = mg + norm_back(normal, norm_scale, dh * vec[0:1])
    half = width // 2
    low_half, high_half = patch[:, :half], patch[:, half:]
    own_rows, other_rows = chosen(first, low_half, high_half), chosen(first, high_half, low_half)
    for b in range(IMGS):
        own_half[b] = transposed(own_rows[b * length : (b + 1) * length])
        other_half[b, :half] = transposed(other_rows[b * length : (b + 1) * length]).astype(BF16)
        other_half[b, half:] = jnp.zeros((16, length), BF16)
    other_half[0, half:, :half] = class_other[...]

    dq_sum = col_sum(join_ref[:, :width].astype(F32))
    dv_sum = col_sum(join_ref[:, 2 * width :].astype(F32))
    late = jnp.concatenate(
        [col_sum(dh * normal), col_sum(dh), dq_sum, dv_sum, pb_grad, jnp.zeros((11, width), F32)], axis=0
    )
    vec0 = vec_in[...] + late
    lane = lax.broadcasted_iota(jnp.int32, (width, 128), 1)
    feature = lax.broadcasted_iota(jnp.int32, (width, 128), 0)
    groups = jnp.where((feature >= lane * size) & (feature < lane * size + size), 1.0, 0.0)
    small = lax.dot_general(
        sum0[...] + sum1[...], groups, (((1,), (0,)), ((), ())),
        preferred_element_type=F32, precision=lax.Precision.HIGHEST,
    )
    tall = jnp.concatenate(
        [vec0[:14, :128], small[16:17], vec0[15:, :128]]
        + [vec0[:, k * 128 : (k + 1) * 128] for k in (1, 2)]
        + [vec_in1[:, k * 128 : (k + 1) * 128] for k in range(3)]
        + [small[:16]],
        axis=0,
    )
    vec_part[...] = tall.astype(BF16)
    send_ref[16, :112] = tall.astype(BF16)
    send_ref[16, 112:] = jnp.zeros((32, 128), BF16)
    block_copy(blocks, kept_ref, 0, 16)
    block_copy(blocks, send_ref, 16, 16)


def assemble(own_half, half_got, class_own, patch_out, class_out, class_grad):
    first = lax.axis_index("pipe") == 0
    half, count = patch_out.shape[1:]
    for b in range(IMGS):
        mine, theirs = own_half[b, :, :count], half_got[b, :half, :count].astype(F32)
        patch_out[b] = chosen(first, mine, theirs)
        patch_out[IMGS + b] = chosen(first, theirs, mine)
    mine, theirs = class_own[...].astype(F32), half_got[0, half:, :half].astype(F32)
    for at, out in ((0, class_out), (8, class_grad)):
        pair = mine[at : at + IMGS], theirs[at : at + IMGS]
        rows = jnp.concatenate([chosen(first, *pair), chosen(first, *pair[::-1])], axis=0)
        out[...] = rows.astype(BF16)


def place_blocks(plan, *refs):
    count = len(plan)
    pieces, (qkv_out, proj_out, fc1_out, fc2_out), (held, sems) = refs[:count], refs[count + 4 : count + 8], refs[count + 8 :]

    def put(at, source, n, first, target):
        for k in range(3):
            held[at, :, k * 128 : (k + 1) * 128] = source[n, first + k * 48 : first + (k + 1) * 48].astype(F32)
        pltpu.make_async_copy(held.at[at], target, sems.at[at]).start()

    @pl.when(lax.axis_index("pipe") == 0)
    def _():
        slot = 0
        for which, source in enumerate(pieces):
            stream, start = plan[which]
            for n in range(source.shape[0]):
                block = position_block(start + n)
                down = pl.ds(pl.multiple_of((block >> 2) * 48, 48), 48)
                along = pl.ds(pl.multiple_of((block & 3) * 384, 384), 384)
                if stream == 0:
                    put(slot, source, n, 0, fc1_out.at[down, along])
                    put(slot + 1, source, n, 144, fc2_out.at[pl.ds(pl.multiple_of(block * 48, 48), 48)])
                    slot += 2
                else:
                    last = (block & 3) == 3

                    @pl.when(last)
                    def _():
                        put(slot, source, n, 0, proj_out.at[down])

                    @pl.when(jnp.logical_not(last))
                    def _():
                        put(slot, source, n, 0, qkv_out.at[down, along])

                    slot += 1
        for at in range(slot):
            pltpu.make_async_copy(held.at[at], fc2_out.at[pl.ds(0, 48)], sems.at[at]).wait()


def vector_outputs(part, *refs):
    vec_outs, (pre_out, post_out, bias_out) = refs[:10], refs[10:]
    first = lax.axis_index("pipe") == 0
    width = vec_outs[0].shape[1]
    tall = part[...].astype(F32)
    rows = [chosen(first, tall[k * 16 : (k + 1) * 16], tall[48 + k * 16 : 48 + (k + 1) * 16]) for k in range(3)]
    rows = jnp.concatenate(rows, axis=1)
    at = 0
    for out in vec_outs:
        for k in range(out.shape[1] // width):
            out[:, k * width : (k + 1) * width] = rows[at : at + 1]
            at += 1
    pre_out[...] = tall[96:104, 0:HEADS]
    post_out[...] = tall[104:112].T[0:HEADS]
    bias_out[...] = tall[14:15, 0:HEADS]


def class_gradients(*refs):
    factor_refs = refs[:-19]
    w_in, p_in, f1_in, f2_in, vec, *outs = refs[-19:-10]
    w, p, f1, f2, factors, *held, sems = refs[-10:]
    width = p.shape[0]

    @pl.when(lax.axis_index("pipe") != 0)
    def _():
        copies = [
            pltpu.make_async_copy(source, target, sems.at[n])
            for n, (source, target) in enumerate(((f1_in, f1), (f2_in, f2), (w_in, w), (p_in, p)))
        ]
        for copy in copies:
            copy.start()
        join_factors(factor_refs, factors)
        group = min(32, factors.shape[0])
        rows = group * IMGS * HEADS
        mask = head_mask(rows, width)
        spread = (
            lax.broadcasted_iota(jnp.int32, (rows, group * IMGS), 0) >> 3
            == lax.broadcasted_iota(jnp.int32, (rows, group * IMGS), 1)
        )
        spread = jnp.where(spread, 1.0, 0.0).astype(BF16)
        bias = jnp.concatenate([vec[8 + k : 9 + k].astype(F32) for k in range(4)], axis=1)
        for copy in copies:
            copy.wait()

        def expanded(vectors):
            return jnp.where(mask, mm(spread, vectors), 0.0).astype(BF16)

        def put(n, at, target, cut, piece):
            target[:, cut] = piece if n == 0 else target[:, cut] + piece
            if n == factors.shape[0] // group - 1:
                done.append(pltpu.make_async_copy(target.at[:, cut], outs[at].at[:, cut], sems.at[4 + len(done)]))
                done[-1].start()

        done = []
        whole = slice(0, width)
        for n in range(factors.shape[0] // group):
            part = slice(n * group, (n + 1) * group)
            wh, g, vectors = (factor_rows(factors, part, start, group) for start in (0, 16, 32))
            hidden_c, att1, bg1, inner1, og1 = (picked(vectors, kind, group) for kind in range(5))
            active, slope = gelu_pair(mm(inner1, f1[...]) + bias)
            ig1 = (mm_nt(og1, f2[...]) * slope).astype(BF16)
            put(n, 3, held[3], whole, mm_tn(active.astype(BF16), og1))
            put(n, 2, held[2], slice(0, f1.shape[1]), mm_tn(inner1, ig1))
            query = (mm(hidden_c, w[:, :width]) + vec[2:3].astype(F32)).astype(BF16)
            da1 = mm_nt(bg1, p[...]).astype(BF16)
            chosen_g = jnp.where(mask, mm(g, w[:, width : 2 * width]), 0.0).astype(BF16)
            dq1 = mm_tn(spread, chosen_g).astype(BF16)
            put(n, 1, held[1], whole, mm_tn(att1, bg1))
            parts = (mm_tn(hidden_c, dq1), mm_tn(g, expanded(query)), mm_tn(wh, expanded(da1)))
            for k, piece in enumerate(parts):
                put(n, 0, held[0], slice(k * width, (k + 1) * width), piece)
        for copy in done:
            copy.wait()


def join_factors(pieces, factors):
    at = 0
    for piece in pieces:
        factors[at : at + piece.shape[0]] = piece[...]
        at += piece.shape[0]


def factor_rows(factors, part, start, group):
    pieces = [factors[part, k * 48 + start : k * 48 + start + 16].reshape(group * 16, 128) for k in range(3)]
    return jnp.concatenate(pieces, axis=1)


def picked(vectors, kind, group):
    rows, cols = group * IMGS, group * 16
    row = lax.broadcasted_iota(jnp.int32, (rows, cols), 0)
    col = lax.broadcasted_iota(jnp.int32, (rows, cols), 1)
    wanted = (row >> 1) * 16 + kind * IMGS + (row & 1)
    return mm(jnp.where(col == wanted, 1.0, 0.0).astype(BF16), vectors).astype(BF16)


VM = pl.BlockSpec(memory_space=pltpu.VMEM)
SM = pl.BlockSpec(memory_space=pltpu.SMEM)
HB = pl.BlockSpec(memory_space=pltpu.HBM)


def call(body, ins, outs, scratch, name, limit, sems=0, far=0, aliases=None):
    return pl.pallas_call(
        body,
        out_shape=[jax.ShapeDtypeStruct(shape, kind) for shape, kind in outs],
        in_specs=[spec for spec, _ in ins],
        out_specs=[HB] * far + [VM] * (len(outs) - far),
        scratch_shapes=[pltpu.VMEM(shape, kind) for shape, kind in scratch]
        + ([pltpu.SemaphoreType.DMA((sems,))] if sems else []),
        compiler_params=pltpu.CompilerParams(vmem_limit_bytes=limit * 1024 * 1024),
        cost_estimate=pl.CostEstimate(flops=0, bytes_accessed=1, transcendentals=0),
        input_output_aliases=aliases or {},
        name=name,
    )(*[value for _, value in ins])


def swapped(array):
    return lax.ppermute(array, "pipe", [(0, 1), (1, 0)])


def exchanged(array, bits, cores=(0, 1)):
    dp = lax.axis_size("dp")
    pairs = [(core * dp + i, core * dp + (i ^ bits[core])) for core in cores for i in range(dp)]
    return lax.ppermute(array, ("pipe", "dp"), pairs)


def total(pieces, start, stop):
    parts = [piece[start:stop].astype(F32) for piece in pieces]
    return sum(parts[1:], parts[0]).astype(BF16)


def after(arrays, *others):
    return lax.optimization_barrier((arrays, others))[0]


NEAR, FAR = (4, 4), (8, 8)
LONG = (("halve", (1, 2)), ("halve", (2, 1)), ("halve", NEAR), ("swap", FAR), ("collect", NEAR), ("pair", (2, 1)), ("last", (1, 2)))
SHORT = (("halve", (1, 2)), ("halve", (2, 1)), ("swap", NEAR), ("swap", FAR), ("collect", (2, 1)), ("collect", (1, 2)))
GATHER = (("gather", FAR), ("gather", NEAR), ("gather", (2, 1)), ("gather", (1, 2)))


class Stream:
    def __init__(self, pieces, steps, rider=None):
        self.pieces, self.steps, self.rider, self.at = list(pieces), steps, rider, 0
        self.whole = lax.axis_size("dp") == 16
        self.leaving, self.count = self.pieces[0], 16 if steps is not GATHER else 1

    def wait(self, *others):
        self.pieces = list(after(tuple(self.pieces), *others))

    def swap(self, message, bits):
        self.leaving = message
        if self.rider is None:
            return exchanged(self.leaving, bits)
        self.leaving = jnp.concatenate([message.reshape(-1, 128), self.rider])
        got = exchanged(self.leaving, bits)
        rows = got.shape[0] - self.rider.shape[0]
        self.rider = total([self.rider, got[rows:]], 0, self.rider.shape[0])
        return got[:rows].reshape(message.shape)

    def step(self):
        if not self.whole:
            return
        kind, bits = self.steps[self.at]
        self.at += 1
        count = self.count
        if kind == "halve":
            got = self.swap(total(self.pieces, count // 2, count), bits)
            self.pieces, self.count = self.pieces + [got], count // 2
        elif kind == "swap":
            run = 1 if bits == FAR else 2
            mid = total(self.pieces, 0, count)
            turned = [total(self.pieces, at ^ run, (at ^ run) + run) for at in range(0, count, run)]
            self.pieces = [mid, self.swap(jnp.concatenate(turned), bits)]
            if self.steps[self.at][0] in ("collect", "pair"):
                self.pieces = [total(self.pieces, 0, count)]
        elif kind == "last":
            self.leaving = self.pieces[1]
            self.pieces = self.pieces + [exchanged(self.leaving, bits)]
        else:
            self.leaving = jnp.concatenate(self.pieces, axis=0) if len(self.pieces) > 1 else self.pieces[0]
            if kind == "pair":
                later = self.steps[self.at][1]
                self.pieces = [self.leaving, exchanged(self.leaving, bits), exchanged(self.leaving, later)]
                return
            self.pieces = [self.leaving, exchanged(self.leaving, bits, (1,) if kind == "gather" else (0, 1))]

    def parts(self):
        if self.whole:
            return self.pieces
        whole = lax.psum(total(self.pieces, 0, 16).astype(F32), "dp").astype(BF16)
        return [whole[at : at + 4] for at in range(0, 16, 4)]

    def ridden(self):
        if self.whole:
            return self.rider
        return lax.psum(self.rider.astype(F32), "dp").astype(BF16)


def local(
    patches, class_token, keep_mask, class_cotangent, norm1_gain, norm1_bias, qkv_weight, qv_bias,
    mix_pre, mix_post, post_bias, proj_weight, proj_bias, scale_attn, norm2_gain, norm2_bias,
    fc1_weight, fc1_bias, fc2_weight, fc2_bias, scale_mlp,
):
    dp = lax.axis_size("dp")
    images, count, width = patches.shape
    hidden_width = fc1_weight.shape[2]
    length, lanes = 208, 256
    half = width // 2
    flat = IMGS * length

    w_own, p_own, f1_own, f2_own = qkv_weight[0], proj_weight[0], fc1_weight[0], fc2_weight[0]
    w_got = swapped(w_own)
    small = (
        norm1_gain, norm1_bias, qv_bias, proj_bias, scale_attn, norm2_gain, norm2_bias, fc1_bias, fc2_bias, scale_mlp,
        mix_pre, mix_post, post_bias[None],
    )
    vec_own, pre_rows, post_rows, bias_row = call(
        prepare,
        [(HB, array) for array in small],
        [((16, width), BF16), ((HEADS, width), F32), ((HEADS, width), F32), ((1, width), F32)],
        [(array.shape, BF16) for array in small],
        "prepare",
        LIMIT_P,
        sems=13,
    )
    vec_got = swapped(vec_own)
    mixing = jnp.stack([mix_pre, mix_post]).astype(F32)
    rows = jnp.pad(patches, ((0, 0), (0, length - count), (0, 0)))
    p_late, f1_late, f2_late = after((p_own, f1_own, f2_own), w_got, vec_got, rows)
    p_got, f1_got, f2_got = swapped(p_late), swapped(f1_late), swapped(f2_late)

    token_shape = (IMGS, length, width)
    wide_shape = (IMGS, lanes, width)
    keep_scratch = ((8, lanes), F32)
    att, hid, queries, keys, values, probs = call(
        attention_forward,
        [(SM, mixing), (VM, rows), (VM, keep_mask), (VM, vec_own), (VM, vec_got), (HB, w_own), (HB, w_got),
         (VM, bias_row)],
        [(token_shape, BF16), (token_shape, BF16), (wide_shape, BF16), (wide_shape, BF16), (wide_shape, BF16),
         ((IMGS, HEADS * lanes, lanes), BF16)],
        [((width, 3 * width), BF16), ((width, HEADS * lanes), BF16), keep_scratch],
        "attention_forward",
        LIMIT_A,
        sems=1,
    )
    vec_shape = (16, width)
    send1, kept1, mg, vec0, vec1, class_own, class_other, factors = call(
        middle_kernel,
        [(VM, att), (VM, rows), (VM, keep_mask), (VM, class_token), (VM, class_cotangent), (VM, vec_own),
         (VM, vec_got), (HB, p_own), (HB, p_got), (HB, f1_own), (HB, f1_got), (HB, f2_own), (HB, f2_got), (HB, w_own),
         (HB, w_got)],
        [((17, 288, 128), BF16), ((16, 288, 128), BF16), (token_shape, F32), (vec_shape, F32), (vec_shape, F32),
         ((16, half), BF16), ((16, half), BF16), ((144, 128), BF16)],
        [((width, width), BF16), ((width, hidden_width), BF16), ((hidden_width, width), BF16),
         ((width, width), BF16), ((width, hidden_width), BF16), ((hidden_width, width), BF16),
         ((width, 3 * width), BF16), ((flat, hidden_width), BF16), ((flat, hidden_width), BF16),
         ((32, 288, 128), BF16), keep_scratch],
        "middle_kernel",
        LIMIT_B,
        sems=7,
    )

    def image_backward(b, mg):
        return call(
            lambda *refs: attention_backward(b, *refs),
            [(SM, mixing), (VM, mg), (VM, keep_mask), (VM, queries), (VM, keys), (VM, values), (VM, probs),
             (VM, vec_own), (VM, vec_got), (HB, p_own), (HB, p_got), (VM, bias_row), (VM, pre_rows), (VM, post_rows)],
            [((length, 3 * width), BF16), ((24, width), F32)],
            [((width, width), BF16), ((HEADS * lanes, lanes), BF16), ((width, HEADS * lanes), BF16),
             ((lanes, width), BF16), keep_scratch],
            f"attention_backward_{b}",
            LIMIT_C,
            sems=1,
        )

    got1 = swapped(send1)
    factors_got = got1[16, :144]
    stream1, shared = Stream((kept1, got1), LONG), Stream((factors[None], factors_got[None]), GATHER)
    join0, sum0 = image_backward(0, mg)
    stream1.wait(join0)
    stream1.step()
    join1, sum1 = image_backward(1, after(mg, stream1.leaving))
    mg = after(mg, join1)
    send2, kept2, vec_part, own_half, other_half = call(
        input_gradients,
        [(VM, mg), (VM, rows), (VM, hid), (VM, att), (VM, join0), (VM, join1), (VM, sum0), (VM, sum1), (VM, vec0),
         (VM, vec1), (VM, vec_own), (VM, vec_got), (HB, w_own), (HB, w_got), (VM, class_other)],
        [((17, 144, 128), BF16), ((16, 144, 128), BF16), ((112, 128), BF16), ((IMGS, half, length), F32), ((IMGS, half + 16, length), BF16)],
        [((width, 3 * width), BF16), ((flat, 3 * width), BF16), ((32, 144, 128), BF16)],
        "input_gradients",
        LIMIT_C,
        sems=1,
    )
    got2, half_got = swapped(send2), swapped(other_half)
    stream2 = Stream((kept2, got2), SHORT, total([vec_part, got2[16, :112]], 0, 112))
    def turn(*streams):
        for stream in streams:
            turn.last = stream.wait(*turn.last) or (stream.step(), stream.leaving)[1:]

    turn.last = (kept2,)
    turn(stream1, stream2)
    turn.last += (half_got,)
    turn(shared, stream1, stream2, shared, stream1, stream2, shared, shared, stream1, stream2, stream1)
    patch_out, class_result, class_grad = call(
        assemble,
        [(VM, part) for part in after((own_half, half_got, class_own), stream1.leaving)],
        [((2 * IMGS, half, count), F32), ((2 * IMGS, half), BF16), ((2 * IMGS, half), BF16)],
        [],
        "assemble",
        LIMIT_C,
    )
    turn.last += tuple(shared.pieces)
    turn(stream2)
    small_outs = call(
        vector_outputs,
        [(VM, stream2.ridden())],
        [((1, size * width), F32) for size in (1, 1, 2, 1, 1, 1, 1, 4, 1, 1)]
        + [((HEADS, HEADS), F32), ((HEADS, HEADS), F32), ((1, HEADS), F32)],
        [],
        "vector_outputs",
        LIMIT_C,
    )
    turn.last += (patch_out, class_result, class_grad, small_outs)
    turn(stream1, stream2)
    if dp == 16:
        factor_parts = after(tuple(shared.pieces), stream2.leaving)
    else:
        factor_parts = tuple(lax.all_gather(part, "dp") for part in (factors, factors_got))
    matrices = [((width, 3 * width), F32), ((width, width), F32), ((width, hidden_width), F32), ((hidden_width, width), F32)]
    outs = call(
        class_gradients,
        [(VM, part) for part in factor_parts]
        + [(HB, w_own), (HB, p_own), (HB, f1_own), (HB, f2_own), (VM, vec_own)],
        matrices,
        [(shape, BF16) for shape, _ in matrices] + [((2 * dp, 144, 128), BF16)] + matrices,
        "class_gradients",
        LIMIT_E,
        sems=10,
        far=4,
    )
    parts = [], []
    for at, stream in enumerate((stream1, stream2)):
        start = 0
        for part in stream.parts():
            parts[at].append((at, start, part))
            start += part.shape[0]
    early = [part for group in parts for part in group if part[1] < (12 if part[0] == 0 else 8)]
    late = [part for group in parts for part in group if part[1] >= (12 if part[0] == 0 else 8)]
    early = [placed for part in early for placed in (part, (part[0], part[1] + 16, swapped(part[2])))]
    early += [part for part in late if part[0] == 0]
    for name in ("first_outputs", "last_outputs"):
        if name == "last_outputs":
            late = [(at, start, after(part, outs[0])) for at, start, part in late]
            own = [part for part in late if part[0] == 1]
            chosen_parts = own + [(at, start + 16, swapped(part)) for at, start, part in late]
        else:
            chosen_parts = early
        plan = [(at, start) for at, start, _ in chosen_parts]
        slots = sum(part.shape[0] * (2 - at) for at, _, part in chosen_parts)
        outs = call(
            lambda *refs: place_blocks(plan, *refs),
            [(VM, part) for _, _, part in chosen_parts] + [(HB, out) for out in outs],
            matrices,
            [((slots, 48, width), F32)],
            name,
            LIMIT_D,
            sems=slots,
            far=4,
            aliases={len(plan) + n: n for n in range(4)},
        )
    qkv_out, proj_out, fc1_out, fc2_out = outs
    n1g, n1b, qvb, pb, sa, n2g, n2b, f1b, f2b, sm, pre, post, bias = small_outs
    return (
        class_result, patch_out.transpose(0, 2, 1), class_grad, n1g, n1b, qkv_out[None], qvb, proj_out[None], pb, sa, n2g, n2b,
        fc1_out[None], f1b, fc2_out[None], f2b, sm, pre, post, bias[0],
    )


def solution(mesh):
    stacked = (P("pipe", None), P("pipe", None), P("pipe", None, None))
    row, _, cube = stacked
    return jax.shard_map(
        local,
        mesh=mesh,
        in_specs=(
            P("dp", None, None), P("dp", None), P("dp", None), P("dp", None),
            row, row, cube, row, P(), P(), P(), cube, row, row, row, row, cube, row, cube, row, row,
        ),
        out_specs=(
            P("dp", "pipe"), P("dp", None, "pipe"), P("dp", "pipe"),
            row, row, cube, row, cube, row, row, row, row, cube, row, cube, row, row, P(), P(), P(),
        ),
        check_vma=False,
    )
```

```python
import jax
import jax.numpy as jnp
from jax import lax
from jax.experimental import pallas as pl
from jax.experimental.pallas import tpu as pltpu
from jax.sharding import PartitionSpec as P

HEADS = 8
IMGS = 2
LIMIT_P, LIMIT_A, LIMIT_B, LIMIT_C, LIMIT_D, LIMIT_E = 60, 24, 24, 24, 24, 24
LOG2E = 1.4426950408889634
F32 = jnp.float32
BF16 = jnp.bfloat16


def mm(left, right):
    return lax.dot_general(left, right, (((1,), (0,)), ((), ())), preferred_element_type=F32)


def mm_nt(left, right):
    return lax.dot_general(left, right, (((1,), (1,)), ((), ())), preferred_element_type=F32)


def mm_tn(left, right):
    return lax.dot_general(left, right, (((0,), (0,)), ((), ())), preferred_element_type=F32)


def normed(rows):
    centred = rows - jnp.mean(rows, -1, keepdims=True)
    scale = lax.rsqrt(jnp.mean(centred * centred, -1, keepdims=True) + 1e-06)
    return centred * scale, scale


def norm_back(normal, scale, grad):
    inner = jnp.mean(grad * normal, -1, keepdims=True)
    return (grad - jnp.mean(grad, -1, keepdims=True) - normal * inner) * scale


def col_sum(rows):
    return jnp.sum(rows, axis=0, keepdims=True)


def gelu_pair(rows):
    phi = 0.5 + 0.5 * lax.erf(rows * 0.7071067811865476)
    return rows * phi, phi + rows * (jnp.exp2(rows * rows * (-0.5 * LOG2E)) * 0.3989422804014327)


def head_mask(rows, width):
    lane = lax.broadcasted_iota(jnp.int32, (rows, width), 1)
    head = lax.rem(lax.broadcasted_iota(jnp.int32, (rows, width), 0), HEADS)
    size = width // HEADS
    return (lane >= head * size) & (lane < head * size + size)


def chosen(is_first, first, other):
    return jnp.where(is_first, first, other)


def scaled_rows(rows, factors):
    size = rows.shape[0] // HEADS
    parts = []
    for head, factor in enumerate(factors):
        part = rows[head * size : (head + 1) * size]
        parts.append(part * jnp.full((1, rows.shape[1]), factor, F32).astype(BF16))
    return jnp.concatenate(parts, axis=0)


def transposed(rows):
    return rows.T


def own_place():
    core = lax.axis_index("pipe")
    return core, core * 16 + (lax.axis_index("dp") if lax.axis_size("dp") == 16 else 0)


def fetch(first, own, got, target, sem):
    @pl.when(first)
    def _():
        pltpu.make_async_copy(own, target, sem).start()

    @pl.when(jnp.logical_not(first))
    def _():
        pltpu.make_async_copy(got, target, sem).start()

    return pltpu.make_async_copy(own, target, sem)


def own_images(first, rows):
    return chosen(first, rows[0:IMGS], rows[IMGS : 2 * IMGS])


def token_rows(rows_ref):
    rows = rows_ref[pl.ds(lax.axis_index("pipe") * IMGS, IMGS)]
    return rows.reshape(-1, rows.shape[2])


def keep_columns(first, mask_ref, scratch):
    scratch[...] = jnp.zeros_like(scratch)
    scratch[0:IMGS, 0 : mask_ref.shape[1]] = own_images(first, mask_ref[...].astype(F32))
    return scratch[...].T


def prepare(*refs):
    sources, (vec_ref, pre_ref, post_ref, bias_ref), held, sems = refs[:13], refs[13:17], refs[17:30], refs[30]
    copies = [pltpu.make_async_copy(*pair, sems.at[n]) for n, pair in enumerate(zip(sources, held))]
    for copy in copies:
        copy.start()
    for copy in copies:
        copy.wait()
    n1g, n1b, qvb, pb, sa, n2g, n2b, f1b, f2b, sm, pre, post, post_bias = held
    width = n1g.shape[1]
    rows = [n1g[...], n1b[...], qvb[:, :width], qvb[:, width:], pb[...], sa[...], n2g[...], n2b[...]]
    rows += [f1b[:, k * width : (k + 1) * width] for k in range(4)] + [f2b[...], sm[...]]
    rows = [row.astype(F32) for row in rows] + [jnp.zeros((2, width), F32)]
    vec_ref[...] = jnp.concatenate(rows, axis=0).astype(BF16)
    spread = jnp.where(head_mask(HEADS, width), 1.0, 0.0).astype(BF16)
    pre_ref[...] = mm(pre[...], spread)
    post_ref[...] = mm_tn(post[...], spread)
    bias_ref[...] = mm(post_bias[...], spread)


def attention_forward(
    mixing, rows_ref, mask_ref, vec_own, vec_got, w_own, w_got, bias_ref,
    att_ref, hid_ref, q_ref, k_ref, v_ref, pt_ref, w_ref, vs_ref, keep_ref, sems,
):
    first = lax.axis_index("pipe") == 0
    weights_copy = fetch(first, w_own, w_got, w_ref, sems.at[0])
    width = rows_ref.shape[2]
    length = rows_ref.shape[1]
    lanes = q_ref.shape[1]
    size = width // HEADS
    keeps = keep_columns(first, mask_ref, keep_ref)

    vec = chosen(first, vec_own[...].astype(F32), vec_got[...].astype(F32))
    scale = size ** (-0.5) * LOG2E
    pad_rows = jnp.zeros((lanes - length, width), BF16)
    same = lax.broadcasted_iota(jnp.int32, (length, lanes), 0) == lax.broadcasted_iota(jnp.int32, (length, lanes), 1)

    for b in range(IMGS):
        normal, _ = normed(rows_ref[lax.axis_index("pipe") * IMGS + b].astype(F32))
        hidden = (normal * vec[0:1] + vec[1:2]).astype(BF16)
        hid_ref[b] = hidden
        if b == 0:
            weights_copy.wait()
        joined = mm(hidden, w_ref[...])
        queries = joined[:, :width] + vec[2:3]
        keys = joined[:, width : 2 * width]
        values = joined[:, 2 * width :] + vec[3:4]
        low_k = keys.astype(BF16)
        low_v = values.astype(BF16)
        q_ref[b, :length] = queries.astype(BF16)
        k_ref[b, :length] = low_k
        v_ref[b, :length] = low_v
        q_ref[b, length:] = pad_rows
        k_ref[b, length:] = pad_rows
        v_ref[b, length:] = pad_rows
        q_t = transposed(q_ref[b])
        v_t = transposed(v_ref[b])
        keep = keeps[:length, b : b + 1]
        allowed = (keep > 0.0) | same
        for h in range(HEADS):
            scaled_q = scaled_rows(q_t, [mixing[0, h, c] for c in range(HEADS)])
            scores = jnp.where(allowed, mm(low_k, scaled_q) * scale, -1e30)
            top = jnp.max(scores, axis=0, keepdims=True)
            weights = jnp.exp2(scores - top)
            weights = weights * (1.0 / jnp.sum(weights, axis=0, keepdims=True))
            pt_ref[b, h * lanes : h * lanes + length] = weights.astype(BF16)
            pt_ref[b, h * lanes + length : (h + 1) * lanes] = jnp.zeros((lanes - length, lanes), BF16)
            vs_ref[:, h * lanes : (h + 1) * lanes] = scaled_rows(v_t, [mixing[1, c, h] for c in range(HEADS)])
        mixed = transposed(mm(vs_ref[...], pt_ref[b]))[:length]
        low_f = low_v.astype(F32)
        extra = bias_ref[...] * (col_sum(low_f * keep) + (1.0 - keep) * low_f)
        att_ref[b] = (mixed + extra).astype(BF16)


def block_copy(source, target, start, count):
    for n in range(count):
        target[n] = source[position_block(start + n)]


def position_block(at):
    core, me = own_place()
    first_bit, second_bit = (at >> 3) & 1, (at >> 2) & 1
    rest = ((at >> 4) << 4) | ((at & 1) << 3) | (((at >> 1) & 1) << 2)
    x_first = rest | first_bit | (second_bit << 1)
    y_first = rest | second_bit | (first_bit << 1)
    return jnp.where(core == (at >> 4), x_first, y_first) ^ me


def block_position(block):
    core, me = own_place()
    apart = block ^ me
    x_bit, y_bit = apart & 1, (apart >> 1) & 1
    half = apart >> 4
    top = jnp.where(core == half, (x_bit << 3) | (y_bit << 2), (y_bit << 3) | (x_bit << 2))
    return (half << 4) | top | (((apart >> 2) & 1) << 1) | ((apart >> 3) & 1)


def put_blocks(target, rows, start, wide):
    tall, across = 48, 384
    for rb in range(rows.shape[0] // tall):
        for cb in range(rows.shape[1] // across):
            block = rb * wide[0] + wide[1] + cb
            for k in range(3):
                piece = rows[rb * tall : (rb + 1) * tall, cb * across + k * 128 : cb * across + (k + 1) * 128]
                target[block, start + k * tall : start + (k + 1) * tall] = piece.astype(BF16)


def middle_kernel(
    att_ref, rows_ref, mask_ref, class_ref, cot_ref,
    vec_own, vec_got, p_own, p_got, f1_own, f1_got, f2_own, f2_got, w_own, w_got,
    send_ref, kept_ref, mg_ref, vec_out, vec_out1, class_own, class_other, factor_ref,
    p0_ref, f10, f20, p1_ref, f11, f21, w1_ref, act_ref, gp_ref, blocks, keep_ref, sems,
):
    first = lax.axis_index("pipe") == 0
    p0_copy = fetch(first, p_own, p_got, p0_ref, sems.at[0])
    w1_copy = fetch(first, w_got, w_own, w1_ref, sems.at[3])
    f10_copy = fetch(first, f1_own, f1_got, f10, sems.at[1])
    f20_copy = fetch(first, f2_own, f2_got, f20, sems.at[2])
    p1_copy = fetch(first, p_got, p_own, p1_ref, sems.at[4])
    f11_copy = fetch(first, f1_got, f1_own, f11, sems.at[5])
    f21_copy = fetch(first, f2_got, f2_own, f21, sems.at[6])
    length, width = rows_ref.shape[1], rows_ref.shape[2]
    flat = IMGS * length
    size = width // HEADS
    patches = mask_ref.shape[1]
    keep_ref[...] = jnp.zeros_like(keep_ref)
    keep_ref[0:IMGS, 0:patches] = own_images(first, mask_ref[...].astype(F32))
    keep_rows = keep_ref[0:IMGS, :length]
    keep_lane = lax.broadcasted_iota(jnp.int32, (IMGS, length), 1)
    keep_rows = jnp.where(keep_lane == patches, 1.0, keep_rows)

    own, got = vec_own[...].astype(F32), vec_got[...].astype(F32)
    vec, vec1 = chosen(first, own, got), chosen(first, got, own)

    def wide_bias(v):
        return jnp.concatenate([v[8 + k : 9 + k] for k in range(4)], axis=1)

    blank = jnp.zeros((8 - IMGS, width), F32)
    class_rows = jnp.concatenate([own_images(first, class_ref[...].astype(F32)), blank], axis=0)
    w1_copy.wait()
    normal_c, _ = normed(class_rows)
    hidden_c = (normal_c * vec1[0:1] + vec1[1:2]).astype(BF16)
    query = (mm(hidden_c, w1_ref[:, :width]) + vec1[2:3]).astype(BF16).astype(F32)
    mask = head_mask(IMGS * HEADS, width)

    def spread(rows):
        both = jnp.concatenate(
            [jnp.broadcast_to(rows[b : b + 1], (HEADS, width)) for b in range(IMGS)], axis=0
        )
        return jnp.where(mask, both, 0.0)

    def gathered(rows):
        kept = jnp.where(mask, rows, 0.0)
        parts = [col_sum(kept[b * HEADS : (b + 1) * HEADS]) for b in range(IMGS)]
        return jnp.concatenate(parts + [jnp.zeros((8 - IMGS, width), F32)], axis=0)

    query_rows = mm_nt(spread(query).astype(BF16), w1_ref[:, width : 2 * width]).astype(BF16)

    p0_copy.wait()
    branch = mm(att_ref[...].reshape(flat, width), p0_ref[...]) + vec[4:5]
    middle = token_rows(rows_ref).astype(F32) + vec[5:6] * branch
    normal, norm_scale = normed(middle)
    inner_low = (normal * vec[6:7] + vec[7:8]).astype(BF16)
    f10_copy.wait()
    bias = wide_bias(vec)
    step = f10.shape[1] // 2
    for k in range(2):
        cut = slice(k * step, (k + 1) * step)
        inner = mm(inner_low, f10[:, cut]) + bias[:, cut]
        active, slope = gelu_pair(inner)
        act_ref[:, cut] = active.astype(BF16)
        gp_ref[:, cut] = slope.astype(BF16)
    f20_copy.wait()
    outer = mm(act_ref[...], f20[...]) + vec[12:13]
    sent = (middle + vec[13:14] * outer).astype(BF16).astype(F32)

    upper1 = jnp.concatenate([own_images(first, cot_ref[...].astype(F32)), blank], axis=0)
    og1 = (upper1 * vec1[13:14]).astype(BF16)
    f21_copy.wait()
    dact1 = mm_nt(og1, f21[...])
    at_row = lax.broadcasted_iota(jnp.int32, (length, width), 0)
    hiddens, normals, scales, probs, low_probs, sums, whs = [], [], [], [], [], [], []
    for b in range(IMGS):
        tokens = jnp.where(at_row == patches, class_rows[b : b + 1], sent[b * length : (b + 1) * length])
        n1, s1 = normed(tokens)
        h1 = (n1 * vec1[0:1] + vec1[1:2]).astype(BF16)
        scores = mm_nt(query_rows[b * HEADS : (b + 1) * HEADS], h1) * (size ** (-0.5) * LOG2E)
        scores = jnp.where(keep_rows[b : b + 1] > 0.0, scores, -1e30)
        weights = jnp.exp2(scores - jnp.max(scores, axis=-1, keepdims=True))
        weights = weights / jnp.sum(weights, axis=-1, keepdims=True)
        low = weights.astype(BF16)
        hiddens.append(h1)
        normals.append(n1)
        scales.append(s1)
        probs.append(weights)
        low_probs.append(low)
        sums.append(jnp.sum(low.astype(F32), axis=-1, keepdims=True))
        whs.append(mm(low, h1))
    wh = jnp.concatenate(whs, axis=0).astype(BF16)
    prob_sum = gathered(jnp.broadcast_to(jnp.concatenate(sums, axis=0), (IMGS * HEADS, width)))
    att1 = (gathered(mm(wh, w1_ref[:, 2 * width :])) + vec1[3:4] * prob_sum).astype(BF16)
    p1_copy.wait()
    branch1 = mm(att1, p1_ref[...]) + vec1[4:5]
    middle1 = class_rows + vec1[5:6] * branch1
    normal2, scale2 = normed(middle1)
    inner1 = (normal2 * vec1[6:7] + vec1[7:8]).astype(BF16)
    f11_copy.wait()
    active1, slope1 = gelu_pair(mm(inner1, f11[...]) + wide_bias(vec1))
    outer1 = mm(active1.astype(BF16), f21[...]) + vec1[12:13]
    class_result = middle1 + vec1[13:14] * outer1

    ig1 = (dact1 * slope1).astype(BF16)
    dh2 = mm_nt(ig1, f11[...])
    mg1 = upper1 + norm_back(normal2, scale2, dh2 * vec1[6:7])
    bg1 = (mg1 * vec1[5:6]).astype(BF16)
    da1 = mm_nt(bg1, p1_ref[...]).astype(BF16).astype(F32)
    value_rows = mm_nt(spread(da1).astype(BF16), w1_ref[:, 2 * width :]).astype(BF16)
    low_grads, gs = [], []
    for b in range(IMGS):
        part = slice(b * HEADS, (b + 1) * HEADS)
        dw = mm_nt(value_rows[part], hiddens[b])
        ds = probs[b] * (dw - jnp.sum(probs[b] * dw, axis=-1, keepdims=True))
        low = (ds * size ** (-0.5)).astype(BF16)
        low_grads.append(low)
        gs.append(mm(low, hiddens[b]))
    g_rows = jnp.concatenate(gs, axis=0).astype(BF16)
    dq1 = gathered(mm(g_rows, w1_ref[:, width : 2 * width])).astype(BF16)
    dclass = mm_nt(dq1, w1_ref[:, :width])
    uppers, grads = [], []
    n1g, n1b = jnp.zeros((1, width), F32), jnp.zeros((1, width), F32)
    for b in range(IMGS):
        part = slice(b * HEADS, (b + 1) * HEADS)
        left = jnp.concatenate([low_grads[b], low_probs[b]], axis=0)
        right = jnp.concatenate([query_rows[part], value_rows[part]], axis=0)
        dh1 = mm_tn(left, right)
        grads.append(dh1)
        n1g = n1g + col_sum(dh1 * normals[b])
        n1b = n1b + col_sum(dh1)
        dtokens = norm_back(normals[b], scales[b], dh1 * vec1[0:1])
        uppers.append(jnp.where(at_row < patches, dtokens, 0.0).astype(BF16).astype(F32))

    def class_row(arrays):
        return jnp.concatenate([array[patches : patches + 1] for array in arrays], axis=0)

    dclass = dclass[0:IMGS]
    class_normal = class_row(normals)
    n1g = n1g + col_sum(dclass * class_normal)
    n1b = n1b + col_sum(dclass)
    class_grads = [
        mg1[0:IMGS] + norm_back(class_normal, class_row(scales), (class_row(grads) + dclass) * vec1[0:1])
    ]
    upper = jnp.concatenate(uppers, axis=0)
    class_rows = jnp.concatenate([class_result] + class_grads + [blank], axis=0)
    low_half, high_half = class_rows[:, : width // 2], class_rows[:, width // 2 :]
    class_own[...] = chosen(first, low_half, high_half).astype(BF16)
    class_other[...] = chosen(first, high_half, low_half).astype(BF16)
    ig1_sum = col_sum(ig1.astype(F32))
    vec_out1[...] = jnp.concatenate(
        [
            n1g,
            n1b,
            col_sum(dq1.astype(F32)),
            col_sum(da1 * prob_sum),
            col_sum(bg1.astype(F32)),
            col_sum(mg1 * branch1),
            col_sum(dh2 * normal2),
            col_sum(dh2),
        ]
        + [ig1_sum[:, k * width : (k + 1) * width] for k in range(4)]
        + [col_sum(og1.astype(F32)), col_sum(upper1 * outer1), jnp.zeros((2, width), F32)],
        axis=0,
    )
    pieces = [piece.astype(F32)[0:IMGS] for piece in (hidden_c, att1, bg1, inner1, og1)]
    vectors = jnp.concatenate(pieces + [jnp.zeros((16 - 5 * IMGS, width), F32)], axis=0).astype(BF16)
    for k in range(3):
        lanes = slice(k * 128, (k + 1) * 128)
        factor_ref[k * 48 : k * 48 + 16] = wh[:, lanes]
        factor_ref[k * 48 + 16 : k * 48 + 32] = g_rows[:, lanes]
        factor_ref[k * 48 + 32 : k * 48 + 48] = vectors[:, lanes]

    sm_grad = col_sum(upper * outer)
    og = (upper * vec[13:14]).astype(BF16)
    put_blocks(blocks, mm_tn(act_ref[...], og), 144, (1, 0))
    dh = jnp.zeros((flat, width), F32)
    fc1_sums = []
    step = f10.shape[1] // 1
    for k in range(1):
        cut = slice(k * step, (k + 1) * step)
        ig = (mm_nt(og, f20[cut, :]) * gp_ref[:, cut].astype(F32)).astype(BF16)
        ig_sum = col_sum(ig.astype(F32))
        fc1_sums += [ig_sum[:, at : at + width] for at in range(0, step, width)]
        put_blocks(blocks, mm_tn(inner_low, ig), 0, (4, k * step // width))
        dh = dh + mm_nt(ig, f10[:, cut])
    mg = upper + norm_back(normal, norm_scale, dh * vec[6:7])
    mg_ref[...] = mg.reshape(IMGS, length, width)
    vec_out[...] = jnp.concatenate(
        [jnp.zeros((4, width), F32), jnp.zeros((1, width), F32), col_sum(mg * branch), col_sum(dh * normal), col_sum(dh)]
        + fc1_sums
        + [col_sum(og.astype(F32)), sm_grad, jnp.zeros((2, width), F32)],
        axis=0,
    )
    block_copy(blocks, kept_ref, 0, 16)
    block_copy(blocks, send_ref, 16, 16)
    send_ref[16, 0:144] = factor_ref[...]
    send_ref[16, 144:288] = jnp.zeros((144, 128), BF16)


def attention_backward(
    b, mixing, mg_ref, mask_ref, q_ref, k_ref, v_ref, pt_ref, vec_own, vec_got, p_own, p_got, bias_ref,
    pre_rows, post_rows, join_ref, sum_ref, p_ref, dm_ref, ks_ref, da_ref, keep_ref, sems,
):
    first = lax.axis_index("pipe") == 0
    p_copy = fetch(first, p_own, p_got, p_ref, sems.at[0])
    length, width = mg_ref.shape[1], mg_ref.shape[2]
    lanes = q_ref.shape[1]
    size = width // HEADS
    root = size ** (-0.5)
    scale_row = chosen(first, vec_own[5:6].astype(F32), vec_got[5:6].astype(F32))
    bg = (mg_ref[b] * scale_row).astype(BF16)
    keep = keep_columns(first, mask_ref, keep_ref)[:length, b : b + 1]
    p_copy.wait()
    da = mm_nt(bg, p_ref[...]).astype(BF16)
    da_ref[:length] = da
    da_ref[length:] = jnp.zeros((lanes - length, width), BF16)
    da_t = transposed(da_ref[...])
    k_t = transposed(k_ref[b])
    low_v = v_ref[b, :length]
    val_f = low_v.astype(F32)
    key_f = k_ref[b, :length].astype(F32)
    da_f = da.astype(F32)
    biased = da_f * bias_ref[...]
    dv = keep * col_sum(biased) + (1.0 - keep) * biased
    bias_sum = col_sum(da_f * (col_sum(val_f * keep) + (1.0 - keep) * val_f))
    post_parts = []
    for c in range(HEADS):
        scaled = scaled_rows(da_t, [mixing[1, h, c] for h in range(HEADS)])
        dp = mm(low_v, scaled)
        weights = pt_ref[b, c * lanes : c * lanes + length]
        w_f = weights.astype(F32)
        dm = w_f * (dp - col_sum(w_f * dp))
        dm_ref[c * lanes : c * lanes + length] = dm.astype(BF16)
        dm_ref[c * lanes + length : (c + 1) * lanes] = jnp.zeros((lanes - length, lanes), BF16)
        moved = mm(weights, da_ref[...])
        dv = dv + moved * post_rows[c : c + 1]
        post_parts.append(col_sum(moved * val_f))
        ks_ref[:, c * lanes : (c + 1) * lanes] = scaled_rows(k_t, [mixing[0, c, h] for h in range(HEADS)])
    dk = jnp.zeros((length, width), F32)
    pre_parts = []
    for h in range(HEADS):
        moved = mm(dm_ref[h * lanes : h * lanes + length], q_ref[b])
        dk = dk + moved * pre_rows[h : h + 1]
        pre_parts.append(col_sum(moved * key_f))
    dq = transposed(mm(ks_ref[...], dm_ref[...]))[:length] * root
    join_ref[:, :width] = dq.astype(BF16)
    join_ref[:, width : 2 * width] = (dk * root).astype(BF16)
    join_ref[:, 2 * width :] = dv.astype(BF16)
    sum_ref[...] = jnp.concatenate(
        [part * root for part in pre_parts] + post_parts + [bias_sum, jnp.zeros((7, width), F32)], axis=0
    )


def input_gradients(
    mg_ref, rows_ref, hid_ref, att_ref, join0, join1, sum0, sum1, vec_in, vec_in1, vec_own, vec_got, w_own, w_got,
    class_other,
    send_ref, kept_ref, vec_part, own_half, other_half, w_ref, join_ref, blocks, sems,
):
    first = lax.axis_index("pipe") == 0
    w_copy = fetch(first, w_own, w_got, w_ref, sems.at[0])
    length, width = rows_ref.shape[1], rows_ref.shape[2]
    size = width // HEADS
    flat = IMGS * length
    vec = chosen(first, vec_own[...].astype(F32), vec_got[...].astype(F32))
    mg = mg_ref[...].reshape(flat, width)
    bg = (mg * vec[5:6]).astype(BF16)
    pb_grad = col_sum(bg.astype(F32))
    put_blocks(blocks, mm_tn(att_ref[...].reshape(flat, width), bg), 0, (4, 3))
    join_ref[:length] = join0[...]
    join_ref[length:] = join1[...]
    hidden = hid_ref[...].reshape(flat, width)
    put_blocks(blocks, mm_tn(hidden, join_ref[...]), 0, (4, 0))
    w_copy.wait()
    dh = mm_nt(join_ref[...], w_ref[...])
    normal, norm_scale = normed(token_rows(rows_ref).astype(F32))
    patch = mg + norm_back(normal, norm_scale, dh * vec[0:1])
    half = width // 2
    low_half, high_half = patch[:, :half], patch[:, half:]
    own_rows, other_rows = chosen(first, low_half, high_half), chosen(first, high_half, low_half)
    for b in range(IMGS):
        own_half[b] = transposed(own_rows[b * length : (b + 1) * length])
        other_half[b, :half] = transposed(other_rows[b * length : (b + 1) * length]).astype(BF16)
        other_half[b, half:] = jnp.zeros((16, length), BF16)
    other_half[0, half:, :half] = class_other[...]

    dq_sum = col_sum(join_ref[:, :width].astype(F32))
    dv_sum = col_sum(join_ref[:, 2 * width :].astype(F32))
    late = jnp.concatenate(
        [col_sum(dh * normal), col_sum(dh), dq_sum, dv_sum, pb_grad, jnp.zeros((11, width), F32)], axis=0
    )
    vec0 = vec_in[...] + late
    lane = lax.broadcasted_iota(jnp.int32, (width, 128), 1)
    feature = lax.broadcasted_iota(jnp.int32, (width, 128), 0)
    groups = jnp.where((feature >= lane * size) & (feature < lane * size + size), 1.0, 0.0)
    later = jnp.where((feature >= (lane - HEADS) * size) & (feature < (lane - HEADS) * size + size), 1.0, 0.0)

    def head_sums(rows, heads):
        return lax.dot_general(
            rows, heads, (((1,), (0,)), ((), ())), preferred_element_type=F32, precision=lax.Precision.HIGHEST
        )

    sums = sum0[...] + sum1[...]
    at_row = lax.broadcasted_iota(jnp.int32, (16, 128), 0)
    small = head_sums(sums[:16], groups) + jnp.where(at_row == 0, head_sums(sums[16:24], later)[0:1], 0.0)
    high = small.astype(BF16).astype(F32)
    tall = jnp.concatenate(
        [vec0[:, k * 128 : (k + 1) * 128] for k in range(3)]
        + [vec_in1[:, k * 128 : (k + 1) * 128] for k in range(3)]
        + [high, small - high],
        axis=0,
    )
    vec_part[...] = tall.astype(BF16)
    send_ref[16, :128] = tall.astype(BF16)
    send_ref[16, 128:] = jnp.zeros((16, 128), BF16)
    block_copy(blocks, kept_ref, 0, 16)
    block_copy(blocks, send_ref, 16, 16)


def assemble(own_half, half_got, class_own, patch_out, class_out, class_grad):
    first = lax.axis_index("pipe") == 0
    half, count = patch_out.shape[1:]
    for b in range(IMGS):
        mine, theirs = own_half[b, :, :count], half_got[b, :half, :count].astype(F32)
        patch_out[b] = chosen(first, mine, theirs)
        patch_out[IMGS + b] = chosen(first, theirs, mine)
    mine, theirs = class_own[...].astype(F32), half_got[0, half:, :half].astype(F32)
    for at, out in ((0, class_out), (8, class_grad)):
        pair = mine[at : at + IMGS], theirs[at : at + IMGS]
        rows = jnp.concatenate([chosen(first, *pair), chosen(first, *pair[::-1])], axis=0)
        out[...] = rows.astype(BF16)


def place_blocks(plan, *refs):
    count = len(plan)
    pieces, (qkv_out, proj_out, fc1_out, fc2_out), (held, sems) = refs[:count], refs[count + 4 : count + 8], refs[count + 8 :]

    def put(at, source, n, first, target):
        for k in range(3):
            held[at, :, k * 128 : (k + 1) * 128] = source[n, first + k * 48 : first + (k + 1) * 48].astype(F32)
        pltpu.make_async_copy(held.at[at], target, sems.at[at]).start()

    @pl.when(lax.axis_index("pipe") == 0)
    def _():
        slot = 0
        for which, source in enumerate(pieces):
            stream, start = plan[which]
            for n in range(source.shape[0]):
                block = position_block(start + n)
                down = pl.ds(pl.multiple_of((block >> 2) * 48, 48), 48)
                along = pl.ds(pl.multiple_of((block & 3) * 384, 384), 384)
                if stream == 0:
                    put(slot, source, n, 0, fc1_out.at[down, along])
                    put(slot + 1, source, n, 144, fc2_out.at[pl.ds(pl.multiple_of(block * 48, 48), 48)])
                    slot += 2
                else:
                    last = (block & 3) == 3

                    @pl.when(last)
                    def _():
                        put(slot, source, n, 0, proj_out.at[down])

                    @pl.when(jnp.logical_not(last))
                    def _():
                        put(slot, source, n, 0, qkv_out.at[down, along])

                    slot += 1
        for at in range(slot):
            pltpu.make_async_copy(held.at[at], fc2_out.at[pl.ds(0, 48)], sems.at[at]).wait()


def vector_outputs(part, *refs):
    vec_outs, (pre_out, post_out, bias_out) = refs[:10], refs[10:]
    first = lax.axis_index("pipe") == 0
    width = vec_outs[0].shape[1]
    tall = part[...].astype(F32)
    rows = [chosen(first, tall[k * 16 : (k + 1) * 16], tall[48 + k * 16 : 48 + (k + 1) * 16]) for k in range(3)]
    rows = jnp.concatenate(rows, axis=1)
    at = 0
    for out in vec_outs:
        for k in range(out.shape[1] // width):
            out[:, k * width : (k + 1) * width] = rows[at : at + 1]
            at += 1
    small = tall[96:112] + tall[112:128]
    pre_out[...] = small[0:8, 0:HEADS]
    post_out[...] = small[8:16].T[0:HEADS]
    bias_out[...] = small[0:1, HEADS : 2 * HEADS]


def class_gradients(*refs):
    factor_refs = refs[:-19]
    w_in, p_in, f1_in, f2_in, vec, *outs = refs[-19:-10]
    w, p, f1, f2, factors, *held, sems = refs[-10:]
    width = p.shape[0]

    @pl.when(lax.axis_index("pipe") != 0)
    def _():
        copies = [
            pltpu.make_async_copy(source, target, sems.at[n])
            for n, (source, target) in enumerate(((f1_in, f1), (f2_in, f2), (w_in, w), (p_in, p)))
        ]
        for copy in copies:
            copy.start()
        join_factors(factor_refs, factors)
        group = min(32, factors.shape[0])
        rows = group * IMGS * HEADS
        mask = head_mask(rows, width)
        spread = (
            lax.broadcasted_iota(jnp.int32, (rows, group * IMGS), 0) >> 3
            == lax.broadcasted_iota(jnp.int32, (rows, group * IMGS), 1)
        )
        spread = jnp.where(spread, 1.0, 0.0).astype(BF16)
        bias = jnp.concatenate([vec[8 + k : 9 + k].astype(F32) for k in range(4)], axis=1)
        for copy in copies:
            copy.wait()

        def expanded(vectors):
            return jnp.where(mask, mm(spread, vectors), 0.0).astype(BF16)

        def put(n, at, target, cut, piece):
            target[:, cut] = piece if n == 0 else target[:, cut] + piece
            if n == factors.shape[0] // group - 1:
                done.append(pltpu.make_async_copy(target.at[:, cut], outs[at].at[:, cut], sems.at[4 + len(done)]))
                done[-1].start()

        done = []
        whole = slice(0, width)
        for n in range(factors.shape[0] // group):
            part = slice(n * group, (n + 1) * group)
            wh, g, vectors = (factor_rows(factors, part, start, group) for start in (0, 16, 32))
            hidden_c, att1, bg1, inner1, og1 = (picked(vectors, kind, group) for kind in range(5))
            active, slope = gelu_pair(mm(inner1, f1[...]) + bias)
            ig1 = (mm_nt(og1, f2[...]) * slope).astype(BF16)
            put(n, 3, held[3], whole, mm_tn(active.astype(BF16), og1))
            put(n, 2, held[2], slice(0, f1.shape[1]), mm_tn(inner1, ig1))
            query = (mm(hidden_c, w[:, :width]) + vec[2:3].astype(F32)).astype(BF16)
            da1 = mm_nt(bg1, p[...]).astype(BF16)
            chosen_g = jnp.where(mask, mm(g, w[:, width : 2 * width]), 0.0).astype(BF16)
            dq1 = mm_tn(spread, chosen_g).astype(BF16)
            put(n, 1, held[1], whole, mm_tn(att1, bg1))
            parts = (mm_tn(hidden_c, dq1), mm_tn(g, expanded(query)), mm_tn(wh, expanded(da1)))
            for k, piece in enumerate(parts):
                put(n, 0, held[0], slice(k * width, (k + 1) * width), piece)
        for copy in done:
            copy.wait()


def join_factors(pieces, factors):
    at = 0
    for piece in pieces:
        factors[at : at + piece.shape[0]] = piece[...]
        at += piece.shape[0]


def factor_rows(factors, part, start, group):
    pieces = [factors[part, k * 48 + start : k * 48 + start + 16].reshape(group * 16, 128) for k in range(3)]
    return jnp.concatenate(pieces, axis=1)


def picked(vectors, kind, group):
    rows, cols = group * IMGS, group * 16
    row = lax.broadcasted_iota(jnp.int32, (rows, cols), 0)
    col = lax.broadcasted_iota(jnp.int32, (rows, cols), 1)
    wanted = (row >> 1) * 16 + kind * IMGS + (row & 1)
    return mm(jnp.where(col == wanted, 1.0, 0.0).astype(BF16), vectors).astype(BF16)


VM = pl.BlockSpec(memory_space=pltpu.VMEM)
SM = pl.BlockSpec(memory_space=pltpu.SMEM)
HB = pl.BlockSpec(memory_space=pltpu.HBM)


def call(body, ins, outs, scratch, name, limit, sems=0, far=0, aliases=None):
    return pl.pallas_call(
        body,
        out_shape=[jax.ShapeDtypeStruct(shape, kind) for shape, kind in outs],
        in_specs=[spec for spec, _ in ins],
        out_specs=[HB] * far + [VM] * (len(outs) - far),
        scratch_shapes=[pltpu.VMEM(shape, kind) for shape, kind in scratch]
        + ([pltpu.SemaphoreType.DMA((sems,))] if sems else []),
        compiler_params=pltpu.CompilerParams(vmem_limit_bytes=limit * 1024 * 1024),
        cost_estimate=pl.CostEstimate(flops=0, bytes_accessed=1, transcendentals=0),
        input_output_aliases=aliases or {},
        name=name,
    )(*[value for _, value in ins])


def swapped(array):
    return lax.ppermute(array, "pipe", [(0, 1), (1, 0)])


def exchanged(array, bits, cores=(0, 1)):
    dp = lax.axis_size("dp")
    pairs = [(core * dp + i, core * dp + (i ^ bits[core])) for core in cores for i in range(dp)]
    return lax.ppermute(array, ("pipe", "dp"), pairs)


def total(pieces, start, stop):
    parts = [piece[start:stop].astype(F32) for piece in pieces]
    return sum(parts[1:], parts[0]).astype(BF16)


def ridden_sum(left, right):
    both = left.astype(F32) + right.astype(F32)
    small = both[96:112] + both[112:]
    high = lax.reduce_precision(small, 8, 7)
    return jnp.concatenate([both[:96], high, small - high], axis=0).astype(BF16)


def after(arrays, *others):
    return lax.optimization_barrier((arrays, others))[0]


NEAR, FAR = (4, 4), (8, 8)
LONG = (("halve", (1, 2)), ("halve", (2, 1)), ("halve", NEAR), ("swap", FAR), ("collect", NEAR), ("pair", (2, 1)), ("last", (1, 2)))
SHORT = (("halve", (1, 2)), ("halve", (2, 1)), ("swap", NEAR), ("swap", FAR), ("collect", (2, 1)), ("collect", (1, 2)))
GATHER = (("gather", FAR), ("gather", NEAR), ("gather", (2, 1)), ("gather", (1, 2)))


class Stream:
    def __init__(self, pieces, steps, rider=None):
        self.pieces, self.steps, self.rider, self.at = list(pieces), steps, rider, 0
        self.whole = lax.axis_size("dp") == 16
        self.leaving, self.count = self.pieces[0], 16 if steps is not GATHER else 1

    def wait(self, *others):
        self.pieces = list(after(tuple(self.pieces), *others))

    def swap(self, message, bits):
        self.leaving = message
        if self.rider is None:
            return exchanged(self.leaving, bits)
        self.leaving = jnp.concatenate([message.reshape(-1, 128), self.rider])
        got = exchanged(self.leaving, bits)
        rows = got.shape[0] - self.rider.shape[0]
        self.rider = ridden_sum(self.rider, got[rows:])
        return got[:rows].reshape(message.shape)

    def step(self):
        if not self.whole:
            return
        kind, bits = self.steps[self.at]
        self.at += 1
        count = self.count
        if kind == "halve":
            got = self.swap(total(self.pieces, count // 2, count), bits)
            self.pieces, self.count = self.pieces + [got], count // 2
        elif kind == "swap":
            run = 1 if bits == FAR else 2
            mid = total(self.pieces, 0, count)
            turned = [total(self.pieces, at ^ run, (at ^ run) + run) for at in range(0, count, run)]
            self.pieces = [mid, self.swap(jnp.concatenate(turned), bits)]
            if self.steps[self.at][0] in ("collect", "pair"):
                self.pieces = [total(self.pieces, 0, count)]
        elif kind == "last":
            self.leaving = self.pieces[1]
            self.pieces = self.pieces + [exchanged(self.leaving, bits)]
        else:
            self.leaving = jnp.concatenate(self.pieces, axis=0) if len(self.pieces) > 1 else self.pieces[0]
            if kind == "pair":
                later = self.steps[self.at][1]
                self.pieces = [self.leaving, exchanged(self.leaving, bits), exchanged(self.leaving, later)]
                return
            self.pieces = [self.leaving, exchanged(self.leaving, bits, (1,) if kind == "gather" else (0, 1))]

    def parts(self):
        if self.whole:
            return self.pieces
        whole = lax.psum(total(self.pieces, 0, 16).astype(F32), "dp").astype(BF16)
        return [whole[at : at + 4] for at in range(0, 16, 4)]

    def ridden(self):
        if self.whole:
            return self.rider
        return lax.psum(self.rider.astype(F32), "dp").astype(BF16)


def local(
    patches, class_token, keep_mask, class_cotangent, norm1_gain, norm1_bias, qkv_weight, qv_bias,
    mix_pre, mix_post, post_bias, proj_weight, proj_bias, scale_attn, norm2_gain, norm2_bias,
    fc1_weight, fc1_bias, fc2_weight, fc2_bias, scale_mlp,
):
    dp = lax.axis_size("dp")
    images, count, width = patches.shape
    hidden_width = fc1_weight.shape[2]
    length, lanes = 208, 256
    half = width // 2
    flat = IMGS * length

    w_own, p_own, f1_own, f2_own = qkv_weight[0], proj_weight[0], fc1_weight[0], fc2_weight[0]
    w_got = swapped(w_own)
    small = (
        norm1_gain, norm1_bias, qv_bias, proj_bias, scale_attn, norm2_gain, norm2_bias, fc1_bias, fc2_bias, scale_mlp,
        mix_pre, mix_post, post_bias[None],
    )
    vec_own, pre_rows, post_rows, bias_row = call(
        prepare,
        [(HB, array) for array in small],
        [((16, width), BF16), ((HEADS, width), F32), ((HEADS, width), F32), ((1, width), F32)],
        [(array.shape, BF16) for array in small],
        "prepare",
        LIMIT_P,
        sems=13,
    )
    vec_got = swapped(vec_own)
    mixing = jnp.stack([mix_pre, mix_post]).astype(F32)
    rows = jnp.pad(patches, ((0, 0), (0, length - count), (0, 0)))
    p_late, f1_late, f2_late = after((p_own, f1_own, f2_own), w_got, vec_got, rows)
    p_got, f1_got, f2_got = swapped(p_late), swapped(f1_late), swapped(f2_late)

    token_shape = (IMGS, length, width)
    wide_shape = (IMGS, lanes, width)
    keep_scratch = ((8, lanes), F32)
    att, hid, queries, keys, values, probs = call(
        attention_forward,
        [(SM, mixing), (VM, rows), (VM, keep_mask), (VM, vec_own), (VM, vec_got), (HB, w_own), (HB, w_got),
         (VM, bias_row)],
        [(token_shape, BF16), (token_shape, BF16), (wide_shape, BF16), (wide_shape, BF16), (wide_shape, BF16),
         ((IMGS, HEADS * lanes, lanes), BF16)],
        [((width, 3 * width), BF16), ((width, HEADS * lanes), BF16), keep_scratch],
        "attention_forward",
        LIMIT_A,
        sems=1,
    )
    vec_shape = (16, width)
    send1, kept1, mg, vec0, vec1, class_own, class_other, factors = call(
        middle_kernel,
        [(VM, att), (VM, rows), (VM, keep_mask), (VM, class_token), (VM, class_cotangent), (VM, vec_own),
         (VM, vec_got), (HB, p_own), (HB, p_got), (HB, f1_own), (HB, f1_got), (HB, f2_own), (HB, f2_got), (HB, w_own),
         (HB, w_got)],
        [((17, 288, 128), BF16), ((16, 288, 128), BF16), (token_shape, F32), (vec_shape, F32), (vec_shape, F32),
         ((16, half), BF16), ((16, half), BF16), ((144, 128), BF16)],
        [((width, width), BF16), ((width, hidden_width), BF16), ((hidden_width, width), BF16),
         ((width, width), BF16), ((width, hidden_width), BF16), ((hidden_width, width), BF16),
         ((width, 3 * width), BF16), ((flat, hidden_width), BF16), ((flat, hidden_width), BF16),
         ((32, 288, 128), BF16), keep_scratch],
        "middle_kernel",
        LIMIT_B,
        sems=7,
    )

    def image_backward(b, mg):
        return call(
            lambda *refs: attention_backward(b, *refs),
            [(SM, mixing), (VM, mg), (VM, keep_mask), (VM, queries), (VM, keys), (VM, values), (VM, probs),
             (VM, vec_own), (VM, vec_got), (HB, p_own), (HB, p_got), (VM, bias_row), (VM, pre_rows), (VM, post_rows)],
            [((length, 3 * width), BF16), ((24, width), F32)],
            [((width, width), BF16), ((HEADS * lanes, lanes), BF16), ((width, HEADS * lanes), BF16),
             ((lanes, width), BF16), keep_scratch],
            f"attention_backward_{b}",
            LIMIT_C,
            sems=1,
        )

    got1 = swapped(send1)
    factors_got = got1[16, :144]
    stream1, shared = Stream((kept1, got1), LONG), Stream((factors[None], factors_got[None]), GATHER)
    join0, sum0 = image_backward(0, mg)
    stream1.wait(join0)
    stream1.step()
    join1, sum1 = image_backward(1, after(mg, stream1.leaving))
    mg = after(mg, join1)
    send2, kept2, vec_part, own_half, other_half = call(
        input_gradients,
        [(VM, mg), (VM, rows), (VM, hid), (VM, att), (VM, join0), (VM, join1), (VM, sum0), (VM, sum1), (VM, vec0),
         (VM, vec1), (VM, vec_own), (VM, vec_got), (HB, w_own), (HB, w_got), (VM, class_other)],
        [((17, 144, 128), BF16), ((16, 144, 128), BF16), ((128, 128), BF16), ((IMGS, half, length), F32), ((IMGS, half + 16, length), BF16)],
        [((width, 3 * width), BF16), ((flat, 3 * width), BF16), ((32, 144, 128), BF16)],
        "input_gradients",
        LIMIT_C,
        sems=1,
    )
    got2, half_got = swapped(send2), swapped(other_half)
    stream2 = Stream((kept2, got2), SHORT, ridden_sum(vec_part, got2[16, :128]))
    def turn(*streams):
        for stream in streams:
            turn.last = stream.wait(*turn.last) or (stream.step(), stream.leaving)[1:]

    turn.last = (kept2,)
    turn(stream1, stream2)
    turn.last += (half_got,)
    turn(shared, stream1, stream2, shared, stream1, stream2, shared, shared, stream1, stream2, stream1)
    patch_out, class_result, class_grad = call(
        assemble,
        [(VM, part) for part in after((own_half, half_got, class_own), stream1.leaving)],
        [((2 * IMGS, half, count), F32), ((2 * IMGS, half), BF16), ((2 * IMGS, half), BF16)],
        [],
        "assemble",
        LIMIT_C,
    )
    turn.last += tuple(shared.pieces)
    turn(stream2)
    small_outs = call(
        vector_outputs,
        [(VM, stream2.ridden())],
        [((1, size * width), F32) for size in (1, 1, 2, 1, 1, 1, 1, 4, 1, 1)]
        + [((HEADS, HEADS), F32), ((HEADS, HEADS), F32), ((1, HEADS), F32)],
        [],
        "vector_outputs",
        LIMIT_C,
    )
    turn.last += (patch_out, class_result, class_grad, small_outs)
    turn(stream1, stream2)
    if dp == 16:
        factor_parts = after(tuple(shared.pieces), stream2.leaving)
    else:
        factor_parts = tuple(lax.all_gather(part, "dp") for part in (factors, factors_got))
    matrices = [((width, 3 * width), F32), ((width, width), F32), ((width, hidden_width), F32), ((hidden_width, width), F32)]
    outs = call(
        class_gradients,
        [(VM, part) for part in factor_parts]
        + [(HB, w_own), (HB, p_own), (HB, f1_own), (HB, f2_own), (VM, vec_own)],
        matrices,
        [(shape, BF16) for shape, _ in matrices] + [((2 * dp, 144, 128), BF16)] + matrices,
        "class_gradients",
        LIMIT_E,
        sems=10,
        far=4,
    )
    parts = [], []
    for at, stream in enumerate((stream1, stream2)):
        start = 0
        for part in stream.parts():
            parts[at].append((at, start, part))
            start += part.shape[0]
    early = [part for group in parts for part in group if part[1] < (12 if part[0] == 0 else 8)]
    late = [part for group in parts for part in group if part[1] >= (12 if part[0] == 0 else 8)]
    early = [placed for part in early for placed in (part, (part[0], part[1] + 16, swapped(part[2])))]
    early += [part for part in late if part[0] == 0]
    for name in ("first_outputs", "last_outputs"):
        if name == "last_outputs":
            late = [(at, start, after(part, outs[0])) for at, start, part in late]
            own = [part for part in late if part[0] == 1]
            chosen_parts = own + [(at, start + 16, swapped(part)) for at, start, part in late]
        else:
            chosen_parts = early
        plan = [(at, start) for at, start, _ in chosen_parts]
        slots = sum(part.shape[0] * (2 - at) for at, _, part in chosen_parts)
        outs = call(
            lambda *refs: place_blocks(plan, *refs),
            [(VM, part) for _, _, part in chosen_parts] + [(HB, out) for out in outs],
            matrices,
            [((slots, 48, width), F32)],
            name,
            LIMIT_D,
            sems=slots,
            far=4,
            aliases={len(plan) + n: n for n in range(4)},
        )
    qkv_out, proj_out, fc1_out, fc2_out = outs
    n1g, n1b, qvb, pb, sa, n2g, n2b, f1b, f2b, sm, pre, post, bias = small_outs
    return (
        class_result, patch_out.transpose(0, 2, 1), class_grad, n1g, n1b, qkv_out[None], qvb, proj_out[None], pb, sa, n2g, n2b,
        fc1_out[None], f1b, fc2_out[None], f2b, sm, pre, post, bias[0],
    )


def solution(mesh):
    stacked = (P("pipe", None), P("pipe", None), P("pipe", None, None))
    row, _, cube = stacked
    return jax.shard_map(
        local,
        mesh=mesh,
        in_specs=(
            P("dp", None, None), P("dp", None), P("dp", None), P("dp", None),
            row, row, cube, row, P(), P(), P(), cube, row, row, row, row, cube, row, cube, row, row,
        ),
        out_specs=(
            P("dp", "pipe"), P("dp", None, "pipe"), P("dp", "pipe"),
            row, row, cube, row, cube, row, row, row, row, cube, row, cube, row, row, P(), P(), P(),
        ),
        check_vma=False,
    )
```
